32 devices in a mesh: rows: 8 (over z, x), blk: 4 (over y, core).
Axes of the slice: x: 2, y: 2, z: 4, core: 2. Of those that a mesh axis runs over, the one named last changes fastest.
Arguments:
- tokens: bfloat16 [32, 1024, 512], P('rows', 'blk'), may hold values from -6 to 6
- seg_lengths: int32 [32, 8], P('rows'), may hold values from 1 to 1017, as said below
- ln1_gain: float32 [512], replicated, may hold values from 0.25 to 1.75
- ln1_bias: float32 [512], replicated, may hold values from -1 to 1
- w_qkv: bfloat16 [512, 1536], replicated, may hold values from -0.25 to 0.25
- b_qv: float32 [1024], replicated, may hold values from -1 to 1
- w_o: bfloat16 [512, 512], replicated, may hold values from -1 to 1
- b_o: float32 [512], replicated, may hold values from -1 to 1
- ln2_gain: float32 [512], replicated, may hold values from 0.25 to 1.75
- ln2_bias: float32 [512], replicated, may hold values from -1 to 1
- w_up: bfloat16 [512, 1024], replicated, may hold values from -0.25 to 0.25
- b_up: float32 [1024], replicated, may hold values from -1 to 1
- w_down: bfloat16 [1024, 512], replicated, may hold values from -0.1875 to 0.1875
- b_down: float32 [512], replicated, may hold values from -1 to 1
- cotangent: bfloat16 [32, 1024, 512], P('rows', 'blk'), may hold values from -6 to 6
Outputs:
- output: bfloat16 [32, 1024, 512], P('rows', 'blk')
- input_grad: float32 [32, 1024, 512], P('rows', 'blk')
- grad_ln1_gain: float32 [512], replicated
- grad_ln1_bias: float32 [512], replicated
- grad_w_qkv: float32 [512, 1536], replicated
- grad_b_qv: float32 [1024], replicated
- grad_w_o: float32 [512, 512], replicated
- grad_b_o: float32 [512], replicated
- grad_ln2_gain: float32 [512], replicated
- grad_ln2_bias: float32 [512], replicated
- grad_w_up: float32 [512, 1024], replicated
- grad_b_up: float32 [1024], replicated
- grad_w_down: float32 [1024, 512], replicated
- grad_b_down: float32 [512], replicated
The draws below stay inside these ranges and needn't reach their ends.
Inputs may be any that keep to these rules, and one draw needn't show every extreme that they name: `seg_lengths`: each row's 8 cell lengths sum to 1024; in each aligned block of 4 rows that starts at a multiple of 4, one row holds a cell of exactly 1017 tokens.
All inputs are finite; a program needn't handle non-finite values.
Results may differ from the reference program's by a relative error of at most 0.009.
Values may be sent and summed in bfloat16 or wider, within the bound.
No kernel may reach another device: no remote copies, remote signals or barrier semaphores. Data moves between devices by JAX's collectives and lax.ppermute only.
A program may use at most 192 MiB of HBM per device.

```python
import math
import jax
import jax.numpy as jnp
from jax import lax

D = 512
HEADS = 8
FF = 1024
CELLS = 8
SEQ_DEV = 4
LENGTH = 1024
SEQS = 32


def draw_seg_lengths(key, part):
    key = jax.random.fold_in(key, 7)
    cut_key, lead_key, pick_key = jax.random.split(key, 3)
    row_keys = jax.random.split(cut_key, SEQS)
    shuffled = jax.vmap(lambda row_key: jax.random.permutation(row_key, LENGTH - 1))(row_keys)
    cut_points = (jnp.sort(shuffled[:, :CELLS - 1], axis=1) + 1).astype(jnp.int32)
    boundaries = jnp.concatenate([jnp.zeros((SEQS, 1), jnp.int32), cut_points, jnp.full((SEQS, 1), LENGTH, jnp.int32)], axis=1)
    drawn = boundaries[:, 1:] - boundaries[:, :-1]
    lead_cell = jax.random.randint(lead_key, (SEQS, 1), 0, CELLS)
    columns = jnp.arange(CELLS, dtype=jnp.int32)[None, :]
    spanning = jnp.where(columns == lead_cell, LENGTH - CELLS + 1, 1).astype(jnp.int32)
    chosen = jax.random.randint(pick_key, (SEQS // SEQ_DEV,), 0, SEQ_DEV)
    special = jnp.arange(SEQS, dtype=jnp.int32) % SEQ_DEV == jnp.repeat(chosen, SEQ_DEV)
    return jnp.where(special[:, None], spanning, drawn).astype(jnp.int32)


def draw_cotangent(key, part):
    key = jax.random.fold_in(key, 11)
    common_key, noise_key = jax.random.split(key, 2)
    common = jnp.clip(jax.random.normal(common_key, (D,), jnp.float32), -2.5, 2.5)
    noise = jnp.clip(jax.random.normal(noise_key, (SEQS, LENGTH, D), jnp.float32), -4.0, 4.0)
    values = 0.7 * common[None, None, :] + 0.7 * noise
    return jnp.clip(values, -6.0, 6.0).astype(jnp.bfloat16)


def shard_levels(own_key, shape, cuts, smallest, largest):
    def one(position, blocks):
        draws = jax.random.uniform(jax.random.fold_in(jax.random.fold_in(own_key, 6), position), (blocks,), jnp.float32, smallest / len(cuts), largest / len(cuts))
        return jnp.repeat(jnp.exp(draws), shape[position] // blocks).reshape((-1,) + (1,) * (len(shape) - position - 1))

    factor_of = one(*cuts[0])
    for cut in cuts[1:]:
        factor_of = factor_of * one(*cut)
    return factor_of


def centred(key, extent, width, reach, cuts=(), kind=jnp.bfloat16):
    loudness = shard_levels(key, extent, cuts, -0.22, 0.18) if cuts else 1.0
    values = jax.random.normal(key, extent, jnp.float32) * width * loudness
    return jnp.minimum(jnp.maximum(values, -reach), reach).astype(kind)


def setup_inputs(seed: int = 0) -> dict:
    seeds = jax.random.split(jax.random.key(seed), 16)
    tokens = centred(seeds[0], (SEQS, LENGTH, D), 1.0, 6.0, ((0, 8), (1, 4)))
    seg_lengths = draw_seg_lengths(jax.random.fold_in(seeds[15], 71), 0)
    ln1_gain = jnp.clip(1.0 + 0.15 * jax.random.normal(seeds[2], (D,), jnp.float32), 0.25, 1.75)
    ln1_bias = centred(seeds[3], (D,), 0.2, 1.0, (), jnp.float32)
    w_qkv = centred(seeds[4], (D, 3 * D), D ** -0.5, 0.25)
    b_qv = centred(seeds[5], (2 * D,), 0.2, 1.0, (), jnp.float32)
    w_o = centred(seeds[6], (D, D), (D // 16) ** -0.5, 1.0)
    b_o = centred(seeds[7], (D,), 0.2, 1.0, (), jnp.float32)
    ln2_gain = jnp.clip(1.0 + 0.15 * jax.random.normal(seeds[8], (D,), jnp.float32), 0.25, 1.75)
    ln2_bias = centred(seeds[9], (D,), 0.2, 1.0, (), jnp.float32)
    w_up = centred(seeds[10], (D, FF), D ** -0.5, 0.25)
    b_up = centred(seeds[11], (FF,), 0.2, 1.0, (), jnp.float32)
    w_down = centred(seeds[12], (FF, D), FF ** -0.5, 0.1875)
    b_down = centred(seeds[13], (D,), 0.2, 1.0, (), jnp.float32)
    cotangent = draw_cotangent(jax.random.fold_in(seeds[15], 71), 0)
    return dict(tokens=tokens, seg_lengths=seg_lengths, ln1_gain=ln1_gain, ln1_bias=ln1_bias, w_qkv=w_qkv, b_qv=b_qv, w_o=w_o, b_o=b_o, ln2_gain=ln2_gain, ln2_bias=ln2_bias, w_up=w_up, b_up=b_up, w_down=w_down, b_down=b_down, cotangent=cotangent)


@jax.custom_vjp
def low(v):
    return lax.optimization_barrier(v.astype(jnp.bfloat16)).astype(jnp.float32)

@jax.custom_vjp
def low_back(v):
    return v

def low_keep(v):
    return (low(v), None)

def low_pass(kept, grad):
    return (grad,)

def back_keep(v):
    return (v, None)

def back_low(kept, grad):
    return (low(grad),)
low.defvjp(low_keep, low_pass)
low_back.defvjp(back_keep, back_low)
norm_eps = 1e-05
neg_big = -1e+30
highest = lax.Precision.HIGHEST

def layer_norm(values, gain_vec, bias_vec):
    average = lax.optimization_barrier(jnp.mean(values, axis=-1, keepdims=True))
    centered = values - average
    variance = lax.optimization_barrier(jnp.mean(centered * centered, axis=-1, keepdims=True))
    return centered * lax.rsqrt(variance + norm_eps) * gain_vec + bias_vec

def segment_of(cell_ends, positions):
    return lax.optimization_barrier(jnp.sum((cell_ends[:, None, :] <= positions[None, :, None]).astype(jnp.int32), axis=-1)).astype(jnp.int32)

def attention(query_heads, key_heads, value_heads, segments):
    batch_rows = query_heads.shape[0]
    block_rows = 512 if LENGTH % 512 == 0 else LENGTH
    positions = jnp.arange(LENGTH, dtype=jnp.int32)
    scale_qk = (D // HEADS) ** (-0.5)

    def one_block(block_index):
        start_row = (block_index * block_rows).astype(jnp.int32)
        query_rows = lax.dynamic_slice_in_dim(query_heads, start_row, block_rows, 1)
        query_pos = lax.dynamic_slice_in_dim(positions, start_row, block_rows, 0)
        query_seg = lax.dynamic_slice_in_dim(segments, start_row, block_rows, 1)
        scores = low_back(jnp.einsum('bqhd,bkhd->bqhk', query_rows, key_heads, precision=highest) * scale_qk)
        allowed = (positions[None, None, None, :] <= query_pos[None, :, None, None]) & (segments[:, None, None, :] == query_seg[:, :, None, None])
        scores = jnp.where(allowed, scores, neg_big)
        softmaxed = low(jax.nn.softmax(scores, axis=-1))
        return jnp.einsum('bqhk,bkhd->bqhd', softmaxed, value_heads, precision=highest)
    blocks = lax.map(jax.checkpoint(one_block), jnp.arange(LENGTH // block_rows, dtype=jnp.int32))
    return jnp.transpose(blocks, (1, 0, 2, 3, 4)).reshape(batch_rows, LENGTH, D)

def block_layer(tokens, params, segments):
    ln1_gain, ln1_bias, w_qkv, b_qv, w_o, b_o, ln2_gain, ln2_bias, w_up, b_up, w_down, b_down = params
    batch_rows = tokens.shape[0]
    head_shape = (batch_rows, LENGTH, HEADS, D // HEADS)
    normed = low(layer_norm(tokens, ln1_gain, ln1_bias))
    projected = jnp.dot(normed, w_qkv, precision=highest)
    query_all = low_back(low(projected[..., :D] + b_qv[:D]))
    key_all = low_back(low(projected[..., D:2 * D]))
    value_all = low_back(low(projected[..., 2 * D:] + b_qv[D:]))
    attended = attention(query_all.reshape(head_shape), key_all.reshape(head_shape), value_all.reshape(head_shape), segments)
    attended = low_back(low(attended))
    branch = low_back(jnp.dot(attended, w_o, precision=highest) + b_o)
    middle = tokens + branch
    normed_two = low(layer_norm(middle, ln2_gain, ln2_bias))
    hidden_pre = low_back(jnp.dot(normed_two, w_up, precision=highest) + b_up)
    hidden = low(jax.nn.gelu(hidden_pre))
    feed_out = low_back(jnp.dot(hidden, w_down, precision=highest) + b_down)
    return middle + feed_out

def reference(tokens, seg_lengths, ln1_gain, ln1_bias, w_qkv, b_qv, w_o, b_o, ln2_gain, ln2_bias, w_up, b_up, w_down, b_down, cotangent):
    params = tuple((array.astype(jnp.float32) for array in (ln1_gain, ln1_bias, w_qkv, b_qv, w_o, b_o, ln2_gain, ln2_bias, w_up, b_up, w_down, b_down)))
    positions = jnp.arange(LENGTH, dtype=jnp.int32)
    segments = segment_of(jnp.cumsum(seg_lengths, axis=1).astype(jnp.int32), positions)
    group_rows = math.gcd(SEQS, max(1, 4096 // LENGTH))
    count_groups = SEQS // group_rows
    inputs = tokens.astype(jnp.float32).reshape(count_groups, group_rows, LENGTH, D)
    cotan_rows = cotangent.astype(jnp.float32).reshape(count_groups, group_rows, LENGTH, D)
    seg_groups = segments.reshape(count_groups, group_rows, LENGTH)

    def step_group(totals, batch_items):
        batch_tokens, batch_cotan, batch_segments = batch_items
        result, pullback = jax.vjp(lambda layer_in, weights: block_layer(layer_in, weights, batch_segments), batch_tokens, params)
        grad_tokens, grad_params = pullback(batch_cotan)
        totals = jax.tree.map(jnp.add, totals, grad_params)
        return (totals, (result.astype(jnp.bfloat16), grad_tokens))
    zero_grads = jax.tree.map(jnp.zeros_like, params)
    totals, (outputs, grads_in) = lax.scan(step_group, zero_grads, (inputs, cotan_rows, seg_groups))
    return (outputs.reshape(SEQS, LENGTH, D), grads_in.reshape(SEQS, LENGTH, D), totals[0], totals[1], totals[2], totals[3], totals[4], totals[5], totals[6], totals[7], totals[8], totals[9], totals[10], totals[11])
```

```python
import functools

import jax
import jax.numpy as jnp
from jax import lax
from jax.experimental import pallas as pl
from jax.experimental.pallas import tpu as pltpu
from jax.sharding import PartitionSpec as P

HEADS = 8
norm_eps = 1e-05
neg_big = -1e30
BOTH = ("rows", "blk")
F32 = jnp.float32
BF16 = jnp.bfloat16
TILE = 256
LANES = 128
VMEM_LIMIT = 56 * 1024 * 1024


def mm(lhs, rhs):
    return lax.dot_general(lhs, rhs, (((1,), (0,)), ((), ())), preferred_element_type=F32)


def mm_nt(lhs, rhs):
    return lax.dot_general(lhs, rhs, (((1,), (1,)), ((), ())), preferred_element_type=F32)


def mm_tn(lhs, rhs):
    return lax.dot_general(lhs, rhs, (((0,), (0,)), ((), ())), preferred_element_type=F32)


def cell_start(ends_ref, positions):
    start = jnp.zeros_like(positions)
    for c in range(ends_ref.shape[0]):
        start = jnp.where(ends_ref[c] <= positions, ends_ref[c], start)
    return start


def norm_parts(values):
    average = jnp.mean(values, axis=-1, keepdims=True)
    centered = values - average
    variance = jnp.mean(centered * centered, axis=-1, keepdims=True)
    scale = lax.rsqrt(variance + norm_eps)
    return centered * scale, scale


def norm_pull(e, n, scale, gain):
    f = e * gain
    return (
        f
        - jnp.mean(f, axis=-1, keepdims=True)
        - n * jnp.mean(f * n, axis=-1, keepdims=True)
    ) * scale


def head_lanes(shape, half):
    lane = lax.broadcasted_iota(jnp.int32, shape, len(shape) - 1)
    return (lane < LANES // 2) if half == 0 else (lane >= LANES // 2)


def only_head(values, half):
    return jnp.where(head_lanes(values.shape, half), values, jnp.zeros_like(values))


def forward_kernel(
    ends_ref, x_ref, gain_ref, bias_ref, w_ref, b_ref,
    q_ref, k_ref, v_ref, n1_ref, att_ref, lse_ref,
    mask_ref,
):
    i = pl.program_id(0)
    tiles = pl.num_programs(0)
    del tiles
    width = x_ref.shape[-1]
    pairs = width // LANES
    scale_qk = (width // HEADS) ** (-0.5)
    n, _ = norm_parts(x_ref[...].astype(F32))
    n1 = (n * gain_ref[...] + bias_ref[...]).astype(BF16)
    n1_ref[...] = n1
    rows = pl.ds(pl.multiple_of(i * TILE, TILE), TILE)
    q = mm(n1, w_ref[:, :width]) + b_ref[:, :width]
    q = (q.astype(BF16).astype(F32) * scale_qk).astype(BF16)
    k = mm(n1, w_ref[:, width : 2 * width]).astype(BF16)
    v = (mm(n1, w_ref[:, 2 * width :]) + b_ref[:, width:]).astype(BF16)
    for g in range(pairs):
        cols = slice(g * LANES, (g + 1) * LANES)
        q_ref[g] = q[:, cols]
        k_ref[g, rows, :] = k[:, cols]
        v_ref[g, rows, :] = v[:, cols]

    def attend(tile):
        reach = (tile + 1) * TILE
        q_pos = tile * TILE + lax.broadcasted_iota(jnp.int32, (TILE, 1), 0)
        k_pos = lax.broadcasted_iota(jnp.int32, (TILE, reach), 1)
        start = cell_start(ends_ref, q_pos)
        mask_ref[:, :reach] = jnp.where((k_pos <= q_pos) & (k_pos >= start), 0.0, neg_big)

        def one_pair(g, lse_all):
            qp = q_ref[g]
            kp = k_ref[g, :reach, :]
            vp = v_ref[g, :reach, :]
            outs = []
            for half in range(2):
                s = mm_nt(only_head(qp, half), kp) + mask_ref[:, :reach]
                top = jnp.max(s, axis=-1, keepdims=True)
                p = jnp.exp(s - top)
                total = jnp.sum(p, axis=-1, keepdims=True)
                outs.append(mm(p.astype(BF16), vp) / total)
                lse = top + jnp.log(total)
                lane = lax.broadcasted_iota(jnp.int32, lse_all.shape, 1)
                lse_all = jnp.where(lane == 2 * g + half, lse, lse_all)
            att_ref[g] = jnp.where(head_lanes(outs[0].shape, 0), outs[0], outs[1])
            return lse_all

        lse_all = lax.fori_loop(0, pairs, one_pair, jnp.zeros((TILE, LANES), F32))
        lse_ref[...] = jnp.transpose(lse_all)[:HEADS]

    for tile in range(k_ref.shape[1] // TILE):
        pl.when(i == tile)(functools.partial(attend, tile))


def whole(shape):
    return pl.BlockSpec(shape, lambda i: (0,) * len(shape))


def by_row(cols):
    return pl.BlockSpec((TILE, cols), lambda i: (i, 0))


def by_pair(pairs):
    return pl.BlockSpec((pairs, TILE, LANES), lambda i: (0, i, 0))


def heads_row():
    return pl.BlockSpec((HEADS, TILE), lambda i: (0, i))


SMEM_SPEC = pl.BlockSpec(memory_space=pltpu.SMEM)


def params():
    return pltpu.CompilerParams(
        dimension_semantics=("arbitrary",), vmem_limit_bytes=VMEM_LIMIT
    )


def cost(flops, moved):
    return pl.CostEstimate(flops=int(flops), bytes_accessed=int(moved), transcendentals=0)


def forward_call(ends, x, gain, bias, w_qkv, b_qv):
    t, d = x.shape
    pairs = d // LANES
    return pl.pallas_call(
        forward_kernel,
        grid=(t // TILE,),
        in_specs=[
            SMEM_SPEC, by_row(d), whole((1, d)), whole((1, d)), whole(w_qkv.shape), whole((1, 2 * d)),
        ],
        out_specs=[
            by_pair(pairs), whole((pairs, t, LANES)), whole((pairs, t, LANES)), by_row(d),
            by_pair(pairs), heads_row(),
        ],
        out_shape=[
            jax.ShapeDtypeStruct((pairs, t, LANES), BF16),
            jax.ShapeDtypeStruct((pairs, t, LANES), BF16),
            jax.ShapeDtypeStruct((pairs, t, LANES), BF16),
            jax.ShapeDtypeStruct((t, d), BF16),
            jax.ShapeDtypeStruct((pairs, t, LANES), F32),
            jax.ShapeDtypeStruct((HEADS, t), F32),
        ],
        scratch_shapes=[pltpu.VMEM((TILE, t), F32)],
        compiler_params=params(),
        cost_estimate=cost(15e9, 10e6),
        name="forward",
    )(ends, x, gain[None], bias[None], w_qkv, b_qv[None])


def middle_kernel(
    att_ref, x_ref, cot_ref, wo_ref, bo_ref, gain_ref, bias_ref, wup_ref, bup_ref, wdown_ref, bdown_ref,
    out_ref, gmid_ref, gatt_ref, delta_ref, gwdown_ref, gwup_ref, gwo_ref, vec_ref,
):
    i = pl.program_id(0)
    pairs = att_ref.shape[0]
    d = x_ref.shape[-1]
    ff = wup_ref.shape[-1]

    @pl.when(i == 0)
    def _():
        gwdown_ref[...] = jnp.zeros_like(gwdown_ref)
        gwup_ref[...] = jnp.zeros_like(gwup_ref)
        gwo_ref[...] = jnp.zeros_like(gwo_ref)
        vec_ref[...] = jnp.zeros_like(vec_ref)

    att = jnp.concatenate([att_ref[g] for g in range(pairs)], axis=-1)
    att_b = att.astype(BF16)
    middle = x_ref[...].astype(F32) + mm(att_b, wo_ref[...]) + bo_ref[...]
    n, scale = norm_parts(middle)
    n2 = (n * gain_ref[...] + bias_ref[...]).astype(BF16)
    pre = mm(n2, wup_ref[...]) + bup_ref[...]
    c0 = 0.7978845608028654
    c1 = 0.044715
    sq = pre * pre
    t = jnp.tanh(c0 * (pre + c1 * (sq * pre)))
    half_one = 0.5 * (1.0 + t)
    hidden = (pre * half_one).astype(BF16)
    slope = half_one + (0.5 * pre) * (1.0 - t * t) * (c0 + (3.0 * c0 * c1) * sq)
    out_ref[...] = (middle + mm(hidden, wdown_ref[...]) + bdown_ref[...]).astype(BF16)

    cot = cot_ref[...]
    cot_f = cot.astype(F32)
    gwdown_ref[...] += mm_tn(hidden, cot)
    gpre = (mm_nt(cot, wdown_ref[...]) * slope).astype(BF16)
    gwup_ref[...] += mm_tn(n2, gpre)
    e = mm_nt(gpre, wup_ref[...])
    gmid = cot_f + norm_pull(e, n, scale, gain_ref[...])
    gmid_ref[...] = gmid
    gbr = gmid.astype(BF16)
    gwo_ref[...] += mm_tn(att_b, gbr)
    gatt = mm_nt(gbr, wo_ref[...]).astype(BF16)
    for g in range(pairs):
        gatt_ref[g] = gatt[:, g * LANES : (g + 1) * LANES]
    prod = gatt.astype(F32) * att
    hi = prod.astype(BF16)
    lo = (prod - hi.astype(F32)).astype(BF16)
    head = lax.broadcasted_iota(jnp.int32, (HEADS, d), 0)
    lane = lax.broadcasted_iota(jnp.int32, (HEADS, d), 1)
    ones = jnp.where(lane // (d // HEADS) == head, 1.0, 0.0).astype(BF16)
    delta_ref[...] = mm_nt(ones, hi) + mm_nt(ones, lo)

    def col(values):
        return jnp.sum(values, axis=0, keepdims=True)

    gsum = col(gpre.astype(F32))
    vec_ref[0:1] += col(cot_f)
    vec_ref[1:2] += gsum[:, :d]
    vec_ref[2:3] += gsum[:, d:]
    vec_ref[3:4] += col(e * n)
    vec_ref[4:5] += col(e)
    vec_ref[5:6] += col(gbr.astype(F32))


def middle_call(att, x, cot, w_o, b_o, gain, bias, w_up, b_up, w_down, b_down):
    t, d = x.shape
    pairs = d // LANES
    ff = w_up.shape[1]
    return pl.pallas_call(
        middle_kernel,
        grid=(t // TILE,),
        in_specs=[
            by_pair(pairs), by_row(d), by_row(d), whole((d, d)), whole((1, d)), whole((1, d)), whole((1, d)),
            whole((d, ff)), whole((1, ff)), whole((ff, d)), whole((1, d)),
        ],
        out_specs=[
            by_row(d), by_row(d), by_pair(pairs), heads_row(), whole((ff, d)), whole((d, ff)),
            whole((d, d)), whole((8, d)),
        ],
        out_shape=[
            jax.ShapeDtypeStruct((t, d), BF16),
            jax.ShapeDtypeStruct((t, d), F32),
            jax.ShapeDtypeStruct((pairs, t, LANES), BF16),
            jax.ShapeDtypeStruct((HEADS, t), F32),
            jax.ShapeDtypeStruct((ff, d), F32),
            jax.ShapeDtypeStruct((d, ff), F32),
            jax.ShapeDtypeStruct((d, d), F32),
            jax.ShapeDtypeStruct((8, d), F32),
        ],
        compiler_params=params(),
        cost_estimate=cost(15e9, 20e6),
        name="middle",
    )(att, x, cot, w_o, b_o[None], gain[None], bias[None], w_up, b_up[None], w_down, b_down[None])


def backward_kernel(first, ends_ref, q_ref, k_ref, v_ref, g_ref, lse_ref, delta_ref, dq_ref, dk_ref, dv_ref, acc_ref):
    pair = pl.program_id(0) + first
    t = q_ref.shape[1]
    scale_qk = (LANES // 2) ** (-0.5)
    pos_row = lax.broadcasted_iota(jnp.int32, (1, t), 1)
    start_row = cell_start(ends_ref, pos_row)
    acc_ref[...] = jnp.zeros_like(acc_ref)
    for j in range(t // TILE):
        low = j * TILE
        kp = k_ref[0, low : low + TILE, :]
        vp = v_ref[0, low : low + TILE, :]
        qp = q_ref[0, low:, :]
        gp = g_ref[0, low:, :]
        k_pos = low + lax.broadcasted_iota(jnp.int32, (TILE, t - low), 0)
        allowed = (k_pos >= start_row[:, low:]) & (k_pos <= pos_row[:, low:])
        dks, dvs = [], []
        for half in range(2):
            lse = lse_ref[pl.ds(2 * pair + half, 1), low:]
            delta = delta_ref[pl.ds(2 * pair + half, 1), low:]
            km = only_head(kp, half)
            s = mm_nt(km, qp)
            p = jnp.exp(jnp.where(allowed, s - lse, neg_big))
            dp = mm_nt(only_head(vp, half), gp)
            ds = (p * (dp - delta)).astype(BF16)
            dvs.append(mm(p.astype(BF16), gp))
            dks.append(mm(ds, qp))
            acc_ref[low:, :] += mm_tn(ds, km)
        first_lanes = head_lanes(dks[0].shape, 0)
        dk_ref[0, low : low + TILE, :] = jnp.where(first_lanes, dks[0], dks[1]).astype(BF16)
        dv_ref[0, low : low + TILE, :] = jnp.where(first_lanes, dvs[0], dvs[1]).astype(BF16)
    dq_ref[0] = (acc_ref[...] * scale_qk).astype(BF16)


def backward_call(ends, q, k, v, gatt, lse, delta, first, count):
    pairs, t, _ = q.shape
    spec = pl.BlockSpec((1, t, LANES), lambda i: (i + first, 0, 0))
    out = pl.BlockSpec((1, t, LANES), lambda i: (i, 0, 0))
    return pl.pallas_call(
        functools.partial(backward_kernel, first),
        grid=(count,),
        in_specs=[SMEM_SPEC, spec, spec, spec, spec, whole((HEADS, t)), whole((HEADS, t))],
        out_specs=[out, out, out],
        out_shape=[jax.ShapeDtypeStruct((count, t, LANES), BF16)] * 3,
        scratch_shapes=[pltpu.VMEM((t, LANES), F32)],
        compiler_params=params(),
        cost_estimate=cost(count * 6e9, count * 3e6),
        name="backward",
    )(ends, q, k, v, gatt, lse, delta)


def last_kernel(dq_ref, dk_ref, dv_ref, n1_ref, x_ref, gmid_ref, gain_ref, w_ref, gin_ref, gw_ref, vec_ref):
    i = pl.program_id(0)
    pairs = dq_ref.shape[0]
    d = x_ref.shape[-1]

    @pl.when(i == 0)
    def _():
        gw_ref[...] = jnp.zeros_like(gw_ref)
        vec_ref[...] = jnp.zeros_like(vec_ref)

    parts = [ref[g] for ref in (dq_ref, dk_ref, dv_ref) for g in range(pairs)]
    gqkv = jnp.concatenate(parts, axis=-1)
    gw_ref[...] += mm_tn(n1_ref[...], gqkv)
    e = mm_nt(gqkv, w_ref[...])
    n, scale = norm_parts(x_ref[...].astype(F32))
    gin_ref[...] = (gmid_ref[...] + norm_pull(e, n, scale, gain_ref[...])).astype(BF16)

    def col(values):
        return jnp.sum(values, axis=0, keepdims=True)

    vec_ref[0:1] += col(e * n)
    vec_ref[1:2] += col(e)
    vec_ref[2:3] += col(gqkv[:, :d].astype(F32))
    vec_ref[3:4] += col(gqkv[:, 2 * d :].astype(F32))


def last_call(dq, dk, dv, n1, x, gmid, gain, w_qkv):
    t, d = x.shape
    pairs = d // LANES
    return pl.pallas_call(
        last_kernel,
        grid=(t // TILE,),
        in_specs=[
            by_pair(pairs), by_pair(pairs), by_pair(pairs), by_row(d), by_row(d), by_row(d),
            whole((1, d)), whole(w_qkv.shape),
        ],
        out_specs=[by_row(d), whole((d, 3 * d)), whole((8, d))],
        out_shape=[
            jax.ShapeDtypeStruct((t, d), BF16),
            jax.ShapeDtypeStruct((d, 3 * d), F32),
            jax.ShapeDtypeStruct((8, d), F32),
        ],
        compiler_params=params(),
        cost_estimate=cost(8e9, 12e6),
        name="last",
    )(dq, dk, dv, n1, x, gmid, gain[None], w_qkv)


def device_bits():
    count = lax.axis_size(BOTH)
    me = lax.axis_index("rows") * lax.axis_size("blk") + lax.axis_index("blk")
    return me, count


def send_xor(values, flip):
    count = lax.axis_size(BOTH)
    return lax.ppermute(values, BOTH, [(i, i ^ flip) for i in range(count)])


def piece(values, index, parts):
    size = values.shape[0] // parts
    return lax.dynamic_slice_in_dim(values, index * size, size, 0)


def scatter_stage(values, shift, parts, me):
    mine = (me >> shift) & (parts - 1)
    total = piece(values, mine, parts)
    for flip in range(1, parts):
        sent = piece(values, mine ^ flip, parts).astype(BF16)
        total = total + send_xor(sent, flip << shift).astype(F32)
    return total


def gather_stage(values, shift, parts, me):
    mine = (me >> shift) & (parts - 1)
    out = jnp.zeros((parts,) + values.shape, values.dtype)
    out = lax.dynamic_update_slice_in_dim(out, values[None], mine, 0)
    for flip in range(1, parts):
        out = lax.dynamic_update_slice_in_dim(
            out, send_xor(values, flip << shift)[None], mine ^ flip, 0
        )
    return out.reshape((parts * values.shape[0],) + values.shape[1:])


STAGES = ((0, 2), (1, 4), (3, 4))


def sum_all(values):
    me, _ = device_bits()
    for shift, parts in STAGES:
        values = scatter_stage(values, shift, parts, me)
    values = values.astype(BF16)
    for shift, parts in reversed(STAGES):
        values = gather_stage(values, shift, parts, me)
    return values.astype(F32)


def sum_small(values):
    for shift, parts in STAGES:
        total = values
        for flip in range(1, parts):
            total = total + send_xor(values, flip << shift)
        values = total
    return values


def row_device(
    tokens, seg_lengths, ln1_gain, ln1_bias, w_qkv, b_qv, w_o, b_o, ln2_gain, ln2_bias,
    w_up, b_up, w_down, b_down, cotangent,
):
    row_count, slice_len, d = tokens.shape
    t = row_count * slice_len
    ff = w_up.shape[1]
    row = lax.axis_index("blk")
    ends = jnp.cumsum(seg_lengths, axis=1)
    ends = lax.dynamic_index_in_dim(ends, row, 0, keepdims=False).astype(jnp.int32)

    def swap(values):
        return lax.all_to_all(values, "blk", 0, 0, tiled=True)

    x = swap(tokens).reshape(t, d)
    cot = swap(cotangent).reshape(t, d)
    q, k, v, n1, att, lse = forward_call(ends, x, ln1_gain, ln1_bias, w_qkv, b_qv)
    out, gmid, gatt, delta, gw_down, gw_up, gw_o, vec_mid = middle_call(
        att, x, cot, w_o, b_o, ln2_gain, ln2_bias, w_up, b_up, w_down, b_down
    )
    output = swap(out.reshape(row_count, slice_len, d))
    dq, dk, dv = backward_call(ends, q, k, v, gatt, lse, delta, 0, d // LANES)
    gin, gw_qkv, vec_last = last_call(dq, dk, dv, n1, x, gmid, ln1_gain, w_qkv)
    input_grad = swap(gin.reshape(row_count, slice_len, d)).astype(F32)
    first = jnp.concatenate([gw_down, gw_up[:, :d], gw_up[:, d:], gw_o], axis=0)
    first = sum_all(first)
    second = jnp.concatenate([gw_qkv[:, :d], gw_qkv[:, d : 2 * d], gw_qkv[:, 2 * d :]], axis=0)
    second = sum_all(second)
    vec = sum_small(jnp.concatenate([vec_mid, vec_last], axis=0))
    return (
        output,
        input_grad,
        vec[8],
        vec[9],
        jnp.concatenate([second[:d], second[d : 2 * d], second[2 * d :]], axis=1),
        jnp.concatenate([vec[10], vec[11]]),
        first[ff + 2 * d :],
        vec[5],
        vec[3],
        vec[4],
        jnp.concatenate([first[ff : ff + d], first[ff + d : ff + 2 * d]], axis=1),
        jnp.concatenate([vec[1], vec[2]]),
        first[:ff],
        vec[0],
    )


def layer_norm(values, gain_vec, bias_vec):
    average = jnp.mean(values, axis=-1, keepdims=True)
    centered = values - average
    variance = jnp.mean(centered * centered, axis=-1, keepdims=True)
    return centered * lax.rsqrt(variance + norm_eps) * gain_vec + bias_vec


def segment_of(cell_ends, positions):
    return jnp.sum((cell_ends[:, None, :] <= positions[None, :, None]).astype(jnp.int32), axis=-1)


def block_scores(query_heads, key_heads, query_pos, key_pos, query_seg, key_seg, scale_qk):
    raw_scores = (
        jnp.einsum("rqhd,rkhd->rqhk", query_heads, key_heads, preferred_element_type=jnp.float32)
        * scale_qk
    )
    causal = key_pos[None, :] <= query_pos[:, None]
    same_cell = query_seg[:, :, None] == key_seg[:, None, :]
    allowed = (causal[None] & same_cell)[:, :, None, :]
    return (jnp.where(allowed, raw_scores, neg_big), allowed)


def block_active(query_pos, key_pos, query_seg, key_seg):
    return (key_pos[0] <= query_pos[-1]) & jnp.any(key_seg[:, -1] >= query_seg[:, 0])


def backward_block(
    query_heads,
    grad_heads,
    log_total,
    delta_sum,
    key_heads,
    value_heads,
    query_pos,
    key_pos,
    query_seg,
    key_seg,
    scale_qk,
):
    scores, allowed = block_scores(
        query_heads, key_heads, query_pos, key_pos, query_seg, key_seg, scale_qk
    )
    softmaxed = jnp.where(allowed, jnp.exp(scores - log_total[..., None]), 0.0)
    grad_probs = jnp.einsum(
        "rqhd,rkhd->rqhk", grad_heads, value_heads, preferred_element_type=jnp.float32
    )
    grad_scores = (softmaxed * (grad_probs - delta_sum[..., None])).astype(jnp.bfloat16)
    grad_query = (
        jnp.einsum("rqhk,rkhd->rqhd", grad_scores, key_heads, preferred_element_type=jnp.float32)
        * scale_qk
    )
    grad_key = (
        jnp.einsum("rqhk,rqhd->rkhd", grad_scores, query_heads, preferred_element_type=jnp.float32)
        * scale_qk
    )
    grad_value = jnp.einsum(
        "rqhk,rqhd->rkhd",
        softmaxed.astype(jnp.bfloat16),
        grad_heads,
        preferred_element_type=jnp.float32,
    )
    return (grad_query, grad_key, grad_value)


def unchanged(old_state):
    return old_state


def general_device(
    tokens,
    seg_lengths,
    ln1_gain,
    ln1_bias,
    w_qkv,
    b_qv,
    w_o,
    b_o,
    ln2_gain,
    ln2_bias,
    w_up,
    b_up,
    w_down,
    b_down,
    cotangent,
):
    row_count, slice_len, width_all = tokens.shape
    head_size = width_all // HEADS
    scale_qk = head_size ** (-0.5)
    head_shape = (row_count, slice_len, HEADS, head_size)
    stat_shape = (row_count, slice_len, HEADS)
    full_length = lax.axis_size("blk") * slice_len
    offsets = jnp.arange(slice_len, dtype=jnp.int32)
    query_pos = lax.axis_index("blk") * slice_len + offsets
    cell_ends = jnp.cumsum(seg_lengths, axis=1)
    query_seg = segment_of(cell_ends, query_pos)

    def take_block(piece, block_index):
        return lax.dynamic_slice_in_dim(piece, block_index * slice_len, slice_len, 1).reshape(
            head_shape
        )

    inputs = tokens.astype(jnp.float32)
    normed_val, first_pull = jax.vjp(layer_norm, inputs, ln1_gain, ln1_bias)
    normed_one = normed_val.astype(jnp.bfloat16)
    projected = jnp.dot(normed_one, w_qkv, preferred_element_type=jnp.float32)
    query_b = (projected[..., :width_all] + b_qv[:width_all]).astype(jnp.bfloat16)
    key_b = projected[..., width_all : 2 * width_all].astype(jnp.bfloat16)
    value_b = (projected[..., 2 * width_all :] + b_qv[width_all:]).astype(jnp.bfloat16)
    query_heads = query_b.reshape(head_shape)
    start_state = (
        jnp.full(stat_shape, neg_big, jnp.float32),
        jnp.zeros(stat_shape, jnp.float32),
        jnp.zeros(head_shape, jnp.float32),
    )
    key_piece = lax.all_gather(key_b, "blk", axis=1, tiled=True)
    value_piece = lax.all_gather(value_b, "blk", axis=1, tiled=True)

    def forward_block_step(block_index, inner_state):
        key_pos = block_index * slice_len + offsets
        key_seg = segment_of(cell_ends, key_pos)
        key_heads = take_block(key_piece, block_index)
        value_heads = take_block(value_piece, block_index)

        def forward_update(old_state):
            running_top, running_total, running_sum = old_state
            scores, allowed = block_scores(
                query_heads, key_heads, query_pos, key_pos, query_seg, key_seg, scale_qk
            )
            new_top = jnp.maximum(running_top, jnp.max(scores, axis=-1))
            factor = jnp.exp(running_top - new_top)
            weights_now = jnp.where(allowed, jnp.exp(scores - new_top[..., None]), 0.0)
            new_total = running_total * factor + jnp.sum(weights_now, axis=-1)
            new_sum = running_sum * factor[..., None] + jnp.einsum(
                "rqhk,rkhd->rqhd",
                weights_now.astype(jnp.bfloat16),
                value_heads,
                preferred_element_type=jnp.float32,
            )
            return (new_top, new_total, new_sum)

        return lax.cond(
            block_active(query_pos, key_pos, query_seg, key_seg),
            forward_update,
            unchanged,
            inner_state,
        )

    running_top, running_total, running_sum = lax.fori_loop(
        0, key_piece.shape[1] // slice_len, forward_block_step, start_state
    )
    attn_f32 = (running_sum / running_total[..., None]).reshape(row_count, slice_len, width_all)
    log_total = running_top + jnp.log(running_total)
    attn_b = attn_f32.astype(jnp.bfloat16)
    middle = inputs + jnp.dot(attn_b, w_o, preferred_element_type=jnp.float32) + b_o
    normed_two_val, second_pull = jax.vjp(layer_norm, middle, ln2_gain, ln2_bias)
    normed_two = normed_two_val.astype(jnp.bfloat16)
    hidden_pre = jnp.dot(normed_two, w_up, preferred_element_type=jnp.float32) + b_up
    hidden_val, gelu_pull = jax.vjp(jax.nn.gelu, hidden_pre)
    hidden_b = hidden_val.astype(jnp.bfloat16)
    output = (
        middle + jnp.dot(hidden_b, w_down, preferred_element_type=jnp.float32) + b_down
    ).astype(jnp.bfloat16)
    grad_out = cotangent.astype(jnp.float32)
    grad_w_down = jnp.einsum("rcf,rcd->fd", hidden_b, cotangent, preferred_element_type=jnp.float32)
    grad_b_down = jnp.sum(grad_out, axis=(0, 1))
    grad_hidden = jnp.einsum("rcd,fd->rcf", cotangent, w_down, preferred_element_type=jnp.float32)
    (grad_pre,) = gelu_pull(grad_hidden)
    grad_pre_b = grad_pre.astype(jnp.bfloat16)
    grad_w_up = jnp.einsum(
        "rcd,rcf->df", normed_two, grad_pre_b, preferred_element_type=jnp.float32
    )
    grad_b_up = jnp.sum(grad_pre_b.astype(jnp.float32), axis=(0, 1))
    grad_normed_two = jnp.einsum(
        "rcf,df->rcd", grad_pre_b, w_up, preferred_element_type=jnp.float32
    )
    grad_mid_norm, grad_ln2_gain, grad_ln2_bias = second_pull(grad_normed_two)
    grad_middle = grad_out + grad_mid_norm
    grad_branch_b = grad_middle.astype(jnp.bfloat16)
    grad_w_o = jnp.einsum("rce,rcd->ed", attn_b, grad_branch_b, preferred_element_type=jnp.float32)
    grad_b_o = jnp.sum(grad_branch_b.astype(jnp.float32), axis=(0, 1))
    grad_attn_b = jnp.einsum(
        "rcd,ed->rce", grad_branch_b, w_o, preferred_element_type=jnp.float32
    ).astype(jnp.bfloat16)
    delta_sum = jnp.sum((grad_attn_b.astype(jnp.float32) * attn_f32).reshape(head_shape), axis=-1)
    grad_heads = grad_attn_b.reshape(head_shape)
    whole_shape = (row_count, full_length, HEADS, head_size)
    back_state = (
        jnp.zeros(head_shape, jnp.float32),
        jnp.zeros(whole_shape, jnp.float32),
        jnp.zeros(whole_shape, jnp.float32),
    )
    backward_key_piece = lax.all_gather(key_b, "blk", axis=1, tiled=True)
    backward_value_piece = lax.all_gather(value_b, "blk", axis=1, tiled=True)

    def backward_block_step(block_index, inner_state):
        key_pos = block_index * slice_len + offsets
        key_seg = segment_of(cell_ends, key_pos)
        key_heads = take_block(backward_key_piece, block_index)
        value_heads = take_block(backward_value_piece, block_index)

        def backward_update(old_state):
            grad_query, grad_key, grad_value = backward_block(
                query_heads,
                grad_heads,
                log_total,
                delta_sum,
                key_heads,
                value_heads,
                query_pos,
                key_pos,
                query_seg,
                key_seg,
                scale_qk,
            )
            at_row = block_index * slice_len
            return (
                old_state[0] + grad_query,
                lax.dynamic_update_slice_in_dim(old_state[1], grad_key, at_row, 1),
                lax.dynamic_update_slice_in_dim(old_state[2], grad_value, at_row, 1),
            )

        return lax.cond(
            block_active(query_pos, key_pos, query_seg, key_seg),
            backward_update,
            unchanged,
            inner_state,
        )

    back_result = lax.fori_loop(
        0, backward_key_piece.shape[1] // slice_len, backward_block_step, back_state
    )
    grad_query_sum = back_result[0]
    grad_key_sum, grad_value_sum = (
        lax.psum_scatter(
            back_result[1].astype(jnp.bfloat16), "blk", scatter_dimension=1, tiled=True
        ).astype(jnp.float32),
        lax.psum_scatter(
            back_result[2].astype(jnp.bfloat16), "blk", scatter_dimension=1, tiled=True
        ).astype(jnp.float32),
    )
    flat_shape = (row_count, slice_len, width_all)
    grad_qkv_b = jnp.concatenate(
        [
            grad_query_sum.reshape(flat_shape),
            grad_key_sum.reshape(flat_shape),
            grad_value_sum.reshape(flat_shape),
        ],
        axis=-1,
    ).astype(jnp.bfloat16)
    grad_w_qkv = jnp.einsum(
        "rcd,rce->de", normed_one, grad_qkv_b, preferred_element_type=jnp.float32
    )
    column_sums = jnp.sum(grad_qkv_b.astype(jnp.float32), axis=(0, 1))
    grad_b_qv = jnp.concatenate([column_sums[:width_all], column_sums[2 * width_all :]])
    grad_normed_one = jnp.einsum(
        "rce,de->rcd", grad_qkv_b, w_qkv, preferred_element_type=jnp.float32
    )
    grad_in_norm, grad_ln1_gain, grad_ln1_bias = first_pull(grad_normed_one)
    input_grad = grad_middle + grad_in_norm
    grads = (
        grad_ln1_gain,
        grad_ln1_bias,
        grad_w_qkv,
        grad_b_qv,
        grad_w_o,
        grad_b_o,
        grad_ln2_gain,
        grad_ln2_bias,
        grad_w_up,
        grad_b_up,
        grad_w_down,
        grad_b_down,
    )
    summed = lax.psum(
        (
            grads[0],
            grads[1],
            grads[2],
            grads[3],
            grads[4],
            grads[5],
            grads[6],
            grads[7],
            grads[8],
            grads[9],
            grads[10],
            grads[11],
        ),
        ("rows", "blk"),
    )
    return (
        output,
        input_grad,
        summed[0],
        summed[1],
        summed[2],
        summed[3],
        summed[4],
        summed[5],
        summed[6],
        summed[7],
        summed[8],
        summed[9],
        summed[10],
        summed[11],
    )


def device_function(tokens, *rest):
    d = tokens.shape[2]
    whole_rows = (
        lax.axis_size("blk") == tokens.shape[0] == 4
        and lax.axis_size("rows") == 8
        and tokens.shape[1] == TILE
        and d == 512
    )
    return (row_device if whole_rows else general_device)(tokens, *rest)


def solution(mesh):
    in_specs = (
        P("rows", "blk", None),
        P("rows", None),
        P(),
        P(),
        P(),
        P(),
        P(),
        P(),
        P(),
        P(),
        P(),
        P(),
        P(),
        P(),
        P("rows", "blk", None),
    )
    out_specs = (
        P("rows", "blk", None),
        P("rows", "blk", None),
        P(),
        P(),
        P(),
        P(),
        P(),
        P(),
        P(),
        P(),
        P(),
        P(),
        P(),
        P(),
    )
    return jax.shard_map(
        device_function, mesh=mesh, in_specs=in_specs, out_specs=out_specs, check_vma=False
    )
```

```python
import functools

import jax
import jax.numpy as jnp
from jax import lax
from jax.experimental import pallas as pl
from jax.experimental.pallas import tpu as pltpu
from jax.sharding import PartitionSpec as P

HEADS = 8
norm_eps = 1e-05
neg_big = -1e30
BOTH = ("rows", "blk")
F32 = jnp.float32
BF16 = jnp.bfloat16
TILE = 256
LANES = 128
MIB = 1024 * 1024
B_FLOPS = 1e9
L_FLOPS = 1e9
MID_TILE = 512
MID_MIB = 28
LAST_MIB = 26


def mm(lhs, rhs):
    return lax.dot_general(lhs, rhs, (((1,), (0,)), ((), ())), preferred_element_type=F32)


def mm_nt(lhs, rhs):
    return lax.dot_general(lhs, rhs, (((1,), (1,)), ((), ())), preferred_element_type=F32)


def mm_tn(lhs, rhs):
    return lax.dot_general(lhs, rhs, (((0,), (0,)), ((), ())), preferred_element_type=F32)


def cell_start(ends_ref, positions):
    start = jnp.zeros_like(positions)
    for c in range(ends_ref.shape[0]):
        start = jnp.where(ends_ref[c] <= positions, ends_ref[c], start)
    return start


def norm_parts(values):
    average = jnp.mean(values, axis=-1, keepdims=True)
    centered = values - average
    variance = jnp.mean(centered * centered, axis=-1, keepdims=True)
    scale = lax.rsqrt(variance + norm_eps)
    return centered * scale, scale


def norm_pull(e, n, scale, gain):
    f = e * gain
    return (
        f
        - jnp.mean(f, axis=-1, keepdims=True)
        - n * jnp.mean(f * n, axis=-1, keepdims=True)
    ) * scale


def head_lanes(shape, half):
    lane = lax.broadcasted_iota(jnp.int32, shape, len(shape) - 1)
    return (lane < LANES // 2) if half == 0 else (lane >= LANES // 2)


def only_head(values, half):
    return jnp.where(head_lanes(values.shape, half), values, jnp.zeros_like(values))


def in_order(blk_ref, pieces, whole_ref):
    size = pieces[0].shape[0]
    for flip, piece_ref in enumerate(pieces):
        at = jnp.bitwise_xor(blk_ref[0], flip) * size
        whole_ref[pl.ds(pl.multiple_of(at, size), size), :] = piece_ref[...]


def forward_kernel(
    ends_ref, blk_ref, x0_ref, x1_ref, x2_ref, x3_ref, gain_ref, bias_ref, w_ref, b_ref,
    x_ref, q_ref, k_ref, v_ref, n1_ref, att_ref, lse_ref,
    mask_ref,
):
    i = pl.program_id(0)

    @pl.when(i == 0)
    def _():
        in_order(blk_ref, (x0_ref, x1_ref, x2_ref, x3_ref), x_ref)

    width = x_ref.shape[-1]
    pairs = width // LANES
    scale_qk = (width // HEADS) ** (-0.5)
    rows = pl.ds(pl.multiple_of(i * TILE, TILE), TILE)
    n, _ = norm_parts(x_ref[rows, :].astype(F32))
    n1 = (n * gain_ref[...] + bias_ref[...]).astype(BF16)
    n1_ref[...] = n1
    q = mm(n1, w_ref[:, :width]) + b_ref[:, :width]
    q = (q.astype(BF16).astype(F32) * scale_qk).astype(BF16)
    k = mm(n1, w_ref[:, width : 2 * width]).astype(BF16)
    v = (mm(n1, w_ref[:, 2 * width :]) + b_ref[:, width:]).astype(BF16)
    for g in range(pairs):
        cols = slice(g * LANES, (g + 1) * LANES)
        q_ref[g] = q[:, cols]
        k_ref[g, rows, :] = k[:, cols]
        v_ref[g, rows, :] = v[:, cols]

    def attend(tile):
        reach = (tile + 1) * TILE
        q_pos = tile * TILE + lax.broadcasted_iota(jnp.int32, (TILE, 1), 0)
        k_pos = lax.broadcasted_iota(jnp.int32, (TILE, reach), 1)
        start = cell_start(ends_ref, q_pos)
        mask_ref[:, :reach] = jnp.where((k_pos <= q_pos) & (k_pos >= start), 0.0, neg_big)

        def one_pair(g, lse_all):
            qp = q_ref[g]
            kp = k_ref[g, :reach, :]
            vp = v_ref[g, :reach, :]
            outs = []
            for half in range(2):
                s = mm_nt(only_head(qp, half), kp) + mask_ref[:, :reach]
                top = jnp.max(s, axis=-1, keepdims=True)
                p = jnp.exp(s - top)
                total = jnp.sum(p, axis=-1, keepdims=True)
                outs.append(mm(p.astype(BF16), vp) / total)
                lse = top + jnp.log(total)
                lane = lax.broadcasted_iota(jnp.int32, lse_all.shape, 1)
                lse_all = jnp.where(lane == 2 * g + half, lse, lse_all)
            att_ref[g] = jnp.where(head_lanes(outs[0].shape, 0), outs[0], outs[1])
            return lse_all

        lse_all = lax.fori_loop(0, pairs, one_pair, jnp.zeros((TILE, LANES), F32))
        lse_ref[...] = jnp.transpose(lse_all)[:HEADS]

    for tile in range(k_ref.shape[1] // TILE):
        pl.when(i == tile)(functools.partial(attend, tile))


def whole(shape):
    return pl.BlockSpec(shape, lambda i: (0,) * len(shape))


def by_row(cols, tile=TILE):
    return pl.BlockSpec((tile, cols), lambda i: (i, 0))


def by_pair(pairs, tile=TILE):
    return pl.BlockSpec((pairs, tile, LANES), lambda i: (0, i, 0))


def heads_row(tile=TILE):
    return pl.BlockSpec((HEADS, tile), lambda i: (0, i))


SMEM_SPEC = pl.BlockSpec(memory_space=pltpu.SMEM)


def params(mib):
    return pltpu.CompilerParams(dimension_semantics=("arbitrary",), vmem_limit_bytes=mib * MIB)


def cost(flops, moved):
    return pl.CostEstimate(flops=int(flops), bytes_accessed=int(moved), transcendentals=0)


def forward_call(ends, blk, pieces, gain, bias, w_qkv, b_qv):
    size, d = pieces[0].shape
    t = size * len(pieces)
    pairs = d // LANES
    return pl.pallas_call(
        forward_kernel,
        grid=(t // TILE,),
        in_specs=[SMEM_SPEC, SMEM_SPEC]
        + [whole((size, d))] * len(pieces)
        + [whole((1, d)), whole((1, d)), whole(w_qkv.shape), whole((1, 2 * d))],
        out_specs=[
            whole((t, d)), by_pair(pairs), whole((pairs, t, LANES)), whole((pairs, t, LANES)), by_row(d),
            by_pair(pairs), heads_row(),
        ],
        out_shape=[
            jax.ShapeDtypeStruct((t, d), BF16),
            pltpu.HBM((pairs, t, LANES), BF16),
            pltpu.HBM((pairs, t, LANES), BF16),
            pltpu.HBM((pairs, t, LANES), BF16),
            pltpu.HBM((t, d), BF16),
            jax.ShapeDtypeStruct((pairs, t, LANES), F32),
            jax.ShapeDtypeStruct((HEADS, t), F32),
        ],
        scratch_shapes=[pltpu.VMEM((TILE, t), F32)],
        compiler_params=params(28),
        cost_estimate=cost(20e9, 10e6),
        name="forward",
    )(ends, blk, *pieces, gain[None], bias[None], w_qkv, b_qv[None])


def split_halves(core_ref, whole_ref, keep_ref, send_ref):
    half = keep_ref.shape[0]
    core = core_ref[0]
    keep_ref[...] = whole_ref[pl.ds(pl.multiple_of(core * half, half), half), :]
    send_ref[...] = whole_ref[pl.ds(pl.multiple_of((1 - core) * half, half), half), :].astype(BF16)


def middle_kernel(
    core_ref, blk_ref, att_ref, x_ref, c0_ref, c1_ref, c2_ref, c3_ref, wo_ref, bo_ref, gain_ref, bias_ref, wup_ref, bup_ref, wdown_ref, bdown_ref,
    out_ref, gmid_ref, gatt_ref, delta_ref, keep_ref, send_ref, vec_ref,
    cot_ref, gw_ref, hidden_ref, gpre_ref, n2_ref, attb_ref, gbr_ref,
):
    pairs = att_ref.shape[0]
    t, d = x_ref.shape
    ff = wup_ref.shape[-1]
    c0 = 0.7978845608028654
    c1 = 0.044715

    def col(values):
        return jnp.sum(values, axis=0, keepdims=True)

    in_order(blk_ref, (c0_ref, c1_ref, c2_ref, c3_ref), cot_ref)
    vec_ref[...] = jnp.zeros_like(vec_ref)
    head = lax.broadcasted_iota(jnp.int32, (HEADS, d), 0)
    lane = lax.broadcasted_iota(jnp.int32, (HEADS, d), 1)
    ones = jnp.where(lane // (d // HEADS) == head, 1.0, 0.0).astype(BF16)
    for low in range(0, t, MID_TILE):
        rows = slice(low, low + MID_TILE)
        att = jnp.concatenate([att_ref[g, rows, :] for g in range(pairs)], axis=-1)
        att_b = att.astype(BF16)
        attb_ref[rows] = att_b
        middle = x_ref[rows].astype(F32) + mm(att_b, wo_ref[...]) + bo_ref[...]
        n, scale = norm_parts(middle)
        n2 = (n * gain_ref[...] + bias_ref[...]).astype(BF16)
        n2_ref[rows] = n2
        pre = mm(n2, wup_ref[...]) + bup_ref[...]
        sq = pre * pre
        th = jnp.tanh(c0 * (pre + c1 * (sq * pre)))
        half_one = 0.5 * (1.0 + th)
        hidden = (pre * half_one).astype(BF16)
        hidden_ref[rows] = hidden
        slope = half_one + (0.5 * pre) * (1.0 - th * th) * (c0 + (3.0 * c0 * c1) * sq)
        out_ref[rows] = (middle + mm(hidden, wdown_ref[...]) + bdown_ref[...]).astype(BF16)
        cot = cot_ref[rows]
        cot_f = cot.astype(F32)
        gpre = (mm_nt(cot, wdown_ref[...]) * slope).astype(BF16)
        gpre_ref[rows] = gpre
        e = mm_nt(gpre, wup_ref[...])
        gmid = cot_f + norm_pull(e, n, scale, gain_ref[...])
        gmid_ref[rows] = gmid
        gbr = gmid.astype(BF16)
        gbr_ref[rows] = gbr
        gatt = mm_nt(gbr, wo_ref[...]).astype(BF16)
        for g in range(pairs):
            gatt_ref[g, rows, :] = gatt[:, g * LANES : (g + 1) * LANES]
        prod = gatt.astype(F32) * att
        hi = prod.astype(BF16)
        lo = (prod - hi.astype(F32)).astype(BF16)
        delta_ref[:, rows] = mm_nt(ones, hi) + mm_nt(ones, lo)
        gsum = col(gpre.astype(F32))
        vec_ref[0:1] += col(cot_f)
        vec_ref[1:2] += gsum[:, :d]
        vec_ref[2:3] += gsum[:, d:]
        vec_ref[3:4] += col(e * n)
        vec_ref[4:5] += col(e)
        vec_ref[5:6] += col(gbr.astype(F32))
    gw_ref[:ff] = mm_tn(hidden_ref[...], cot_ref[...])
    gw_ref[ff : ff + d] = mm_tn(n2_ref[...], gpre_ref[:, :d])
    gw_ref[ff + d : ff + 2 * d] = mm_tn(n2_ref[...], gpre_ref[:, d:])
    gw_ref[ff + 2 * d :] = mm_tn(attb_ref[...], gbr_ref[...])
    split_halves(core_ref, gw_ref, keep_ref, send_ref)


def middle_call(core, blk, att, x, cots, w_o, b_o, gain, bias, w_up, b_up, w_down, b_down):
    t, d = x.shape
    pairs = d // LANES
    ff = w_up.shape[1]
    half = (ff + 3 * d) // 2
    return pl.pallas_call(
        middle_kernel,
        grid=(1,),
        in_specs=[
            SMEM_SPEC, SMEM_SPEC,
            by_pair(pairs, t), by_row(d, t), *[whole(c.shape) for c in cots], whole((d, d)), whole((1, d)), whole((1, d)), whole((1, d)),
            whole((d, ff)), whole((1, ff)), whole((ff, d)), whole((1, d)),
        ],
        out_specs=[
            by_row(d, t), by_row(d, t), by_pair(pairs, t), heads_row(t), whole((half, d)), whole((half, d)),
            whole((8, d)),
        ],
        out_shape=[
            jax.ShapeDtypeStruct((t, d), BF16),
            pltpu.HBM((t, d), F32),
            pltpu.HBM((pairs, t, LANES), BF16),
            jax.ShapeDtypeStruct((HEADS, t), F32),
            jax.ShapeDtypeStruct((half, d), F32),
            jax.ShapeDtypeStruct((half, d), BF16),
            jax.ShapeDtypeStruct((8, d), F32),
        ],
        scratch_shapes=[
            pltpu.VMEM((t, d), BF16),
            pltpu.VMEM((2 * half, d), F32),
            pltpu.VMEM((t, ff), BF16),
            pltpu.VMEM((t, ff), BF16),
            pltpu.VMEM((t, d), BF16),
            pltpu.VMEM((t, d), BF16),
            pltpu.VMEM((t, d), BF16),
        ],
        compiler_params=params(28),
        cost_estimate=cost(15e9, 20e6),
        name="middle",
    )(core, blk, att, x, *cots, w_o, b_o[None], gain[None], bias[None], w_up, b_up[None], w_down, b_down[None])


def backward_kernel(first, ends_ref, q_ref, k_ref, v_ref, g_ref, lse_ref, delta_ref, dq_ref, dk_ref, dv_ref, acc_ref):
    pair = pl.program_id(0) + first
    t = q_ref.shape[1]
    scale_qk = (LANES // 2) ** (-0.5)
    pos_row = lax.broadcasted_iota(jnp.int32, (1, t), 1)
    start_row = cell_start(ends_ref, pos_row)
    acc_ref[...] = jnp.zeros_like(acc_ref)

    for j in range(t // TILE):
        low = j * TILE
        kp = k_ref[0, low : low + TILE, :]
        vp = v_ref[0, low : low + TILE, :]
        kt = jnp.transpose(kp)
        qp = q_ref[0, low:, :]
        gp = g_ref[0, low:, :]
        k_pos = low + lax.broadcasted_iota(jnp.int32, (TILE, t - low), 0)
        allowed = (k_pos >= start_row[:, low:]) & (k_pos <= pos_row[:, low:])
        dks, dvs = [], []
        for half in range(2):
            lse = lse_ref[pl.ds(2 * pair + half, 1), low:]
            delta = delta_ref[pl.ds(2 * pair + half, 1), low:]
            rows = slice(half * 64, half * 64 + 64)
            s = mm_nt(only_head(kp, half), qp)
            p = jnp.exp(jnp.where(allowed, s - lse, neg_big))
            dp = mm_nt(only_head(vp, half), gp)
            ds = (p * (dp - delta)).astype(BF16)
            dvs.append(mm(p.astype(BF16), gp))
            dks.append(mm(ds, qp))
            acc_ref[rows, low:] += mm(kt[rows], ds)
        first_lanes = head_lanes(dks[0].shape, 0)
        dk_ref[0, low : low + TILE, :] = jnp.where(first_lanes, dks[0], dks[1]).astype(BF16)
        dv_ref[0, low : low + TILE, :] = jnp.where(first_lanes, dvs[0], dvs[1]).astype(BF16)
    dq_ref[0] = jnp.transpose((acc_ref[...] * scale_qk)).astype(BF16)


def backward_call(ends, q, k, v, gatt, lse, delta, first, count):
    pairs, t, _ = q.shape
    spec = pl.BlockSpec((1, t, LANES), lambda i: (i + first, 0, 0))
    out = pl.BlockSpec((1, t, LANES), lambda i: (i, 0, 0))
    return pl.pallas_call(
        functools.partial(backward_kernel, first),
        grid=(count,),
        in_specs=[SMEM_SPEC, spec, spec, spec, spec, whole((HEADS, t)), whole((HEADS, t))],
        out_specs=[out, out, out],
        out_shape=[jax.ShapeDtypeStruct((count, t, LANES), BF16)] * 3,
        scratch_shapes=[pltpu.VMEM((LANES, t), F32)],
        compiler_params=params(28),
        cost_estimate=cost(count * B_FLOPS, count * 1e5),
        name="backward",
    )(ends, *(pltpu.with_memory_space_constraint(a, pltpu.HBM) for a in (q, k, v, gatt)), lse, delta)


VEC_ROWS = 128


def last_kernel(*refs):
    core_ref = refs[0]
    pairs = (len(refs) - 11) // 3
    grads = refs[1 : 1 + 3 * pairs]
    n1_ref, x_ref, gmid_ref, gain_ref, w_ref, vecmid_ref = refs[1 + 3 * pairs : 7 + 3 * pairs]
    gin_ref, keep_ref, send_ref, gw_ref = refs[7 + 3 * pairs :]
    d = x_ref.shape[-1]
    half = keep_ref.shape[0]
    gqkv = jnp.concatenate([grads[3 * g + part][0] for part in range(3) for g in range(pairs)], axis=-1)
    gw = mm_tn(n1_ref[...], gqkv)
    blocks = 3 * pairs
    for p in range(blocks):
        at = (p // (blocks // 2)) * half + (p % (blocks // 2)) * d
        gw_ref[at : at + d] = gw[:, p * LANES : (p + 1) * LANES]
    e = mm_nt(gqkv, w_ref[...])
    n, scale = norm_parts(x_ref[...].astype(F32))
    gin_ref[...] = (gmid_ref[...] + norm_pull(e, n, scale, gain_ref[...])).astype(BF16)

    def col(values):
        return jnp.sum(values, axis=0, keepdims=True)

    rows = [vecmid_ref[r : r + 1] for r in range(6)]
    rows += [col(e * n), col(e), col(gqkv[:, :d].astype(F32)), col(gqkv[:, 2 * d :].astype(F32))]
    base = half - VEC_ROWS
    gw_ref[base:half] = jnp.zeros((VEC_ROWS, LANES), F32)
    gw_ref[half + base :] = jnp.zeros((VEC_ROWS, LANES), F32)
    for r, row in enumerate(rows):
        for g in range(d // LANES):
            at = base + r * (d // LANES) + g
            gw_ref[at : at + 1] = row[:, g * LANES : (g + 1) * LANES]
    split_halves(core_ref, gw_ref, keep_ref, send_ref)


def last_call(core, grads, n1, x, gmid, gain, w_qkv, vec_mid):
    t, d = x.shape
    half = 3 * d * d // LANES // 2 + VEC_ROWS
    return pl.pallas_call(
        last_kernel,
        grid=(1,),
        in_specs=[SMEM_SPEC]
        + [whole(a.shape) for a in grads]
        + [by_row(d, t), by_row(d, t), by_row(d, t), whole((1, d)), whole(w_qkv.shape), whole((8, d))],
        out_specs=[by_row(d, t), whole((half, LANES)), whole((half, LANES))],
        out_shape=[
            jax.ShapeDtypeStruct((t, d), BF16),
            jax.ShapeDtypeStruct((half, LANES), F32),
            jax.ShapeDtypeStruct((half, LANES), BF16),
        ],
        scratch_shapes=[pltpu.VMEM((2 * half, LANES), F32)],
        compiler_params=params(28),
        cost_estimate=cost(L_FLOPS, 1e5),
        name="last",
    )(core, *grads, n1, x, gmid, gain[None], w_qkv, vec_mid)


def ordered_halves(core_ref, own_ref, got_ref, write):
    pl.when(core_ref[0] == 0)(functools.partial(write, own_ref, got_ref))
    pl.when(core_ref[0] == 1)(functools.partial(write, got_ref, own_ref))


def finish_mid_kernel(core_ref, own_ref, got_ref, down_ref, up_ref, wo_ref):
    ff, d = down_ref.shape
    half = own_ref.shape[0]

    def write(low_ref, high_ref):
        def take(first, last):
            if last <= half:
                return low_ref[first:last].astype(F32)
            if first >= half:
                return high_ref[first - half : last - half].astype(F32)
            return jnp.concatenate([take(first, half), take(half, last)], axis=0)

        down_ref[...] = take(0, ff)
        up_ref[:, :d] = take(ff, ff + d)
        up_ref[:, d:] = take(ff + d, ff + 2 * d)
        wo_ref[...] = take(ff + 2 * d, ff + 3 * d)

    ordered_halves(core_ref, own_ref, got_ref, write)


def finish_last_kernel(core_ref, own_ref, got_ref, qkv_ref, vec_ref):
    d = qkv_ref.shape[0]
    half = own_ref.shape[0]
    blocks = qkv_ref.shape[1] // LANES

    def write(low_ref, high_ref):
        for p in range(blocks):
            ref = (low_ref, high_ref)[p // (blocks // 2)]
            at = (p % (blocks // 2)) * d
            qkv_ref[:, p * LANES : (p + 1) * LANES] = ref[at : at + d].astype(F32)
        vec_ref[...] = low_ref[half - VEC_ROWS :].astype(F32)

    ordered_halves(core_ref, own_ref, got_ref, write)


def finish_call(kernel, core, own, got, shapes, name):
    return pl.pallas_call(
        kernel,
        grid=(1,),
        in_specs=[SMEM_SPEC, whole(own.shape), whole(got.shape)],
        out_specs=[whole(shape) for shape in shapes],
        out_shape=[jax.ShapeDtypeStruct(shape, F32) for shape in shapes],
        compiler_params=params(28),
        cost_estimate=cost(1e8, 8e6),
        name=name,
    )(core, own, got)


def send_xor(values, flip):
    count = lax.axis_size(BOTH)
    return lax.ppermute(values, BOTH, [(i, i ^ flip) for i in range(count)])


def add_kernel(place_ref, *refs):
    outs = place_ref.shape[0]
    terms, results = refs[:-outs], refs[-outs:]
    size = results[0].shape[0]
    for flip, result in enumerate(results):
        rows = pl.ds(pl.multiple_of(jnp.bitwise_xor(place_ref[0], flip) * size, size), size)
        total = terms[0][rows, :].astype(F32)
        for term in terms[1:]:
            total = total + term[rows, :].astype(F32)
        result[...] = total.astype(result.dtype)


def add_call(place, parts, terms, own_dtype):
    rows, lanes = terms[0].shape
    shape = (rows // parts, lanes)
    places = jnp.broadcast_to(place, (parts,)).astype(jnp.int32)
    return pl.pallas_call(
        add_kernel,
        grid=(1,),
        in_specs=[SMEM_SPEC] + [whole(a.shape) for a in terms],
        out_specs=[whole(shape)] * parts,
        out_shape=[jax.ShapeDtypeStruct(shape, own_dtype if p == 0 else BF16) for p in range(parts)],
        compiler_params=params(28),
        cost_estimate=cost(1e8, 4e6),
        name="add",
    )(places, *terms)


def join_kernel(place_ref, *refs):
    out_ref = refs[-1]
    for flip, ref in enumerate(refs[:-1]):
        size = ref.shape[0]
        rows = pl.ds(pl.multiple_of(jnp.bitwise_xor(place_ref[0], flip) * size, size), size)
        out_ref[rows, :] = ref[...]


def join_call(place, pieces):
    rows, lanes = pieces[0].shape
    shape = (rows * len(pieces), lanes)
    return pl.pallas_call(
        join_kernel,
        grid=(1,),
        in_specs=[SMEM_SPEC] + [whole(p.shape) for p in pieces],
        out_specs=whole(shape),
        out_shape=jax.ShapeDtypeStruct(shape, pieces[0].dtype),
        compiler_params=params(28),
        cost_estimate=cost(1e8, 2e6),
        name="join",
    )(place[None].astype(jnp.int32), *pieces)


def swap_parts(parts, shift):
    return [send_xor(part, (flip + 1) << shift) for flip, part in enumerate(parts)]


def spread(part, shift, parts):
    return [send_xor(part, flip << shift) for flip in range(1, parts)]


def after(values, *others):
    return lax.optimization_barrier((values,) + others)[0]


def row_device(
    tokens, seg_lengths, ln1_gain, ln1_bias, w_qkv, b_qv, w_o, b_o, ln2_gain, ln2_bias,
    w_up, b_up, w_down, b_down, cotangent,
):
    row_count, slice_len, d = tokens.shape
    row = lax.axis_index("blk")
    me = lax.axis_index("rows") * lax.axis_size("blk") + row
    place_core = me & 1
    place_plane = (me >> 1) & 3
    place_deep = me >> 3
    core = place_core[None].astype(jnp.int32)
    blk = row[None].astype(jnp.int32)
    ends = jnp.cumsum(seg_lengths, axis=1)
    ends = lax.dynamic_index_in_dim(ends, row, 0, keepdims=False).astype(jnp.int32)

    def cut(values):
        return [lax.dynamic_index_in_dim(values, row ^ flip, 0, keepdims=False) for flip in range(row_count)]

    def swap(pieces):
        return [pieces[0]] + swap_parts(pieces[1:], 0)

    x = swap(cut(tokens))
    cot = cut(cotangent)
    cot = lax.optimization_barrier(tuple(cot) + tuple(x))[:row_count]
    cot = swap(list(cot))
    x, q, k, v, n1, att, lse = forward_call(ends, blk, x, ln1_gain, ln1_bias, w_qkv, b_qv)
    out, gmid, gatt, delta, keep, send, vec_mid = middle_call(
        core, blk, att, x, cot, w_o, b_o, ln2_gain, ln2_bias, w_up, b_up, w_down, b_down
    )

    def home(values):
        return lax.all_to_all(values.reshape(tokens.shape), "blk", 0, 0, tiled=True)

    def grads(pair, *deps):
        return backward_call(after(ends, *deps), q, k, v, gatt, lse, delta, pair, 1)

    g0 = grads(0)
    own, *parts = add_call(place_plane, 4, [keep, send_xor(send, 1)], F32)
    g1 = grads(1, own, g0[0])
    g2 = grads(2, g1[0])
    own, *parts = add_call(place_deep, 4, [own] + swap_parts(parts, 1), F32)
    g3 = grads(3, own, g2[0])
    output = home(after(out, own))
    (first,) = add_call(0, 1, [own] + swap_parts(parts, 3), BF16)
    gin, keep, send = last_call(
        after(core, first), (*g0, *g1, *g2, *g3), n1, x, gmid, ln1_gain, w_qkv, vec_mid
    )
    first = join_call(place_deep, [first] + spread(first, 3, 4))
    place = after(place_plane, first, output)
    own, *parts = add_call(place, 4, [keep, send_xor(send, 1)], F32)
    first, *parts = lax.optimization_barrier((first, *parts))
    second = swap_parts(parts, 1)
    own, *parts = add_call(place_deep, 4, [own] + second, F32)
    first, gin = lax.optimization_barrier((first, gin, own))[:2]
    first = join_call(place_plane & 1, [first] + spread(first, 1, 2))
    first = join_call(place_plane >> 1, [first] + spread(first, 2, 2))
    gin = home(gin)
    (second,) = add_call(0, 1, [own] + swap_parts(parts, 3), BF16)
    gw_down, gw_up, gw_o = finish_call(
        finish_mid_kernel, core, first, send_xor(first, 1), [w_down.shape, w_up.shape, w_o.shape], "finish_mid"
    )
    second = join_call(place_deep, [second] + spread(second, 3, 4))
    second, gin = lax.optimization_barrier((second, gin))
    second = join_call(place_plane, [second] + spread(second, 1, 4))
    input_grad = gin.astype(F32)
    gw_qkv, vec = finish_call(
        finish_last_kernel, core, second, send_xor(second, 1), [w_qkv.shape, (VEC_ROWS, LANES)], "finish_last"
    )
    vec = vec.reshape(-1, d)
    return (
        output,
        input_grad,
        vec[6],
        vec[7],
        gw_qkv,
        jnp.concatenate([vec[8], vec[9]]),
        gw_o,
        vec[5],
        vec[3],
        vec[4],
        gw_up,
        jnp.concatenate([vec[1], vec[2]]),
        gw_down,
        vec[0],
    )


def layer_norm(values, gain_vec, bias_vec):
    average = jnp.mean(values, axis=-1, keepdims=True)
    centered = values - average
    variance = jnp.mean(centered * centered, axis=-1, keepdims=True)
    return centered * lax.rsqrt(variance + norm_eps) * gain_vec + bias_vec


def segment_of(cell_ends, positions):
    return jnp.sum((cell_ends[:, None, :] <= positions[None, :, None]).astype(jnp.int32), axis=-1)


def block_scores(query_heads, key_heads, query_pos, key_pos, query_seg, key_seg, scale_qk):
    raw_scores = (
        jnp.einsum("rqhd,rkhd->rqhk", query_heads, key_heads, preferred_element_type=jnp.float32)
        * scale_qk
    )
    causal = key_pos[None, :] <= query_pos[:, None]
    same_cell = query_seg[:, :, None] == key_seg[:, None, :]
    allowed = (causal[None] & same_cell)[:, :, None, :]
    return (jnp.where(allowed, raw_scores, neg_big), allowed)


def block_active(query_pos, key_pos, query_seg, key_seg):
    return (key_pos[0] <= query_pos[-1]) & jnp.any(key_seg[:, -1] >= query_seg[:, 0])


def backward_block(
    query_heads,
    grad_heads,
    log_total,
    delta_sum,
    key_heads,
    value_heads,
    query_pos,
    key_pos,
    query_seg,
    key_seg,
    scale_qk,
):
    scores, allowed = block_scores(
        query_heads, key_heads, query_pos, key_pos, query_seg, key_seg, scale_qk
    )
    softmaxed = jnp.where(allowed, jnp.exp(scores - log_total[..., None]), 0.0)
    grad_probs = jnp.einsum(
        "rqhd,rkhd->rqhk", grad_heads, value_heads, preferred_element_type=jnp.float32
    )
    grad_scores = (softmaxed * (grad_probs - delta_sum[..., None])).astype(jnp.bfloat16)
    grad_query = (
        jnp.einsum("rqhk,rkhd->rqhd", grad_scores, key_heads, preferred_element_type=jnp.float32)
        * scale_qk
    )
    grad_key = (
        jnp.einsum("rqhk,rqhd->rkhd", grad_scores, query_heads, preferred_element_type=jnp.float32)
        * scale_qk
    )
    grad_value = jnp.einsum(
        "rqhk,rqhd->rkhd",
        softmaxed.astype(jnp.bfloat16),
        grad_heads,
        preferred_element_type=jnp.float32,
    )
    return (grad_query, grad_key, grad_value)


def unchanged(old_state):
    return old_state


def general_device(
    tokens,
    seg_lengths,
    ln1_gain,
    ln1_bias,
    w_qkv,
    b_qv,
    w_o,
    b_o,
    ln2_gain,
    ln2_bias,
    w_up,
    b_up,
    w_down,
    b_down,
    cotangent,
):
    row_count, slice_len, width_all = tokens.shape
    head_size = width_all // HEADS
    scale_qk = head_size ** (-0.5)
    head_shape = (row_count, slice_len, HEADS, head_size)
    stat_shape = (row_count, slice_len, HEADS)
    full_length = lax.axis_size("blk") * slice_len
    offsets = jnp.arange(slice_len, dtype=jnp.int32)
    query_pos = lax.axis_index("blk") * slice_len + offsets
    cell_ends = jnp.cumsum(seg_lengths, axis=1)
    query_seg = segment_of(cell_ends, query_pos)

    def take_block(piece, block_index):
        return lax.dynamic_slice_in_dim(piece, block_index * slice_len, slice_len, 1).reshape(
            head_shape
        )

    inputs = tokens.astype(jnp.float32)
    normed_val, first_pull = jax.vjp(layer_norm, inputs, ln1_gain, ln1_bias)
    normed_one = normed_val.astype(jnp.bfloat16)
    projected = jnp.dot(normed_one, w_qkv, preferred_element_type=jnp.float32)
    query_b = (projected[..., :width_all] + b_qv[:width_all]).astype(jnp.bfloat16)
    key_b = projected[..., width_all : 2 * width_all].astype(jnp.bfloat16)
    value_b = (projected[..., 2 * width_all :] + b_qv[width_all:]).astype(jnp.bfloat16)
    query_heads = query_b.reshape(head_shape)
    start_state = (
        jnp.full(stat_shape, neg_big, jnp.float32),
        jnp.zeros(stat_shape, jnp.float32),
        jnp.zeros(head_shape, jnp.float32),
    )
    key_piece = lax.all_gather(key_b, "blk", axis=1, tiled=True)
    value_piece = lax.all_gather(value_b, "blk", axis=1, tiled=True)

    def forward_block_step(block_index, inner_state):
        key_pos = block_index * slice_len + offsets
        key_seg = segment_of(cell_ends, key_pos)
        key_heads = take_block(key_piece, block_index)
        value_heads = take_block(value_piece, block_index)

        def forward_update(old_state):
            running_top, running_total, running_sum = old_state
            scores, allowed = block_scores(
                query_heads, key_heads, query_pos, key_pos, query_seg, key_seg, scale_qk
            )
            new_top = jnp.maximum(running_top, jnp.max(scores, axis=-1))
            factor = jnp.exp(running_top - new_top)
            weights_now = jnp.where(allowed, jnp.exp(scores - new_top[..., None]), 0.0)
            new_total = running_total * factor + jnp.sum(weights_now, axis=-1)
            new_sum = running_sum * factor[..., None] + jnp.einsum(
                "rqhk,rkhd->rqhd",
                weights_now.astype(jnp.bfloat16),
                value_heads,
                preferred_element_type=jnp.float32,
            )
            return (new_top, new_total, new_sum)

        return lax.cond(
            block_active(query_pos, key_pos, query_seg, key_seg),
            forward_update,
            unchanged,
            inner_state,
        )

    running_top, running_total, running_sum = lax.fori_loop(
        0, key_piece.shape[1] // slice_len, forward_block_step, start_state
    )
    attn_f32 = (running_sum / running_total[..., None]).reshape(row_count, slice_len, width_all)
    log_total = running_top + jnp.log(running_total)
    attn_b = attn_f32.astype(jnp.bfloat16)
    middle = inputs + jnp.dot(attn_b, w_o, preferred_element_type=jnp.float32) + b_o
    normed_two_val, second_pull = jax.vjp(layer_norm, middle, ln2_gain, ln2_bias)
    normed_two = normed_two_val.astype(jnp.bfloat16)
    hidden_pre = jnp.dot(normed_two, w_up, preferred_element_type=jnp.float32) + b_up
    hidden_val, gelu_pull = jax.vjp(jax.nn.gelu, hidden_pre)
    hidden_b = hidden_val.astype(jnp.bfloat16)
    output = (
        middle + jnp.dot(hidden_b, w_down, preferred_element_type=jnp.float32) + b_down
    ).astype(jnp.bfloat16)
    grad_out = cotangent.astype(jnp.float32)
    grad_w_down = jnp.einsum("rcf,rcd->fd", hidden_b, cotangent, preferred_element_type=jnp.float32)
    grad_b_down = jnp.sum(grad_out, axis=(0, 1))
    grad_hidden = jnp.einsum("rcd,fd->rcf", cotangent, w_down, preferred_element_type=jnp.float32)
    (grad_pre,) = gelu_pull(grad_hidden)
    grad_pre_b = grad_pre.astype(jnp.bfloat16)
    grad_w_up = jnp.einsum(
        "rcd,rcf->df", normed_two, grad_pre_b, preferred_element_type=jnp.float32
    )
    grad_b_up = jnp.sum(grad_pre_b.astype(jnp.float32), axis=(0, 1))
    grad_normed_two = jnp.einsum(
        "rcf,df->rcd", grad_pre_b, w_up, preferred_element_type=jnp.float32
    )
    grad_mid_norm, grad_ln2_gain, grad_ln2_bias = second_pull(grad_normed_two)
    grad_middle = grad_out + grad_mid_norm
    grad_branch_b = grad_middle.astype(jnp.bfloat16)
    grad_w_o = jnp.einsum("rce,rcd->ed", attn_b, grad_branch_b, preferred_element_type=jnp.float32)
    grad_b_o = jnp.sum(grad_branch_b.astype(jnp.float32), axis=(0, 1))
    grad_attn_b = jnp.einsum(
        "rcd,ed->rce", grad_branch_b, w_o, preferred_element_type=jnp.float32
    ).astype(jnp.bfloat16)
    delta_sum = jnp.sum((grad_attn_b.astype(jnp.float32) * attn_f32).reshape(head_shape), axis=-1)
    grad_heads = grad_attn_b.reshape(head_shape)
    whole_shape = (row_count, full_length, HEADS, head_size)
    back_state = (
        jnp.zeros(head_shape, jnp.float32),
        jnp.zeros(whole_shape, jnp.float32),
        jnp.zeros(whole_shape, jnp.float32),
    )
    backward_key_piece = lax.all_gather(key_b, "blk", axis=1, tiled=True)
    backward_value_piece = lax.all_gather(value_b, "blk", axis=1, tiled=True)

    def backward_block_step(block_index, inner_state):
        key_pos = block_index * slice_len + offsets
        key_seg = segment_of(cell_ends, key_pos)
        key_heads = take_block(backward_key_piece, block_index)
        value_heads = take_block(backward_value_piece, block_index)

        def backward_update(old_state):
            grad_query, grad_key, grad_value = backward_block(
                query_heads,
                grad_heads,
                log_total,
                delta_sum,
                key_heads,
                value_heads,
                query_pos,
                key_pos,
                query_seg,
                key_seg,
                scale_qk,
            )
            at_row = block_index * slice_len
            return (
                old_state[0] + grad_query,
                lax.dynamic_update_slice_in_dim(old_state[1], grad_key, at_row, 1),
                lax.dynamic_update_slice_in_dim(old_state[2], grad_value, at_row, 1),
            )

        return lax.cond(
            block_active(query_pos, key_pos, query_seg, key_seg),
            backward_update,
            unchanged,
            inner_state,
        )

    back_result = lax.fori_loop(
        0, backward_key_piece.shape[1] // slice_len, backward_block_step, back_state
    )
    grad_query_sum = back_result[0]
    grad_key_sum, grad_value_sum = (
        lax.psum_scatter(
            back_result[1].astype(jnp.bfloat16), "blk", scatter_dimension=1, tiled=True
        ).astype(jnp.float32),
        lax.psum_scatter(
            back_result[2].astype(jnp.bfloat16), "blk", scatter_dimension=1, tiled=True
        ).astype(jnp.float32),
    )
    flat_shape = (row_count, slice_len, width_all)
    grad_qkv_b = jnp.concatenate(
        [
            grad_query_sum.reshape(flat_shape),
            grad_key_sum.reshape(flat_shape),
            grad_value_sum.reshape(flat_shape),
        ],
        axis=-1,
    ).astype(jnp.bfloat16)
    grad_w_qkv = jnp.einsum(
        "rcd,rce->de", normed_one, grad_qkv_b, preferred_element_type=jnp.float32
    )
    column_sums = jnp.sum(grad_qkv_b.astype(jnp.float32), axis=(0, 1))
    grad_b_qv = jnp.concatenate([column_sums[:width_all], column_sums[2 * width_all :]])
    grad_normed_one = jnp.einsum(
        "rce,de->rcd", grad_qkv_b, w_qkv, preferred_element_type=jnp.float32
    )
    grad_in_norm, grad_ln1_gain, grad_ln1_bias = first_pull(grad_normed_one)
    input_grad = grad_middle + grad_in_norm
    grads = (
        grad_ln1_gain,
        grad_ln1_bias,
        grad_w_qkv,
        grad_b_qv,
        grad_w_o,
        grad_b_o,
        grad_ln2_gain,
        grad_ln2_bias,
        grad_w_up,
        grad_b_up,
        grad_w_down,
        grad_b_down,
    )
    summed = lax.psum(
        (
            grads[0],
            grads[1],
            grads[2],
            grads[3],
            grads[4],
            grads[5],
            grads[6],
            grads[7],
            grads[8],
            grads[9],
            grads[10],
            grads[11],
        ),
        ("rows", "blk"),
    )
    return (
        output,
        input_grad,
        summed[0],
        summed[1],
        summed[2],
        summed[3],
        summed[4],
        summed[5],
        summed[6],
        summed[7],
        summed[8],
        summed[9],
        summed[10],
        summed[11],
    )


def device_function(tokens, *rest):
    d = tokens.shape[2]
    whole_rows = (
        lax.axis_size("blk") == tokens.shape[0] == 4
        and lax.axis_size("rows") == 8
        and tokens.shape[1] == TILE
        and d == 512
    )
    return (row_device if whole_rows else general_device)(tokens, *rest)


def solution(mesh):
    in_specs = (
        P("rows", "blk", None),
        P("rows", None),
        P(),
        P(),
        P(),
        P(),
        P(),
        P(),
        P(),
        P(),
        P(),
        P(),
        P(),
        P(),
        P("rows", "blk", None),
    )
    out_specs = (
        P("rows", "blk", None),
        P("rows", "blk", None),
        P(),
        P(),
        P(),
        P(),
        P(),
        P(),
        P(),
        P(),
        P(),
        P(),
        P(),
        P(),
    )
    return jax.shard_map(
        device_function, mesh=mesh, in_specs=in_specs, out_specs=out_specs, check_vma=False
    )
```

```python
import functools

import jax
import jax.numpy as jnp
from jax import lax
from jax.experimental import pallas as pl
from jax.experimental.pallas import tpu as pltpu
from jax.sharding import PartitionSpec as P

HEADS = 8
norm_eps = 1e-05
neg_big = -1e30
BOTH = ("rows", "blk")
F32 = jnp.float32
BF16 = jnp.bfloat16
TILE = 256
LANES = 128
MIB = 1024 * 1024
B_FLOPS = 1e9
L_FLOPS = 1e9
MID_TILE = 512
MID_MIB = 28
LAST_MIB = 26


def mm(lhs, rhs):
    return lax.dot_general(lhs, rhs, (((1,), (0,)), ((), ())), preferred_element_type=F32)


def mm_nt(lhs, rhs):
    return lax.dot_general(lhs, rhs, (((1,), (1,)), ((), ())), preferred_element_type=F32)


def mm_tn(lhs, rhs):
    return lax.dot_general(lhs, rhs, (((0,), (0,)), ((), ())), preferred_element_type=F32)


def cell_start(ends_ref, positions):
    start = jnp.zeros_like(positions)
    for c in range(ends_ref.shape[0]):
        start = jnp.where(ends_ref[c] <= positions, ends_ref[c], start)
    return start


def norm_parts(values):
    average = jnp.mean(values, axis=-1, keepdims=True)
    centered = values - average
    variance = jnp.mean(centered * centered, axis=-1, keepdims=True)
    scale = lax.rsqrt(variance + norm_eps)
    return centered * scale, scale


def norm_pull(e, n, scale, gain):
    f = e * gain
    return (
        f
        - jnp.mean(f, axis=-1, keepdims=True)
        - n * jnp.mean(f * n, axis=-1, keepdims=True)
    ) * scale


def head_lanes(shape, half):
    lane = lax.broadcasted_iota(jnp.int32, shape, len(shape) - 1)
    return (lane < LANES // 2) if half == 0 else (lane >= LANES // 2)


def only_head(values, half):
    return jnp.where(head_lanes(values.shape, half), values, jnp.zeros_like(values))


def in_order(blk_ref, pieces, whole_ref):
    size = pieces[0].shape[0]
    for flip, piece_ref in enumerate(pieces):
        at = jnp.bitwise_xor(blk_ref[0], flip) * size
        whole_ref[pl.ds(pl.multiple_of(at, size), size), :] = piece_ref[...]


def forward_kernel(
    ends_ref, blk_ref, x0_ref, x1_ref, x2_ref, x3_ref, gain_ref, bias_ref, w_ref, b_ref,
    x_ref, q_ref, k_ref, v_ref, n1_ref, att_ref, lse_ref,
    mask_ref,
):
    in_order(blk_ref, (x0_ref, x1_ref, x2_ref, x3_ref), x_ref)
    t, width = x_ref.shape
    pairs = width // LANES
    scale_qk = (width // HEADS) ** (-0.5)
    for low in range(0, t, 512):
        rows = slice(low, low + 512)
        n, _ = norm_parts(x_ref[rows].astype(F32))
        n1 = (n * gain_ref[...] + bias_ref[...]).astype(BF16)
        n1_ref[rows] = n1
        q = mm(n1, w_ref[:, :width]) + b_ref[:, :width]
        q = (q.astype(BF16).astype(F32) * scale_qk).astype(BF16)
        k = mm(n1, w_ref[:, width : 2 * width]).astype(BF16)
        v = (mm(n1, w_ref[:, 2 * width :]) + b_ref[:, width:]).astype(BF16)
        for g in range(pairs):
            cols = slice(g * LANES, (g + 1) * LANES)
            q_ref[g, rows, :] = q[:, cols]
            k_ref[g, rows, :] = k[:, cols]
            v_ref[g, rows, :] = v[:, cols]
    for low in range(0, t, TILE):
        reach = low + TILE
        rows = slice(low, reach)
        q_pos = low + lax.broadcasted_iota(jnp.int32, (TILE, 1), 0)
        k_pos = lax.broadcasted_iota(jnp.int32, (TILE, reach), 1)
        start = cell_start(ends_ref, q_pos)
        mask_ref[:, :reach] = jnp.where((k_pos <= q_pos) & (k_pos >= start), 0.0, neg_big)
        lse_all = jnp.zeros((TILE, LANES), F32)
        lane = lax.broadcasted_iota(jnp.int32, lse_all.shape, 1)
        for g in range(pairs):
            qp = q_ref[g, rows, :]
            kp = k_ref[g, :reach, :]
            vp = v_ref[g, :reach, :]
            outs = []
            for half in range(2):
                s = mm_nt(only_head(qp, half), kp) + mask_ref[:, :reach]
                top = jnp.max(s, axis=-1, keepdims=True)
                p = jnp.exp(s - top)
                total = jnp.sum(p, axis=-1, keepdims=True)
                outs.append(mm(p.astype(BF16), vp) / total)
                lse_all = jnp.where(lane == 2 * g + half, top + jnp.log(total), lse_all)
            att_ref[g, rows, :] = jnp.where(head_lanes(outs[0].shape, 0), outs[0], outs[1])
        lse_ref[:, rows] = jnp.transpose(lse_all)[:HEADS]


def whole(shape):
    return pl.BlockSpec(shape, lambda i: (0,) * len(shape))


def by_row(cols, tile=TILE):
    return pl.BlockSpec((tile, cols), lambda i: (i, 0))


def by_pair(pairs, tile=TILE):
    return pl.BlockSpec((pairs, tile, LANES), lambda i: (0, i, 0))


def heads_row(tile=TILE):
    return pl.BlockSpec((HEADS, tile), lambda i: (0, i))


SMEM_SPEC = pl.BlockSpec(memory_space=pltpu.SMEM)


def params(mib):
    return pltpu.CompilerParams(dimension_semantics=("arbitrary",), vmem_limit_bytes=mib * MIB)


def cost(flops, moved):
    return pl.CostEstimate(flops=int(flops), bytes_accessed=int(moved), transcendentals=0)


def forward_call(ends, blk, pieces, gain, bias, w_qkv, b_qv):
    size, d = pieces[0].shape
    t = size * len(pieces)
    pairs = d // LANES
    return pl.pallas_call(
        forward_kernel,
        grid=(1,),
        in_specs=[SMEM_SPEC, SMEM_SPEC]
        + [whole((size, d))] * len(pieces)
        + [whole((1, d)), whole((1, d)), whole(w_qkv.shape), whole((1, 2 * d))],
        out_specs=[
            whole((t, d)), whole((pairs, t, LANES)), whole((pairs, t, LANES)), whole((pairs, t, LANES)), whole((t, d)),
            whole((pairs, t, LANES)), whole((HEADS, t)),
        ],
        out_shape=[
            jax.ShapeDtypeStruct((t, d), BF16),
            pltpu.HBM((pairs, t, LANES), BF16),
            pltpu.HBM((pairs, t, LANES), BF16),
            pltpu.HBM((pairs, t, LANES), BF16),
            pltpu.HBM((t, d), BF16),
            jax.ShapeDtypeStruct((pairs, t, LANES), F32),
            jax.ShapeDtypeStruct((HEADS, t), F32),
        ],
        scratch_shapes=[pltpu.VMEM((TILE, t), F32)],
        compiler_params=params(34),
        cost_estimate=cost(20e9, 10e6),
        name="forward",
    )(ends, blk, *pieces, gain[None], bias[None], w_qkv, b_qv[None])


def split_halves(core_ref, whole_ref, keep_ref, send_ref):
    half = keep_ref.shape[0]
    core = core_ref[0]
    keep_ref[...] = whole_ref[pl.ds(pl.multiple_of(core * half, half), half), :]
    send_ref[...] = whole_ref[pl.ds(pl.multiple_of((1 - core) * half, half), half), :].astype(BF16)


def middle_kernel(
    core_ref, blk_ref, att_ref, x_ref, c0_ref, c1_ref, c2_ref, c3_ref, wo_ref, bo_ref, gain_ref, bias_ref, wup_ref, bup_ref, wdown_ref, bdown_ref,
    out_ref, gmid_ref, gatt_ref, delta_ref, keep_ref, send_ref, vec_ref,
    cot_ref, gw_ref, hidden_ref, gpre_ref, n2_ref, attb_ref, gbr_ref,
):
    pairs = att_ref.shape[0]
    t, d = x_ref.shape
    ff = wup_ref.shape[-1]
    c0 = 0.7978845608028654
    c1 = 0.044715

    def col(values):
        return jnp.sum(values, axis=0, keepdims=True)

    in_order(blk_ref, (c0_ref, c1_ref, c2_ref, c3_ref), cot_ref)
    vec_ref[...] = jnp.zeros_like(vec_ref)
    head = lax.broadcasted_iota(jnp.int32, (HEADS, d), 0)
    lane = lax.broadcasted_iota(jnp.int32, (HEADS, d), 1)
    ones = jnp.where(lane // (d // HEADS) == head, 1.0, 0.0).astype(BF16)
    for low in range(0, t, MID_TILE):
        rows = slice(low, low + MID_TILE)
        att = jnp.concatenate([att_ref[g, rows, :] for g in range(pairs)], axis=-1)
        att_b = att.astype(BF16)
        attb_ref[rows] = att_b
        middle = x_ref[rows].astype(F32) + mm(att_b, wo_ref[...]) + bo_ref[...]
        n, scale = norm_parts(middle)
        n2 = (n * gain_ref[...] + bias_ref[...]).astype(BF16)
        n2_ref[rows] = n2
        pre = mm(n2, wup_ref[...]) + bup_ref[...]
        sq = pre * pre
        th = jnp.tanh(c0 * (pre + c1 * (sq * pre)))
        half_one = 0.5 * (1.0 + th)
        hidden = (pre * half_one).astype(BF16)
        hidden_ref[rows] = hidden
        slope = half_one + (0.5 * pre) * (1.0 - th * th) * (c0 + (3.0 * c0 * c1) * sq)
        out_ref[rows] = (middle + mm(hidden, wdown_ref[...]) + bdown_ref[...]).astype(BF16)
        cot = cot_ref[rows]
        cot_f = cot.astype(F32)
        gpre = (mm_nt(cot, wdown_ref[...]) * slope).astype(BF16)
        gpre_ref[rows] = gpre
        e = mm_nt(gpre, wup_ref[...])
        gmid = cot_f + norm_pull(e, n, scale, gain_ref[...])
        gmid_ref[rows] = gmid
        gbr = gmid.astype(BF16)
        gbr_ref[rows] = gbr
        gatt = mm_nt(gbr, wo_ref[...]).astype(BF16)
        for g in range(pairs):
            gatt_ref[g, rows, :] = gatt[:, g * LANES : (g + 1) * LANES]
        prod = gatt.astype(F32) * att
        hi = prod.astype(BF16)
        lo = (prod - hi.astype(F32)).astype(BF16)
        delta_ref[:, rows] = mm_nt(ones, hi) + mm_nt(ones, lo)
        gsum = col(gpre.astype(F32))
        vec_ref[0:1] += col(cot_f)
        vec_ref[1:2] += gsum[:, :d]
        vec_ref[2:3] += gsum[:, d:]
        vec_ref[3:4] += col(e * n)
        vec_ref[4:5] += col(e)
        vec_ref[5:6] += col(gbr.astype(F32))
    gw_ref[:ff] = mm_tn(hidden_ref[...], cot_ref[...])
    gw_ref[ff : ff + d] = mm_tn(n2_ref[...], gpre_ref[:, :d])
    gw_ref[ff + d : ff + 2 * d] = mm_tn(n2_ref[...], gpre_ref[:, d:])
    gw_ref[ff + 2 * d :] = mm_tn(attb_ref[...], gbr_ref[...])
    split_halves(core_ref, gw_ref, keep_ref, send_ref)


def middle_call(core, blk, att, x, cots, w_o, b_o, gain, bias, w_up, b_up, w_down, b_down):
    t, d = x.shape
    pairs = d // LANES
    ff = w_up.shape[1]
    half = (ff + 3 * d) // 2
    return pl.pallas_call(
        middle_kernel,
        grid=(1,),
        in_specs=[
            SMEM_SPEC, SMEM_SPEC,
            by_pair(pairs, t), by_row(d, t), *[whole(c.shape) for c in cots], whole((d, d)), whole((1, d)), whole((1, d)), whole((1, d)),
            whole((d, ff)), whole((1, ff)), whole((ff, d)), whole((1, d)),
        ],
        out_specs=[
            by_row(d, t), by_row(d, t), by_pair(pairs, t), heads_row(t), whole((half, d)), whole((half, d)),
            whole((8, d)),
        ],
        out_shape=[
            pltpu.HBM((t, d), BF16),
            pltpu.HBM((t, d), F32),
            pltpu.HBM((pairs, t, LANES), BF16),
            jax.ShapeDtypeStruct((HEADS, t), F32),
            jax.ShapeDtypeStruct((half, d), F32),
            jax.ShapeDtypeStruct((half, d), BF16),
            jax.ShapeDtypeStruct((8, d), F32),
        ],
        scratch_shapes=[
            pltpu.VMEM((t, d), BF16),
            pltpu.VMEM((2 * half, d), F32),
            pltpu.VMEM((t, ff), BF16),
            pltpu.VMEM((t, ff), BF16),
            pltpu.VMEM((t, d), BF16),
            pltpu.VMEM((t, d), BF16),
            pltpu.VMEM((t, d), BF16),
        ],
        compiler_params=params(28),
        cost_estimate=cost(15e9, 20e6),
        name="middle",
    )(core, blk, att, x, *cots, w_o, b_o[None], gain[None], bias[None], w_up, b_up[None], w_down, b_down[None])


def backward_kernel(first, ends_ref, q_ref, k_ref, v_ref, g_ref, lse_ref, delta_ref, dq_ref, dk_ref, dv_ref, acc_ref):
    pair = pl.program_id(0) + first
    t = q_ref.shape[1]
    scale_qk = (LANES // 2) ** (-0.5)
    pos_row = lax.broadcasted_iota(jnp.int32, (1, t), 1)
    start_row = cell_start(ends_ref, pos_row)
    acc_ref[...] = jnp.zeros_like(acc_ref)
    jobs = [(j, half) for j in range(t // TILE) for half in range(2)]
    lses = [lse_ref[pl.ds(2 * pair + half, 1), :] for half in range(2)]
    deltas = [delta_ref[pl.ds(2 * pair + half, 1), :] for half in range(2)]
    kts = {}
    outs = {}

    def scores(job):
        j, half = job
        low = j * TILE
        km = only_head(k_ref[0, low : low + TILE, :], half)
        vm = only_head(v_ref[0, low : low + TILE, :], half)
        return mm_nt(km, q_ref[0, low:, :]), mm_nt(vm, g_ref[0, low:, :])

    def rest(job, s, dp):
        j, half = job
        low = j * TILE
        k_pos = low + lax.broadcasted_iota(jnp.int32, (TILE, t - low), 0)
        high = low + TILE
        diag = (k_pos[:, :TILE] >= start_row[:, low:high]) & (k_pos[:, :TILE] <= pos_row[:, low:high])
        p = jnp.exp(jnp.where(diag, s[:, :TILE] - lses[half][:, low:high], neg_big))
        if high < t:
            far = k_pos[:, TILE:] >= start_row[:, high:]
            p = jnp.concatenate([p, jnp.exp(jnp.where(far, s[:, TILE:] - lses[half][:, high:], neg_big))], axis=1)
        ds = (p * (dp - deltas[half][:, low:])).astype(BF16)
        dv = mm(p.astype(BF16), g_ref[0, low:, :])
        dk = mm(ds, q_ref[0, low:, :])
        kt = jnp.transpose(k_ref[0, low : low + TILE, :])
        rows = slice(half * 64, half * 64 + 64)
        acc_ref[rows, low:] += mm(kt[rows], ds)
        if half == 0:
            outs[j] = (dk, dv)
        else:
            first_lanes = head_lanes(dk.shape, 0)
            dk_ref[0, low : low + TILE, :] = jnp.where(first_lanes, outs[j][0], dk).astype(BF16)
            dv_ref[0, low : low + TILE, :] = jnp.where(first_lanes, outs[j][1], dv).astype(BF16)

    ready = scores(jobs[0])
    for at, job in enumerate(jobs):
        now = ready
        if at + 1 < len(jobs):
            ready = scores(jobs[at + 1])
        rest(job, *now)
    dq_ref[0] = jnp.transpose((acc_ref[...] * scale_qk)).astype(BF16)


def backward_call(ends, q, k, v, gatt, lse, delta, first, count):
    pairs, t, _ = q.shape
    spec = pl.BlockSpec((1, t, LANES), lambda i: (i + first, 0, 0))
    out = pl.BlockSpec((1, t, LANES), lambda i: (i, 0, 0))
    return pl.pallas_call(
        functools.partial(backward_kernel, first),
        grid=(count,),
        in_specs=[SMEM_SPEC, spec, spec, spec, spec, whole((HEADS, t)), whole((HEADS, t))],
        out_specs=[out, out, out],
        out_shape=[jax.ShapeDtypeStruct((count, t, LANES), BF16)] * 3,
        scratch_shapes=[pltpu.VMEM((LANES, t), F32)],
        compiler_params=params(28),
        cost_estimate=cost(count * B_FLOPS, count * 1e5),
        name="backward",
    )(ends, *(pltpu.with_memory_space_constraint(a, pltpu.HBM) for a in (q, k, v, gatt)), lse, delta)


VEC_ROWS = 128


def last_kernel(*refs):
    core_ref = refs[0]
    pairs = (len(refs) - 11) // 3
    grads = refs[1 : 1 + 3 * pairs]
    n1_ref, x_ref, gmid_ref, gain_ref, w_ref, vecmid_ref = refs[1 + 3 * pairs : 7 + 3 * pairs]
    gin_ref, keep_ref, send_ref, gw_ref = refs[7 + 3 * pairs :]
    d = x_ref.shape[-1]
    half = keep_ref.shape[0]
    gqkv = jnp.concatenate([grads[3 * g + part][0] for part in range(3) for g in range(pairs)], axis=-1)
    gw = mm_tn(n1_ref[...], gqkv)
    blocks = 3 * pairs
    for p in range(blocks):
        at = (p // (blocks // 2)) * half + (p % (blocks // 2)) * d
        gw_ref[at : at + d] = gw[:, p * LANES : (p + 1) * LANES]
    e = mm_nt(gqkv, w_ref[...])
    n, scale = norm_parts(x_ref[...].astype(F32))
    gin_ref[...] = (gmid_ref[...] + norm_pull(e, n, scale, gain_ref[...])).astype(BF16)

    def col(values):
        return jnp.sum(values, axis=0, keepdims=True)

    rows = [vecmid_ref[r : r + 1] for r in range(6)]
    rows += [col(e * n), col(e), col(gqkv[:, :d].astype(F32)), col(gqkv[:, 2 * d :].astype(F32))]
    base = half - VEC_ROWS
    gw_ref[base:half] = jnp.zeros((VEC_ROWS, LANES), F32)
    gw_ref[half + base :] = jnp.zeros((VEC_ROWS, LANES), F32)
    for r, row in enumerate(rows):
        for g in range(d // LANES):
            at = base + r * (d // LANES) + g
            gw_ref[at : at + 1] = row[:, g * LANES : (g + 1) * LANES]
    split_halves(core_ref, gw_ref, keep_ref, send_ref)


def last_call(core, grads, n1, x, gmid, gain, w_qkv, vec_mid):
    t, d = x.shape
    half = 3 * d * d // LANES // 2 + VEC_ROWS
    return pl.pallas_call(
        last_kernel,
        grid=(1,),
        in_specs=[SMEM_SPEC]
        + [whole(a.shape) for a in grads]
        + [by_row(d, t), by_row(d, t), by_row(d, t), whole((1, d)), whole(w_qkv.shape), whole((8, d))],
        out_specs=[by_row(d, t), whole((half, LANES)), whole((half, LANES))],
        out_shape=[
            pltpu.HBM((t, d), BF16),
            jax.ShapeDtypeStruct((half, LANES), F32),
            jax.ShapeDtypeStruct((half, LANES), BF16),
        ],
        scratch_shapes=[pltpu.VMEM((2 * half, LANES), F32)],
        compiler_params=params(28),
        cost_estimate=cost(L_FLOPS, 1e5),
        name="last",
    )(core, *grads, n1, x, gmid, gain[None], w_qkv, vec_mid)


def ordered_halves(core_ref, own_ref, got_ref, write):
    pl.when(core_ref[0] == 0)(functools.partial(write, own_ref, got_ref))
    pl.when(core_ref[0] == 1)(functools.partial(write, got_ref, own_ref))


def finish_mid_kernel(core_ref, own_ref, got_ref, down_ref, up_ref, wo_ref):
    ff, d = down_ref.shape
    half = own_ref.shape[0]

    def write(low_ref, high_ref):
        def take(first, last):
            if last <= half:
                return low_ref[first:last].astype(F32)
            if first >= half:
                return high_ref[first - half : last - half].astype(F32)
            return jnp.concatenate([take(first, half), take(half, last)], axis=0)

        down_ref[...] = take(0, ff)
        up_ref[:, :d] = take(ff, ff + d)
        up_ref[:, d:] = take(ff + d, ff + 2 * d)
        wo_ref[...] = take(ff + 2 * d, ff + 3 * d)

    ordered_halves(core_ref, own_ref, got_ref, write)


def copy_kernel(in_ref, out_ref):
    out_ref[...] = in_ref[...].astype(out_ref.dtype)


def copy_call(order, values, dtype):
    parts, rows, d = values.shape
    spec = pl.BlockSpec((1, rows, d), lambda i: (i, 0, 0))
    return pl.pallas_call(
        lambda order_ref, in_ref, out_ref: copy_kernel(in_ref, out_ref),
        grid=(parts,),
        in_specs=[SMEM_SPEC, spec],
        out_specs=spec,
        out_shape=jax.ShapeDtypeStruct(values.shape, dtype),
        compiler_params=params(28),
        cost_estimate=cost(1e7, 1e5),
        name="copy",
    )(order, values)


def finish_last_kernel(core_ref, own_ref, got_ref, qkv_ref, *vec_refs):
    d = qkv_ref.shape[0]
    half = own_ref.shape[0]
    blocks = qkv_ref.shape[1] // LANES

    def write(low_ref, high_ref):
        for p in range(blocks):
            ref = (low_ref, high_ref)[p // (blocks // 2)]
            at = (p % (blocks // 2)) * d
            qkv_ref[:, p * LANES : (p + 1) * LANES] = ref[at : at + d].astype(F32)
        at = half - VEC_ROWS
        for ref in vec_refs:
            for g in range(ref.shape[1] // LANES):
                ref[:, g * LANES : (g + 1) * LANES] = low_ref[at : at + 1].astype(F32)
                at += 1

    ordered_halves(core_ref, own_ref, got_ref, write)


def finish_call(kernel, core, own, got, shapes, name):
    return pl.pallas_call(
        kernel,
        grid=(1,),
        in_specs=[SMEM_SPEC, whole(own.shape), whole(got.shape)],
        out_specs=[whole(shape) for shape in shapes],
        out_shape=[jax.ShapeDtypeStruct(shape, F32) for shape in shapes],
        compiler_params=params(28),
        cost_estimate=cost(1e8, 8e6),
        name=name,
    )(core, own, got)


def send_xor(values, flip):
    count = lax.axis_size(BOTH)
    return lax.ppermute(values, BOTH, [(i, i ^ flip) for i in range(count)])


def add_kernel(place_ref, *refs):
    outs = place_ref.shape[0]
    terms, results = refs[:-outs], refs[-outs:]
    size = results[0].shape[0]
    for flip, result in enumerate(results):
        rows = pl.ds(pl.multiple_of(jnp.bitwise_xor(place_ref[0], flip) * size, size), size)
        total = terms[0][rows, :].astype(F32)
        for term in terms[1:]:
            total = total + term[rows, :].astype(F32)
        result[...] = total.astype(result.dtype)


def add_call(place, parts, terms, own_dtype):
    rows, lanes = terms[0].shape
    shape = (rows // parts, lanes)
    places = jnp.broadcast_to(place, (parts,)).astype(jnp.int32)
    return pl.pallas_call(
        add_kernel,
        grid=(1,),
        in_specs=[SMEM_SPEC] + [whole(a.shape) for a in terms],
        out_specs=[whole(shape)] * parts,
        out_shape=[jax.ShapeDtypeStruct(shape, own_dtype if p == 0 else BF16) for p in range(parts)],
        compiler_params=params(28),
        cost_estimate=cost(1e8, 4e6),
        name="add",
    )(places, *terms)


def join_kernel(place_ref, *refs):
    out_ref = refs[-1]
    for flip, ref in enumerate(refs[:-1]):
        size = ref.shape[0]
        rows = pl.ds(pl.multiple_of(jnp.bitwise_xor(place_ref[0], flip) * size, size), size)
        out_ref[rows, :] = ref[...]


def join_call(place, pieces):
    rows, lanes = pieces[0].shape
    shape = (rows * len(pieces), lanes)
    return pl.pallas_call(
        join_kernel,
        grid=(1,),
        in_specs=[SMEM_SPEC] + [whole(p.shape) for p in pieces],
        out_specs=whole(shape),
        out_shape=jax.ShapeDtypeStruct(shape, pieces[0].dtype),
        compiler_params=params(28),
        cost_estimate=cost(1e8, 2e6),
        name="join",
    )(place[None].astype(jnp.int32), *pieces)


def swap_parts(parts, shift):
    return [send_xor(part, (flip + 1) << shift) for flip, part in enumerate(parts)]


def spread(part, shift, parts):
    return [send_xor(part, flip << shift) for flip in range(1, parts)]


def after(values, *others):
    return lax.optimization_barrier((values,) + others)[0]


def row_device(
    tokens, seg_lengths, ln1_gain, ln1_bias, w_qkv, b_qv, w_o, b_o, ln2_gain, ln2_bias,
    w_up, b_up, w_down, b_down, cotangent,
):
    row_count, slice_len, d = tokens.shape
    row = lax.axis_index("blk")
    me = lax.axis_index("rows") * lax.axis_size("blk") + row
    place_core = me & 1
    place_plane = (me >> 1) & 3
    place_deep = me >> 3
    core = place_core[None].astype(jnp.int32)
    blk = row[None].astype(jnp.int32)
    ends = jnp.cumsum(seg_lengths, axis=1)
    ends = lax.dynamic_index_in_dim(ends, row, 0, keepdims=False).astype(jnp.int32)

    def cut(values):
        return [lax.dynamic_index_in_dim(values, row ^ flip, 0, keepdims=False) for flip in range(row_count)]

    def swap(pieces):
        return [pieces[0]] + swap_parts(pieces[1:], 0)

    x = swap(cut(tokens))
    cot = cut(cotangent)
    cot = lax.optimization_barrier(tuple(cot) + tuple(x))[:row_count]
    cot = swap(list(cot))
    x, q, k, v, n1, att, lse = forward_call(ends, blk, x, ln1_gain, ln1_bias, w_qkv, b_qv)
    out, gmid, gatt, delta, keep, send, vec_mid = middle_call(
        core, blk, att, x, cot, w_o, b_o, ln2_gain, ln2_bias, w_up, b_up, w_down, b_down
    )

    def home(values):
        return lax.all_to_all(values.reshape(tokens.shape), "blk", 0, 0, tiled=True)

    def grads(pair, *deps):
        return backward_call(after(ends, *deps), q, k, v, gatt, lse, delta, pair, 1)

    g0 = grads(0)
    own, *parts = add_call(place_plane, 4, [keep, send_xor(send, 1)], F32)
    g1 = grads(1, own, g0[0])
    g2 = grads(2, g1[0])
    own, *parts = add_call(place_deep, 4, [own] + swap_parts(parts, 1), F32)
    g3 = grads(3, own, g2[0])
    output = home(after(out, own))
    (first,) = add_call(0, 1, [own] + swap_parts(parts, 3), BF16)
    gin, keep, send = last_call(
        after(core, first), (*g0, *g1, *g2, *g3), n1, x, gmid, ln1_gain, w_qkv, vec_mid
    )
    first = join_call(place_deep & 1, [first] + spread(first, 3, 2))
    send, first = lax.optimization_barrier((send, first))
    first_z = spread(first, 4, 2)
    own, *parts = add_call(place_plane, 4, [keep, send_xor(send, 1)], F32)
    first = join_call(after(place_deep >> 1, own), [first] + first_z)
    second = swap_parts(parts, 1)
    own, *parts = add_call(place_deep, 4, [own] + second, F32)
    first, gin, output = lax.optimization_barrier((first, gin, output, own))[:3]
    gin = home(gin)
    (second,) = add_call(0, 1, [own] + swap_parts(parts, 3), BF16)
    first = join_call(after(place_plane & 1, second), [first] + spread(first, 1, 2))
    second = join_call(after(place_deep, gin), [second] + spread(second, 3, 4))
    first = join_call(after(place_plane >> 1, second), [first] + spread(first, 2, 2))
    order, output, gin = lax.optimization_barrier((core, output, gin, second))[:3]
    output = copy_call(order, output, BF16)
    input_grad = copy_call(order, gin, F32)
    second = join_call(after(place_plane, output, input_grad), [second] + spread(second, 1, 4))
    gw_down, gw_up, gw_o = finish_call(
        finish_mid_kernel, core, first, send_xor(first, 1), [w_down.shape, w_up.shape, w_o.shape], "finish_mid"
    )
    gw_qkv, *vecs = finish_call(
        finish_last_kernel, after(core, gw_down), second, send_xor(second, 1),
        [w_qkv.shape] + [(1, size) for size in (d, 2 * d, d, d, d, d, d, 2 * d)], "finish_last",
    )
    vecs = [vec.reshape(-1) for vec in vecs]
    g_down_b, g_up_b, g_ln2_gain, g_ln2_bias, g_o_b, g_ln1_gain, g_ln1_bias, g_qv_b = vecs
    return (
        output, input_grad, g_ln1_gain, g_ln1_bias, gw_qkv, g_qv_b, gw_o, g_o_b, g_ln2_gain, g_ln2_bias,
        gw_up, g_up_b, gw_down, g_down_b,
    )


def layer_norm(values, gain_vec, bias_vec):
    average = jnp.mean(values, axis=-1, keepdims=True)
    centered = values - average
    variance = jnp.mean(centered * centered, axis=-1, keepdims=True)
    return centered * lax.rsqrt(variance + norm_eps) * gain_vec + bias_vec


def segment_of(cell_ends, positions):
    return jnp.sum((cell_ends[:, None, :] <= positions[None, :, None]).astype(jnp.int32), axis=-1)


def block_scores(query_heads, key_heads, query_pos, key_pos, query_seg, key_seg, scale_qk):
    raw_scores = (
        jnp.einsum("rqhd,rkhd->rqhk", query_heads, key_heads, preferred_element_type=jnp.float32)
        * scale_qk
    )
    causal = key_pos[None, :] <= query_pos[:, None]
    same_cell = query_seg[:, :, None] == key_seg[:, None, :]
    allowed = (causal[None] & same_cell)[:, :, None, :]
    return (jnp.where(allowed, raw_scores, neg_big), allowed)


def block_active(query_pos, key_pos, query_seg, key_seg):
    return (key_pos[0] <= query_pos[-1]) & jnp.any(key_seg[:, -1] >= query_seg[:, 0])


def backward_block(
    query_heads,
    grad_heads,
    log_total,
    delta_sum,
    key_heads,
    value_heads,
    query_pos,
    key_pos,
    query_seg,
    key_seg,
    scale_qk,
):
    scores, allowed = block_scores(
        query_heads, key_heads, query_pos, key_pos, query_seg, key_seg, scale_qk
    )
    softmaxed = jnp.where(allowed, jnp.exp(scores - log_total[..., None]), 0.0)
    grad_probs = jnp.einsum(
        "rqhd,rkhd->rqhk", grad_heads, value_heads, preferred_element_type=jnp.float32
    )
    grad_scores = (softmaxed * (grad_probs - delta_sum[..., None])).astype(jnp.bfloat16)
    grad_query = (
        jnp.einsum("rqhk,rkhd->rqhd", grad_scores, key_heads, preferred_element_type=jnp.float32)
        * scale_qk
    )
    grad_key = (
        jnp.einsum("rqhk,rqhd->rkhd", grad_scores, query_heads, preferred_element_type=jnp.float32)
        * scale_qk
    )
    grad_value = jnp.einsum(
        "rqhk,rqhd->rkhd",
        softmaxed.astype(jnp.bfloat16),
        grad_heads,
        preferred_element_type=jnp.float32,
    )
    return (grad_query, grad_key, grad_value)


def unchanged(old_state):
    return old_state


def general_device(
    tokens,
    seg_lengths,
    ln1_gain,
    ln1_bias,
    w_qkv,
    b_qv,
    w_o,
    b_o,
    ln2_gain,
    ln2_bias,
    w_up,
    b_up,
    w_down,
    b_down,
    cotangent,
):
    row_count, slice_len, width_all = tokens.shape
    head_size = width_all // HEADS
    scale_qk = head_size ** (-0.5)
    head_shape = (row_count, slice_len, HEADS, head_size)
    stat_shape = (row_count, slice_len, HEADS)
    full_length = lax.axis_size("blk") * slice_len
    offsets = jnp.arange(slice_len, dtype=jnp.int32)
    query_pos = lax.axis_index("blk") * slice_len + offsets
    cell_ends = jnp.cumsum(seg_lengths, axis=1)
    query_seg = segment_of(cell_ends, query_pos)

    def take_block(piece, block_index):
        return lax.dynamic_slice_in_dim(piece, block_index * slice_len, slice_len, 1).reshape(
            head_shape
        )

    inputs = tokens.astype(jnp.float32)
    normed_val, first_pull = jax.vjp(layer_norm, inputs, ln1_gain, ln1_bias)
    normed_one = normed_val.astype(jnp.bfloat16)
    projected = jnp.dot(normed_one, w_qkv, preferred_element_type=jnp.float32)
    query_b = (projected[..., :width_all] + b_qv[:width_all]).astype(jnp.bfloat16)
    key_b = projected[..., width_all : 2 * width_all].astype(jnp.bfloat16)
    value_b = (projected[..., 2 * width_all :] + b_qv[width_all:]).astype(jnp.bfloat16)
    query_heads = query_b.reshape(head_shape)
    start_state = (
        jnp.full(stat_shape, neg_big, jnp.float32),
        jnp.zeros(stat_shape, jnp.float32),
        jnp.zeros(head_shape, jnp.float32),
    )
    key_piece = lax.all_gather(key_b, "blk", axis=1, tiled=True)
    value_piece = lax.all_gather(value_b, "blk", axis=1, tiled=True)

    def forward_block_step(block_index, inner_state):
        key_pos = block_index * slice_len + offsets
        key_seg = segment_of(cell_ends, key_pos)
        key_heads = take_block(key_piece, block_index)
        value_heads = take_block(value_piece, block_index)

        def forward_update(old_state):
            running_top, running_total, running_sum = old_state
            scores, allowed = block_scores(
                query_heads, key_heads, query_pos, key_pos, query_seg, key_seg, scale_qk
            )
            new_top = jnp.maximum(running_top, jnp.max(scores, axis=-1))
            factor = jnp.exp(running_top - new_top)
            weights_now = jnp.where(allowed, jnp.exp(scores - new_top[..., None]), 0.0)
            new_total = running_total * factor + jnp.sum(weights_now, axis=-1)
            new_sum = running_sum * factor[..., None] + jnp.einsum(
                "rqhk,rkhd->rqhd",
                weights_now.astype(jnp.bfloat16),
                value_heads,
                preferred_element_type=jnp.float32,
            )
            return (new_top, new_total, new_sum)

        return lax.cond(
            block_active(query_pos, key_pos, query_seg, key_seg),
            forward_update,
            unchanged,
            inner_state,
        )

    running_top, running_total, running_sum = lax.fori_loop(
        0, key_piece.shape[1] // slice_len, forward_block_step, start_state
    )
    attn_f32 = (running_sum / running_total[..., None]).reshape(row_count, slice_len, width_all)
    log_total = running_top + jnp.log(running_total)
    attn_b = attn_f32.astype(jnp.bfloat16)
    middle = inputs + jnp.dot(attn_b, w_o, preferred_element_type=jnp.float32) + b_o
    normed_two_val, second_pull = jax.vjp(layer_norm, middle, ln2_gain, ln2_bias)
    normed_two = normed_two_val.astype(jnp.bfloat16)
    hidden_pre = jnp.dot(normed_two, w_up, preferred_element_type=jnp.float32) + b_up
    hidden_val, gelu_pull = jax.vjp(jax.nn.gelu, hidden_pre)
    hidden_b = hidden_val.astype(jnp.bfloat16)
    output = (
        middle + jnp.dot(hidden_b, w_down, preferred_element_type=jnp.float32) + b_down
    ).astype(jnp.bfloat16)
    grad_out = cotangent.astype(jnp.float32)
    grad_w_down = jnp.einsum("rcf,rcd->fd", hidden_b, cotangent, preferred_element_type=jnp.float32)
    grad_b_down = jnp.sum(grad_out, axis=(0, 1))
    grad_hidden = jnp.einsum("rcd,fd->rcf", cotangent, w_down, preferred_element_type=jnp.float32)
    (grad_pre,) = gelu_pull(grad_hidden)
    grad_pre_b = grad_pre.astype(jnp.bfloat16)
    grad_w_up = jnp.einsum(
        "rcd,rcf->df", normed_two, grad_pre_b, preferred_element_type=jnp.float32
    )
    grad_b_up = jnp.sum(grad_pre_b.astype(jnp.float32), axis=(0, 1))
    grad_normed_two = jnp.einsum(
        "rcf,df->rcd", grad_pre_b, w_up, preferred_element_type=jnp.float32
    )
    grad_mid_norm, grad_ln2_gain, grad_ln2_bias = second_pull(grad_normed_two)
    grad_middle = grad_out + grad_mid_norm
    grad_branch_b = grad_middle.astype(jnp.bfloat16)
    grad_w_o = jnp.einsum("rce,rcd->ed", attn_b, grad_branch_b, preferred_element_type=jnp.float32)
    grad_b_o = jnp.sum(grad_branch_b.astype(jnp.float32), axis=(0, 1))
    grad_attn_b = jnp.einsum(
        "rcd,ed->rce", grad_branch_b, w_o, preferred_element_type=jnp.float32
    ).astype(jnp.bfloat16)
    delta_sum = jnp.sum((grad_attn_b.astype(jnp.float32) * attn_f32).reshape(head_shape), axis=-1)
    grad_heads = grad_attn_b.reshape(head_shape)
    whole_shape = (row_count, full_length, HEADS, head_size)
    back_state = (
        jnp.zeros(head_shape, jnp.float32),
        jnp.zeros(whole_shape, jnp.float32),
        jnp.zeros(whole_shape, jnp.float32),
    )
    backward_key_piece = lax.all_gather(key_b, "blk", axis=1, tiled=True)
    backward_value_piece = lax.all_gather(value_b, "blk", axis=1, tiled=True)

    def backward_block_step(block_index, inner_state):
        key_pos = block_index * slice_len + offsets
        key_seg = segment_of(cell_ends, key_pos)
        key_heads = take_block(backward_key_piece, block_index)
        value_heads = take_block(backward_value_piece, block_index)

        def backward_update(old_state):
            grad_query, grad_key, grad_value = backward_block(
                query_heads,
                grad_heads,
                log_total,
                delta_sum,
                key_heads,
                value_heads,
                query_pos,
                key_pos,
                query_seg,
                key_seg,
                scale_qk,
            )
            at_row = block_index * slice_len
            return (
                old_state[0] + grad_query,
                lax.dynamic_update_slice_in_dim(old_state[1], grad_key, at_row, 1),
                lax.dynamic_update_slice_in_dim(old_state[2], grad_value, at_row, 1),
            )

        return lax.cond(
            block_active(query_pos, key_pos, query_seg, key_seg),
            backward_update,
            unchanged,
            inner_state,
        )

    back_result = lax.fori_loop(
        0, backward_key_piece.shape[1] // slice_len, backward_block_step, back_state
    )
    grad_query_sum = back_result[0]
    grad_key_sum, grad_value_sum = (
        lax.psum_scatter(
            back_result[1].astype(jnp.bfloat16), "blk", scatter_dimension=1, tiled=True
        ).astype(jnp.float32),
        lax.psum_scatter(
            back_result[2].astype(jnp.bfloat16), "blk", scatter_dimension=1, tiled=True
        ).astype(jnp.float32),
    )
    flat_shape = (row_count, slice_len, width_all)
    grad_qkv_b = jnp.concatenate(
        [
            grad_query_sum.reshape(flat_shape),
            grad_key_sum.reshape(flat_shape),
            grad_value_sum.reshape(flat_shape),
        ],
        axis=-1,
    ).astype(jnp.bfloat16)
    grad_w_qkv = jnp.einsum(
        "rcd,rce->de", normed_one, grad_qkv_b, preferred_element_type=jnp.float32
    )
    column_sums = jnp.sum(grad_qkv_b.astype(jnp.float32), axis=(0, 1))
    grad_b_qv = jnp.concatenate([column_sums[:width_all], column_sums[2 * width_all :]])
    grad_normed_one = jnp.einsum(
        "rce,de->rcd", grad_qkv_b, w_qkv, preferred_element_type=jnp.float32
    )
    grad_in_norm, grad_ln1_gain, grad_ln1_bias = first_pull(grad_normed_one)
    input_grad = grad_middle + grad_in_norm
    grads = (
        grad_ln1_gain,
        grad_ln1_bias,
        grad_w_qkv,
        grad_b_qv,
        grad_w_o,
        grad_b_o,
        grad_ln2_gain,
        grad_ln2_bias,
        grad_w_up,
        grad_b_up,
        grad_w_down,
        grad_b_down,
    )
    summed = lax.psum(
        (
            grads[0],
            grads[1],
            grads[2],
            grads[3],
            grads[4],
            grads[5],
            grads[6],
            grads[7],
            grads[8],
            grads[9],
            grads[10],
            grads[11],
        ),
        ("rows", "blk"),
    )
    return (
        output,
        input_grad,
        summed[0],
        summed[1],
        summed[2],
        summed[3],
        summed[4],
        summed[5],
        summed[6],
        summed[7],
        summed[8],
        summed[9],
        summed[10],
        summed[11],
    )


def device_function(tokens, *rest):
    d = tokens.shape[2]
    whole_rows = (
        lax.axis_size("blk") == tokens.shape[0] == 4
        and lax.axis_size("rows") == 8
        and tokens.shape[1] == TILE
        and d == 512
    )
    return (row_device if whole_rows else general_device)(tokens, *rest)


def solution(mesh):
    in_specs = (
        P("rows", "blk", None),
        P("rows", None),
        P(),
        P(),
        P(),
        P(),
        P(),
        P(),
        P(),
        P(),
        P(),
        P(),
        P(),
        P(),
        P("rows", "blk", None),
    )
    out_specs = (
        P("rows", "blk", None),
        P("rows", "blk", None),
        P(),
        P(),
        P(),
        P(),
        P(),
        P(),
        P(),
        P(),
        P(),
        P(),
        P(),
        P(),
    )
    return jax.shard_map(
        device_function, mesh=mesh, in_specs=in_specs, out_specs=out_specs, check_vma=False
    )
```

```python
import functools

import jax
import jax.numpy as jnp
from jax import lax
from jax.experimental import pallas as pl
from jax.experimental.pallas import tpu as pltpu
from jax.sharding import PartitionSpec as P

HEADS = 8
norm_eps = 1e-05
neg_big = -1e30
BOTH = ("rows", "blk")
F32 = jnp.float32
BF16 = jnp.bfloat16
TILE = 256
LANES = 128
MIB = 1024 * 1024
B_FLOPS = 1e9
L_FLOPS = 1e9
MID_TILE = 512
MID_MIB = 28
LAST_MIB = 26


def mm(lhs, rhs):
    return lax.dot_general(lhs, rhs, (((1,), (0,)), ((), ())), preferred_element_type=F32)


def mm_nt(lhs, rhs):
    return lax.dot_general(lhs, rhs, (((1,), (1,)), ((), ())), preferred_element_type=F32)


def mm_tn(lhs, rhs):
    return lax.dot_general(lhs, rhs, (((0,), (0,)), ((), ())), preferred_element_type=F32)


def cell_start(ends_ref, positions):
    start = jnp.zeros_like(positions)
    for c in range(ends_ref.shape[0]):
        start = jnp.where(ends_ref[c] <= positions, ends_ref[c], start)
    return start


def norm_parts(values):
    average = jnp.mean(values, axis=-1, keepdims=True)
    centered = values - average
    variance = jnp.mean(centered * centered, axis=-1, keepdims=True)
    scale = lax.rsqrt(variance + norm_eps)
    return centered * scale, scale


def norm_pull(e, n, scale, gain):
    f = e * gain
    return (
        f
        - jnp.mean(f, axis=-1, keepdims=True)
        - n * jnp.mean(f * n, axis=-1, keepdims=True)
    ) * scale


def head_lanes(shape, half):
    lane = lax.broadcasted_iota(jnp.int32, shape, len(shape) - 1)
    return (lane < LANES // 2) if half == 0 else (lane >= LANES // 2)


def only_head(values, half):
    return jnp.where(head_lanes(values.shape, half), values, jnp.zeros_like(values))


def in_order(blk_ref, pieces, whole_ref):
    size = pieces[0].shape[0]
    for flip, piece_ref in enumerate(pieces):
        at = jnp.bitwise_xor(blk_ref[0], flip) * size
        whole_ref[pl.ds(pl.multiple_of(at, size), size), :] = piece_ref[...]


def forward_kernel(
    ends_ref, blk_ref, x0_ref, x1_ref, x2_ref, x3_ref, gain_ref, bias_ref, w_ref, b_ref,
    x_ref, q_ref, k_ref, v_ref, n1_ref, att_ref, lse_ref,
    mask_ref,
):
    in_order(blk_ref, (x0_ref, x1_ref, x2_ref, x3_ref), x_ref)
    t, width = x_ref.shape
    pairs = width // LANES
    scale_qk = (width // HEADS) ** (-0.5)
    for low in range(0, t, 512):
        rows = slice(low, low + 512)
        n, _ = norm_parts(x_ref[rows].astype(F32))
        n1 = (n * gain_ref[...] + bias_ref[...]).astype(BF16)
        n1_ref[rows] = n1
        q = mm(n1, w_ref[:, :width]) + b_ref[:, :width]
        q = (q.astype(BF16).astype(F32) * scale_qk).astype(BF16)
        k = mm(n1, w_ref[:, width : 2 * width]).astype(BF16)
        v = (mm(n1, w_ref[:, 2 * width :]) + b_ref[:, width:]).astype(BF16)
        for g in range(pairs):
            cols = slice(g * LANES, (g + 1) * LANES)
            q_ref[g, rows, :] = q[:, cols]
            k_ref[g, rows, :] = k[:, cols]
            v_ref[g, rows, :] = v[:, cols]
    for low in range(0, t, TILE):
        reach = low + TILE
        rows = slice(low, reach)
        q_pos = low + lax.broadcasted_iota(jnp.int32, (TILE, 1), 0)
        k_pos = lax.broadcasted_iota(jnp.int32, (TILE, reach), 1)
        start = cell_start(ends_ref, q_pos)
        mask_ref[:, :reach] = jnp.where((k_pos <= q_pos) & (k_pos >= start), 0.0, neg_big)
        lse_all = jnp.zeros((TILE, LANES), F32)
        lane = lax.broadcasted_iota(jnp.int32, lse_all.shape, 1)
        for g in range(pairs):
            qp = q_ref[g, rows, :]
            kp = k_ref[g, :reach, :]
            vp = v_ref[g, :reach, :]
            outs = []
            for half in range(2):
                s = mm_nt(only_head(qp, half), kp) + mask_ref[:, :reach]
                top = jnp.max(s, axis=-1, keepdims=True)
                p = jnp.exp(s - top)
                total = jnp.sum(p, axis=-1, keepdims=True)
                outs.append(mm(p.astype(BF16), vp) / total)
                lse_all = jnp.where(lane == 2 * g + half, top + jnp.log(total), lse_all)
            att_ref[g, rows, :] = jnp.where(head_lanes(outs[0].shape, 0), outs[0], outs[1])
        lse_ref[:, rows] = jnp.transpose(lse_all)[:HEADS]


def whole(shape):
    return pl.BlockSpec(shape, lambda i: (0,) * len(shape))


def by_row(cols, tile=TILE):
    return pl.BlockSpec((tile, cols), lambda i: (i, 0))


def by_pair(pairs, tile=TILE):
    return pl.BlockSpec((pairs, tile, LANES), lambda i: (0, i, 0))


def heads_row(tile=TILE):
    return pl.BlockSpec((HEADS, tile), lambda i: (0, i))


SMEM_SPEC = pl.BlockSpec(memory_space=pltpu.SMEM)


def in_hbm(*arrays):
    return [pltpu.with_memory_space_constraint(a, pltpu.HBM) for a in arrays]


def params(mib):
    return pltpu.CompilerParams(dimension_semantics=("arbitrary",), vmem_limit_bytes=mib * MIB)


def cost(flops, moved):
    return pl.CostEstimate(flops=int(flops), bytes_accessed=int(moved), transcendentals=0)


def forward_call(ends, blk, pieces, gain, bias, w_qkv, b_qv):
    size, d = pieces[0].shape
    t = size * len(pieces)
    pairs = d // LANES
    return pl.pallas_call(
        forward_kernel,
        grid=(1,),
        in_specs=[SMEM_SPEC, SMEM_SPEC]
        + [whole((size, d))] * len(pieces)
        + [whole((1, d)), whole((1, d)), whole(w_qkv.shape), whole((1, 2 * d))],
        out_specs=[
            whole((t, d)), whole((pairs, t, LANES)), whole((pairs, t, LANES)), whole((pairs, t, LANES)), whole((t, d)),
            whole((pairs, t, LANES)), whole((HEADS, t)),
        ],
        out_shape=[
            jax.ShapeDtypeStruct((t, d), BF16),
            pltpu.HBM((pairs, t, LANES), BF16),
            pltpu.HBM((pairs, t, LANES), BF16),
            pltpu.HBM((pairs, t, LANES), BF16),
            pltpu.HBM((t, d), BF16),
            jax.ShapeDtypeStruct((pairs, t, LANES), F32),
            jax.ShapeDtypeStruct((HEADS, t), F32),
        ],
        scratch_shapes=[pltpu.VMEM((TILE, t), F32)],
        compiler_params=params(34),
        cost_estimate=cost(20e9, 10e6),
        name="forward",
    )(ends, blk, *pieces, gain[None], bias[None], w_qkv, b_qv[None])


def split_halves(core_ref, whole_ref, keep_ref, send_ref):
    half = keep_ref.shape[0]
    core = core_ref[0]
    keep_ref[...] = whole_ref[pl.ds(pl.multiple_of(core * half, half), half), :]
    send_ref[...] = whole_ref[pl.ds(pl.multiple_of((1 - core) * half, half), half), :].astype(BF16)


def middle_kernel(
    core_ref, blk_ref, att_ref, x_ref, c0_ref, c1_ref, c2_ref, c3_ref, wo_ref, bo_ref, gain_ref, bias_ref, wup_ref, bup_ref, wdown_ref, bdown_ref,
    out_ref, gmid_ref, gatt_ref, delta_ref, keep_ref, send_ref, vec_ref,
    cot_ref, gw_ref, hidden_ref, gpre_ref, n2_ref, attb_ref, gbr_ref,
):
    pairs = att_ref.shape[0]
    t, d = x_ref.shape
    ff = wup_ref.shape[-1]
    c0 = 0.7978845608028654
    c1 = 0.044715

    def col(values):
        return jnp.sum(values, axis=0, keepdims=True)

    in_order(blk_ref, (c0_ref, c1_ref, c2_ref, c3_ref), cot_ref)
    vec_ref[...] = jnp.zeros_like(vec_ref)
    head = lax.broadcasted_iota(jnp.int32, (HEADS, d), 0)
    lane = lax.broadcasted_iota(jnp.int32, (HEADS, d), 1)
    ones = jnp.where(lane // (d // HEADS) == head, 1.0, 0.0).astype(BF16)
    def tile(step, carry):
        rows = pl.ds(pl.multiple_of(step * MID_TILE, MID_TILE), MID_TILE)
        att = jnp.concatenate([att_ref[g, rows, :] for g in range(pairs)], axis=-1)
        att_b = att.astype(BF16)
        attb_ref[rows, :] = att_b
        middle = x_ref[rows, :].astype(F32) + mm(att_b, wo_ref[...]) + bo_ref[...]
        n, scale = norm_parts(middle)
        n2 = (n * gain_ref[...] + bias_ref[...]).astype(BF16)
        n2_ref[rows, :] = n2
        pre = mm(n2, wup_ref[...]) + bup_ref[...]
        sq = pre * pre
        th = jnp.tanh(c0 * (pre + c1 * (sq * pre)))
        half_one = 0.5 * (1.0 + th)
        hidden = (pre * half_one).astype(BF16)
        hidden_ref[rows, :] = hidden
        slope = half_one + (0.5 * pre) * (1.0 - th * th) * (c0 + (3.0 * c0 * c1) * sq)
        out_ref[rows, :] = (middle + mm(hidden, wdown_ref[...]) + bdown_ref[...]).astype(BF16)
        cot = cot_ref[rows, :]
        cot_f = cot.astype(F32)
        gpre = (mm_nt(cot, wdown_ref[...]) * slope).astype(BF16)
        gpre_ref[rows, :] = gpre
        e = mm_nt(gpre, wup_ref[...])
        gmid = cot_f + norm_pull(e, n, scale, gain_ref[...])
        gmid_ref[rows, :] = gmid
        gbr = gmid.astype(BF16)
        gbr_ref[rows, :] = gbr
        gatt = mm_nt(gbr, wo_ref[...]).astype(BF16)
        for g in range(pairs):
            gatt_ref[g, rows, :] = gatt[:, g * LANES : (g + 1) * LANES]
        prod = gatt.astype(F32) * att
        hi = prod.astype(BF16)
        lo = (prod - hi.astype(F32)).astype(BF16)
        delta_ref[:, rows] = mm_nt(ones, hi) + mm_nt(ones, lo)
        gsum = col(gpre.astype(F32))
        vec_ref[0:1] += col(cot_f)
        vec_ref[1:2] += gsum[:, :d]
        vec_ref[2:3] += gsum[:, d:]
        vec_ref[3:4] += col(e * n)
        vec_ref[4:5] += col(e)
        vec_ref[5:6] += col(gbr.astype(F32))
        return carry

    lax.fori_loop(0, t // MID_TILE, tile, 0)
    gw_ref[:ff] = mm_tn(hidden_ref[...], cot_ref[...])
    gw_ref[ff : ff + d] = mm_tn(n2_ref[...], gpre_ref[:, :d])
    gw_ref[ff + d : ff + 2 * d] = mm_tn(n2_ref[...], gpre_ref[:, d:])
    gw_ref[ff + 2 * d :] = mm_tn(attb_ref[...], gbr_ref[...])
    split_halves(core_ref, gw_ref, keep_ref, send_ref)


def middle_call(core, blk, att, x, cots, w_o, b_o, gain, bias, w_up, b_up, w_down, b_down):
    t, d = x.shape
    pairs = d // LANES
    ff = w_up.shape[1]
    half = (ff + 3 * d) // 2
    return pl.pallas_call(
        middle_kernel,
        grid=(1,),
        in_specs=[
            SMEM_SPEC, SMEM_SPEC,
            by_pair(pairs, t), by_row(d, t), *[whole(c.shape) for c in cots], whole((d, d)), whole((1, d)), whole((1, d)), whole((1, d)),
            whole((d, ff)), whole((1, ff)), whole((ff, d)), whole((1, d)),
        ],
        out_specs=[
            by_row(d, t), by_row(d, t), by_pair(pairs, t), heads_row(t), whole((half, d)), whole((half, d)),
            whole((8, d)),
        ],
        out_shape=[
            pltpu.HBM((t, d), BF16),
            pltpu.HBM((t, d), F32),
            pltpu.HBM((pairs, t, LANES), BF16),
            jax.ShapeDtypeStruct((HEADS, t), F32),
            jax.ShapeDtypeStruct((half, d), F32),
            jax.ShapeDtypeStruct((half, d), BF16),
            jax.ShapeDtypeStruct((8, d), F32),
        ],
        scratch_shapes=[
            pltpu.VMEM((t, d), BF16),
            pltpu.VMEM((2 * half, d), F32),
            pltpu.VMEM((t, ff), BF16),
            pltpu.VMEM((t, ff), BF16),
            pltpu.VMEM((t, d), BF16),
            pltpu.VMEM((t, d), BF16),
            pltpu.VMEM((t, d), BF16),
        ],
        compiler_params=params(28),
        cost_estimate=cost(15e9, 20e6),
        name="middle",
    )(core, blk, att, x, *cots, w_o, b_o[None], gain[None], bias[None], w_up, b_up[None], w_down, b_down[None])


def backward_kernel(first, ends_ref, q_ref, k_ref, v_ref, g_ref, lse_ref, delta_ref, dq_ref, dk_ref, dv_ref, acc_ref):
    pair = pl.program_id(0) + first
    t = q_ref.shape[1]
    scale_qk = (LANES // 2) ** (-0.5)
    pos_row = lax.broadcasted_iota(jnp.int32, (1, t), 1)
    start_row = cell_start(ends_ref, pos_row)
    acc_ref[...] = jnp.zeros_like(acc_ref)
    jobs = [(j, half) for j in range(t // TILE) for half in range(2)]
    lses = [lse_ref[pl.ds(2 * pair + half, 1), :] for half in range(2)]
    deltas = [delta_ref[pl.ds(2 * pair + half, 1), :] for half in range(2)]
    kts = {}
    outs = {}

    def scores(job):
        j, half = job
        low = j * TILE
        km = only_head(k_ref[0, low : low + TILE, :], half)
        vm = only_head(v_ref[0, low : low + TILE, :], half)
        return mm_nt(km, q_ref[0, low:, :]), mm_nt(vm, g_ref[0, low:, :])

    def rest(job, s, dp):
        j, half = job
        low = j * TILE
        k_pos = low + lax.broadcasted_iota(jnp.int32, (TILE, t - low), 0)
        high = low + TILE
        diag = (k_pos[:, :TILE] >= start_row[:, low:high]) & (k_pos[:, :TILE] <= pos_row[:, low:high])
        p = jnp.exp(jnp.where(diag, s[:, :TILE] - lses[half][:, low:high], neg_big))
        if high < t:
            far = k_pos[:, TILE:] >= start_row[:, high:]
            p = jnp.concatenate([p, jnp.exp(jnp.where(far, s[:, TILE:] - lses[half][:, high:], neg_big))], axis=1)
        ds = (p * (dp - deltas[half][:, low:])).astype(BF16)
        dv = mm(p.astype(BF16), g_ref[0, low:, :])
        dk = mm(ds, q_ref[0, low:, :])
        kt = jnp.transpose(k_ref[0, low : low + TILE, :])
        rows = slice(half * 64, half * 64 + 64)
        acc_ref[rows, low:] += mm(kt[rows], ds)
        if half == 0:
            outs[j] = (dk, dv)
        else:
            first_lanes = head_lanes(dk.shape, 0)
            dk_ref[0, low : low + TILE, :] = jnp.where(first_lanes, outs[j][0], dk).astype(BF16)
            dv_ref[0, low : low + TILE, :] = jnp.where(first_lanes, outs[j][1], dv).astype(BF16)

    ready = scores(jobs[0])
    for at, job in enumerate(jobs):
        now = ready
        if at + 1 < len(jobs):
            ready = scores(jobs[at + 1])
        rest(job, *now)
    dq_ref[0] = jnp.transpose((acc_ref[...] * scale_qk)).astype(BF16)


def backward_call(ends, q, k, v, gatt, lse, delta, first, count):
    pairs, t, _ = q.shape
    spec = pl.BlockSpec((1, t, LANES), lambda i: (i + first, 0, 0))
    out = pl.BlockSpec((1, t, LANES), lambda i: (i, 0, 0))
    return pl.pallas_call(
        functools.partial(backward_kernel, first),
        grid=(count,),
        in_specs=[SMEM_SPEC, spec, spec, spec, spec, whole((HEADS, t)), whole((HEADS, t))],
        out_specs=[out, out, out],
        out_shape=[pltpu.HBM((count, t, LANES), BF16)] * 3,
        scratch_shapes=[pltpu.VMEM((LANES, t), F32)],
        compiler_params=params(28),
        cost_estimate=cost(count * B_FLOPS, count * 1e5),
        name="backward",
    )(ends, *in_hbm(q, k, v, gatt), lse, delta)


VEC_ROWS = 128


def last_kernel(*refs):
    core_ref = refs[0]
    grads = refs[1:4]
    n1_ref, x_ref, gmid_ref, gain_ref, w_ref, vecmid_ref, gin_ref, keep_ref, send_ref, gw_ref = refs[4:]
    pairs = grads[0].shape[0]
    d = x_ref.shape[-1]
    half = keep_ref.shape[0]
    gqkv = jnp.concatenate([grads[part][g] for part in range(3) for g in range(pairs)], axis=-1)
    gw = mm_tn(n1_ref[...], gqkv)
    blocks = 3 * pairs
    for p in range(blocks):
        at = (p // (blocks // 2)) * half + (p % (blocks // 2)) * d
        gw_ref[at : at + d] = gw[:, p * LANES : (p + 1) * LANES]
    e = mm_nt(gqkv, w_ref[...])
    n, scale = norm_parts(x_ref[...].astype(F32))
    gin_ref[...] = (gmid_ref[...] + norm_pull(e, n, scale, gain_ref[...])).astype(BF16)

    def col(values):
        return jnp.sum(values, axis=0, keepdims=True)

    rows = [vecmid_ref[r : r + 1] for r in range(6)]
    rows += [col(e * n), col(e), col(gqkv[:, :d].astype(F32)), col(gqkv[:, 2 * d :].astype(F32))]
    base = half - VEC_ROWS
    gw_ref[base:half] = jnp.zeros((VEC_ROWS, LANES), F32)
    gw_ref[half + base :] = jnp.zeros((VEC_ROWS, LANES), F32)
    for r, row in enumerate(rows):
        for g in range(d // LANES):
            at = base + r * (d // LANES) + g
            gw_ref[at : at + 1] = row[:, g * LANES : (g + 1) * LANES]
    split_halves(core_ref, gw_ref, keep_ref, send_ref)


def last_call(core, grads, n1, x, gmid, gain, w_qkv, vec_mid):
    t, d = x.shape
    half = 3 * d * d // LANES // 2 + VEC_ROWS
    return pl.pallas_call(
        last_kernel,
        grid=(1,),
        in_specs=[SMEM_SPEC]
        + [whole(a.shape) for a in grads]
        + [by_row(d, t), by_row(d, t), by_row(d, t), whole((1, d)), whole(w_qkv.shape), whole((8, d))],
        out_specs=[by_row(d, t), whole((half, LANES)), whole((half, LANES))],
        out_shape=[
            pltpu.HBM((t, d), BF16),
            jax.ShapeDtypeStruct((half, LANES), F32),
            jax.ShapeDtypeStruct((half, LANES), BF16),
        ],
        scratch_shapes=[pltpu.VMEM((2 * half, LANES), F32)],
        compiler_params=params(28),
        cost_estimate=cost(L_FLOPS, 1e5),
        name="last",
    )(core, *in_hbm(*grads), n1, x, gmid, gain[None], w_qkv, vec_mid)


def ordered_halves(core_ref, own_ref, got_ref, write):
    pl.when(core_ref[0] == 0)(functools.partial(write, own_ref, got_ref))
    pl.when(core_ref[0] == 1)(functools.partial(write, got_ref, own_ref))


def finish_mid_kernel(core_ref, own_ref, got_ref, down_ref, up_ref, wo_ref):
    ff, d = down_ref.shape
    half = own_ref.shape[0]

    def write(low_ref, high_ref):
        def take(first, last):
            if last <= half:
                return low_ref[first:last].astype(F32)
            if first >= half:
                return high_ref[first - half : last - half].astype(F32)
            return jnp.concatenate([take(first, half), take(half, last)], axis=0)

        down_ref[...] = take(0, ff)
        up_ref[:, :d] = take(ff, ff + d)
        up_ref[:, d:] = take(ff + d, ff + 2 * d)
        wo_ref[...] = take(ff + 2 * d, ff + 3 * d)

    ordered_halves(core_ref, own_ref, got_ref, write)


def copy_kernel(in_ref, out_ref):
    out_ref[...] = in_ref[...].astype(out_ref.dtype)


def copy_call(order, values, dtype):
    parts, rows, d = values.shape
    spec = pl.BlockSpec((1, rows, d), lambda i: (i, 0, 0))
    return pl.pallas_call(
        lambda order_ref, in_ref, out_ref: copy_kernel(in_ref, out_ref),
        grid=(parts,),
        in_specs=[SMEM_SPEC, spec],
        out_specs=spec,
        out_shape=jax.ShapeDtypeStruct(values.shape, dtype),
        compiler_params=params(28),
        cost_estimate=cost(1e7, 1e5),
        name="copy",
    )(order, values)


def finish_last_kernel(core_ref, own_ref, got_ref, qkv_ref, *vec_refs):
    d = qkv_ref.shape[0]
    half = own_ref.shape[0]
    blocks = qkv_ref.shape[1] // LANES

    def write(low_ref, high_ref):
        for p in range(blocks):
            ref = (low_ref, high_ref)[p // (blocks // 2)]
            at = (p % (blocks // 2)) * d
            qkv_ref[:, p * LANES : (p + 1) * LANES] = ref[at : at + d].astype(F32)
        at = half - VEC_ROWS
        for ref in vec_refs:
            for g in range(ref.shape[1] // LANES):
                ref[:, g * LANES : (g + 1) * LANES] = low_ref[at : at + 1].astype(F32)
                at += 1

    ordered_halves(core_ref, own_ref, got_ref, write)


def finish_call(kernel, core, own, got, shapes, name):
    return pl.pallas_call(
        kernel,
        grid=(1,),
        in_specs=[SMEM_SPEC, whole(own.shape), whole(got.shape)],
        out_specs=[whole(shape) for shape in shapes],
        out_shape=[jax.ShapeDtypeStruct(shape, F32) for shape in shapes],
        compiler_params=params(28),
        cost_estimate=cost(1e8, 8e6),
        name=name,
    )(core, own, got)


def send_xor(values, flip):
    count = lax.axis_size(BOTH)
    return lax.ppermute(values, BOTH, [(i, i ^ flip) for i in range(count)])


def add_kernel(place_ref, *refs):
    outs = place_ref.shape[0]
    terms, results = refs[:-outs], refs[-outs:]
    size = results[0].shape[0]
    for flip, result in enumerate(results):
        rows = pl.ds(pl.multiple_of(jnp.bitwise_xor(place_ref[0], flip) * size, size), size)
        total = terms[0][rows, :].astype(F32)
        for term in terms[1:]:
            total = total + term[rows, :].astype(F32)
        result[...] = total.astype(result.dtype)


def add_call(place, parts, terms, own_dtype):
    rows, lanes = terms[0].shape
    shape = (rows // parts, lanes)
    places = jnp.broadcast_to(place, (parts,)).astype(jnp.int32)
    return pl.pallas_call(
        add_kernel,
        grid=(1,),
        in_specs=[SMEM_SPEC] + [whole(a.shape) for a in terms],
        out_specs=[whole(shape)] * parts,
        out_shape=[jax.ShapeDtypeStruct(shape, own_dtype if p == 0 else BF16) for p in range(parts)],
        compiler_params=params(28),
        cost_estimate=cost(1e8, 4e6),
        name="add",
    )(places, *terms)


def join_kernel(place_ref, *refs):
    out_ref = refs[-1]
    for flip, ref in enumerate(refs[:-1]):
        size = ref.shape[0]
        rows = pl.ds(pl.multiple_of(jnp.bitwise_xor(place_ref[0], flip) * size, size), size)
        out_ref[rows, :] = ref[...]


def join_call(place, pieces):
    rows, lanes = pieces[0].shape
    shape = (rows * len(pieces), lanes)
    return pl.pallas_call(
        join_kernel,
        grid=(1,),
        in_specs=[SMEM_SPEC] + [whole(p.shape) for p in pieces],
        out_specs=whole(shape),
        out_shape=jax.ShapeDtypeStruct(shape, pieces[0].dtype),
        compiler_params=params(28),
        cost_estimate=cost(1e8, 2e6),
        name="join",
    )(place[None].astype(jnp.int32), *pieces)


def swap_parts(parts, shift):
    return [send_xor(part, (flip + 1) << shift) for flip, part in enumerate(parts)]


def spread(part, shift, parts):
    return [send_xor(part, flip << shift) for flip in range(1, parts)]


def after(values, *others):
    return lax.optimization_barrier((values,) + others)[0]


def row_device(
    tokens, seg_lengths, ln1_gain, ln1_bias, w_qkv, b_qv, w_o, b_o, ln2_gain, ln2_bias,
    w_up, b_up, w_down, b_down, cotangent,
):
    row_count, slice_len, d = tokens.shape
    row = lax.axis_index("blk")
    me = lax.axis_index("rows") * lax.axis_size("blk") + row
    place_core = me & 1
    place_plane = (me >> 1) & 3
    place_deep = me >> 3
    core = place_core[None].astype(jnp.int32)
    blk = row[None].astype(jnp.int32)
    ends = jnp.cumsum(seg_lengths, axis=1)
    ends = lax.dynamic_index_in_dim(ends, row, 0, keepdims=False).astype(jnp.int32)

    def cut(values):
        return [lax.dynamic_index_in_dim(values, row ^ flip, 0, keepdims=False) for flip in range(row_count)]

    def swap(pieces):
        return [pieces[0]] + swap_parts(pieces[1:], 0)

    x = swap(cut(tokens))
    cot = cut(cotangent)
    cot = lax.optimization_barrier(tuple(cot) + tuple(x))[:row_count]
    cot = swap(list(cot))
    x, q, k, v, n1, att, lse = forward_call(ends, blk, x, ln1_gain, ln1_bias, w_qkv, b_qv)
    out, gmid, gatt, delta, keep, send, vec_mid = middle_call(
        core, blk, att, x, cot, w_o, b_o, ln2_gain, ln2_bias, w_up, b_up, w_down, b_down
    )

    def home(values):
        return lax.all_to_all(values.reshape(tokens.shape), "blk", 0, 0, tiled=True)

    own, *parts = add_call(place_plane, 4, [keep, send_xor(send, 1)], F32)
    grads = backward_call(after(ends, own), q, k, v, gatt, lse, delta, 0, d // LANES)
    own, *parts = add_call(after(place_deep, grads[0]), 4, [own] + swap_parts(parts, 1), F32)
    first = [own] + swap_parts(parts, 3)
    gin, keep, send = last_call(after(core, own), grads, n1, x, gmid, ln1_gain, w_qkv, vec_mid)
    output = home(after(out, send))
    (first,) = add_call(0, 1, first, BF16)
    send, first = lax.optimization_barrier((send, first))
    first_z = spread(first, 3, 2)
    own, *parts = add_call(place_plane, 4, [keep, send_xor(send, 1)], F32)
    first = join_call(after(place_deep & 1, own), [first] + first_z)
    first_z = spread(first, 4, 2)
    second = swap_parts(parts, 1)
    own, *parts = add_call(place_deep, 4, [own] + second, F32)
    first = join_call(place_deep >> 1, [first] + first_z)
    first, gin, output = lax.optimization_barrier((first, gin, output, own))[:3]
    gin = home(gin)
    (second,) = add_call(0, 1, [own] + swap_parts(parts, 3), BF16)
    first = join_call(after(place_plane & 1, second), [first] + spread(first, 1, 2))
    second = join_call(after(place_deep, gin), [second] + spread(second, 3, 4))
    first = join_call(after(place_plane >> 1, second), [first] + spread(first, 2, 2))
    order, output, gin = lax.optimization_barrier((core, output, gin, second))[:3]
    output = copy_call(order, output, BF16)
    input_grad = copy_call(order, gin, F32)
    second = join_call(after(place_plane, output, input_grad), [second] + spread(second, 1, 4))
    gw_down, gw_up, gw_o = finish_call(
        finish_mid_kernel, core, first, send_xor(first, 1), [w_down.shape, w_up.shape, w_o.shape], "finish_mid"
    )
    gw_qkv, *vecs = finish_call(
        finish_last_kernel, after(core, gw_down), second, send_xor(second, 1),
        [w_qkv.shape] + [(1, size) for size in (d, 2 * d, d, d, d, d, d, 2 * d)], "finish_last",
    )
    vecs = [vec.reshape(-1) for vec in vecs]
    g_down_b, g_up_b, g_ln2_gain, g_ln2_bias, g_o_b, g_ln1_gain, g_ln1_bias, g_qv_b = vecs
    return (
        output, input_grad, g_ln1_gain, g_ln1_bias, gw_qkv, g_qv_b, gw_o, g_o_b, g_ln2_gain, g_ln2_bias,
        gw_up, g_up_b, gw_down, g_down_b,
    )


def layer_norm(values, gain_vec, bias_vec):
    average = jnp.mean(values, axis=-1, keepdims=True)
    centered = values - average
    variance = jnp.mean(centered * centered, axis=-1, keepdims=True)
    return centered * lax.rsqrt(variance + norm_eps) * gain_vec + bias_vec


def segment_of(cell_ends, positions):
    return jnp.sum((cell_ends[:, None, :] <= positions[None, :, None]).astype(jnp.int32), axis=-1)


def block_scores(query_heads, key_heads, query_pos, key_pos, query_seg, key_seg, scale_qk):
    raw_scores = (
        jnp.einsum("rqhd,rkhd->rqhk", query_heads, key_heads, preferred_element_type=jnp.float32)
        * scale_qk
    )
    causal = key_pos[None, :] <= query_pos[:, None]
    same_cell = query_seg[:, :, None] == key_seg[:, None, :]
    allowed = (causal[None] & same_cell)[:, :, None, :]
    return (jnp.where(allowed, raw_scores, neg_big), allowed)


def block_active(query_pos, key_pos, query_seg, key_seg):
    return (key_pos[0] <= query_pos[-1]) & jnp.any(key_seg[:, -1] >= query_seg[:, 0])


def backward_block(
    query_heads,
    grad_heads,
    log_total,
    delta_sum,
    key_heads,
    value_heads,
    query_pos,
    key_pos,
    query_seg,
    key_seg,
    scale_qk,
):
    scores, allowed = block_scores(
        query_heads, key_heads, query_pos, key_pos, query_seg, key_seg, scale_qk
    )
    softmaxed = jnp.where(allowed, jnp.exp(scores - log_total[..., None]), 0.0)
    grad_probs = jnp.einsum(
        "rqhd,rkhd->rqhk", grad_heads, value_heads, preferred_element_type=jnp.float32
    )
    grad_scores = (softmaxed * (grad_probs - delta_sum[..., None])).astype(jnp.bfloat16)
    grad_query = (
        jnp.einsum("rqhk,rkhd->rqhd", grad_scores, key_heads, preferred_element_type=jnp.float32)
        * scale_qk
    )
    grad_key = (
        jnp.einsum("rqhk,rqhd->rkhd", grad_scores, query_heads, preferred_element_type=jnp.float32)
        * scale_qk
    )
    grad_value = jnp.einsum(
        "rqhk,rqhd->rkhd",
        softmaxed.astype(jnp.bfloat16),
        grad_heads,
        preferred_element_type=jnp.float32,
    )
    return (grad_query, grad_key, grad_value)


def unchanged(old_state):
    return old_state


def general_device(
    tokens,
    seg_lengths,
    ln1_gain,
    ln1_bias,
    w_qkv,
    b_qv,
    w_o,
    b_o,
    ln2_gain,
    ln2_bias,
    w_up,
    b_up,
    w_down,
    b_down,
    cotangent,
):
    row_count, slice_len, width_all = tokens.shape
    head_size = width_all // HEADS
    scale_qk = head_size ** (-0.5)
    head_shape = (row_count, slice_len, HEADS, head_size)
    stat_shape = (row_count, slice_len, HEADS)
    full_length = lax.axis_size("blk") * slice_len
    offsets = jnp.arange(slice_len, dtype=jnp.int32)
    query_pos = lax.axis_index("blk") * slice_len + offsets
    cell_ends = jnp.cumsum(seg_lengths, axis=1)
    query_seg = segment_of(cell_ends, query_pos)

    def take_block(piece, block_index):
        return lax.dynamic_slice_in_dim(piece, block_index * slice_len, slice_len, 1).reshape(
            head_shape
        )

    inputs = tokens.astype(jnp.float32)
    normed_val, first_pull = jax.vjp(layer_norm, inputs, ln1_gain, ln1_bias)
    normed_one = normed_val.astype(jnp.bfloat16)
    projected = jnp.dot(normed_one, w_qkv, preferred_element_type=jnp.float32)
    query_b = (projected[..., :width_all] + b_qv[:width_all]).astype(jnp.bfloat16)
    key_b = projected[..., width_all : 2 * width_all].astype(jnp.bfloat16)
    value_b = (projected[..., 2 * width_all :] + b_qv[width_all:]).astype(jnp.bfloat16)
    query_heads = query_b.reshape(head_shape)
    start_state = (
        jnp.full(stat_shape, neg_big, jnp.float32),
        jnp.zeros(stat_shape, jnp.float32),
        jnp.zeros(head_shape, jnp.float32),
    )
    key_piece = lax.all_gather(key_b, "blk", axis=1, tiled=True)
    value_piece = lax.all_gather(value_b, "blk", axis=1, tiled=True)

    def forward_block_step(block_index, inner_state):
        key_pos = block_index * slice_len + offsets
        key_seg = segment_of(cell_ends, key_pos)
        key_heads = take_block(key_piece, block_index)
        value_heads = take_block(value_piece, block_index)

        def forward_update(old_state):
            running_top, running_total, running_sum = old_state
            scores, allowed = block_scores(
                query_heads, key_heads, query_pos, key_pos, query_seg, key_seg, scale_qk
            )
            new_top = jnp.maximum(running_top, jnp.max(scores, axis=-1))
            factor = jnp.exp(running_top - new_top)
            weights_now = jnp.where(allowed, jnp.exp(scores - new_top[..., None]), 0.0)
            new_total = running_total * factor + jnp.sum(weights_now, axis=-1)
            new_sum = running_sum * factor[..., None] + jnp.einsum(
                "rqhk,rkhd->rqhd",
                weights_now.astype(jnp.bfloat16),
                value_heads,
                preferred_element_type=jnp.float32,
            )
            return (new_top, new_total, new_sum)

        return lax.cond(
            block_active(query_pos, key_pos, query_seg, key_seg),
            forward_update,
            unchanged,
            inner_state,
        )

    running_top, running_total, running_sum = lax.fori_loop(
        0, key_piece.shape[1] // slice_len, forward_block_step, start_state
    )
    attn_f32 = (running_sum / running_total[..., None]).reshape(row_count, slice_len, width_all)
    log_total = running_top + jnp.log(running_total)
    attn_b = attn_f32.astype(jnp.bfloat16)
    middle = inputs + jnp.dot(attn_b, w_o, preferred_element_type=jnp.float32) + b_o
    normed_two_val, second_pull = jax.vjp(layer_norm, middle, ln2_gain, ln2_bias)
    normed_two = normed_two_val.astype(jnp.bfloat16)
    hidden_pre = jnp.dot(normed_two, w_up, preferred_element_type=jnp.float32) + b_up
    hidden_val, gelu_pull = jax.vjp(jax.nn.gelu, hidden_pre)
    hidden_b = hidden_val.astype(jnp.bfloat16)
    output = (
        middle + jnp.dot(hidden_b, w_down, preferred_element_type=jnp.float32) + b_down
    ).astype(jnp.bfloat16)
    grad_out = cotangent.astype(jnp.float32)
    grad_w_down = jnp.einsum("rcf,rcd->fd", hidden_b, cotangent, preferred_element_type=jnp.float32)
    grad_b_down = jnp.sum(grad_out, axis=(0, 1))
    grad_hidden = jnp.einsum("rcd,fd->rcf", cotangent, w_down, preferred_element_type=jnp.float32)
    (grad_pre,) = gelu_pull(grad_hidden)
    grad_pre_b = grad_pre.astype(jnp.bfloat16)
    grad_w_up = jnp.einsum(
        "rcd,rcf->df", normed_two, grad_pre_b, preferred_element_type=jnp.float32
    )
    grad_b_up = jnp.sum(grad_pre_b.astype(jnp.float32), axis=(0, 1))
    grad_normed_two = jnp.einsum(
        "rcf,df->rcd", grad_pre_b, w_up, preferred_element_type=jnp.float32
    )
    grad_mid_norm, grad_ln2_gain, grad_ln2_bias = second_pull(grad_normed_two)
    grad_middle = grad_out + grad_mid_norm
    grad_branch_b = grad_middle.astype(jnp.bfloat16)
    grad_w_o = jnp.einsum("rce,rcd->ed", attn_b, grad_branch_b, preferred_element_type=jnp.float32)
    grad_b_o = jnp.sum(grad_branch_b.astype(jnp.float32), axis=(0, 1))
    grad_attn_b = jnp.einsum(
        "rcd,ed->rce", grad_branch_b, w_o, preferred_element_type=jnp.float32
    ).astype(jnp.bfloat16)
    delta_sum = jnp.sum((grad_attn_b.astype(jnp.float32) * attn_f32).reshape(head_shape), axis=-1)
    grad_heads = grad_attn_b.reshape(head_shape)
    whole_shape = (row_count, full_length, HEADS, head_size)
    back_state = (
        jnp.zeros(head_shape, jnp.float32),
        jnp.zeros(whole_shape, jnp.float32),
        jnp.zeros(whole_shape, jnp.float32),
    )
    backward_key_piece = lax.all_gather(key_b, "blk", axis=1, tiled=True)
    backward_value_piece = lax.all_gather(value_b, "blk", axis=1, tiled=True)

    def backward_block_step(block_index, inner_state):
        key_pos = block_index * slice_len + offsets
        key_seg = segment_of(cell_ends, key_pos)
        key_heads = take_block(backward_key_piece, block_index)
        value_heads = take_block(backward_value_piece, block_index)

        def backward_update(old_state):
            grad_query, grad_key, grad_value = backward_block(
                query_heads,
                grad_heads,
                log_total,
                delta_sum,
                key_heads,
                value_heads,
                query_pos,
                key_pos,
                query_seg,
                key_seg,
                scale_qk,
            )
            at_row = block_index * slice_len
            return (
                old_state[0] + grad_query,
                lax.dynamic_update_slice_in_dim(old_state[1], grad_key, at_row, 1),
                lax.dynamic_update_slice_in_dim(old_state[2], grad_value, at_row, 1),
            )

        return lax.cond(
            block_active(query_pos, key_pos, query_seg, key_seg),
            backward_update,
            unchanged,
            inner_state,
        )

    back_result = lax.fori_loop(
        0, backward_key_piece.shape[1] // slice_len, backward_block_step, back_state
    )
    grad_query_sum = back_result[0]
    grad_key_sum, grad_value_sum = (
        lax.psum_scatter(
            back_result[1].astype(jnp.bfloat16), "blk", scatter_dimension=1, tiled=True
        ).astype(jnp.float32),
        lax.psum_scatter(
            back_result[2].astype(jnp.bfloat16), "blk", scatter_dimension=1, tiled=True
        ).astype(jnp.float32),
    )
    flat_shape = (row_count, slice_len, width_all)
    grad_qkv_b = jnp.concatenate(
        [
            grad_query_sum.reshape(flat_shape),
            grad_key_sum.reshape(flat_shape),
            grad_value_sum.reshape(flat_shape),
        ],
        axis=-1,
    ).astype(jnp.bfloat16)
    grad_w_qkv = jnp.einsum(
        "rcd,rce->de", normed_one, grad_qkv_b, preferred_element_type=jnp.float32
    )
    column_sums = jnp.sum(grad_qkv_b.astype(jnp.float32), axis=(0, 1))
    grad_b_qv = jnp.concatenate([column_sums[:width_all], column_sums[2 * width_all :]])
    grad_normed_one = jnp.einsum(
        "rce,de->rcd", grad_qkv_b, w_qkv, preferred_element_type=jnp.float32
    )
    grad_in_norm, grad_ln1_gain, grad_ln1_bias = first_pull(grad_normed_one)
    input_grad = grad_middle + grad_in_norm
    grads = (
        grad_ln1_gain,
        grad_ln1_bias,
        grad_w_qkv,
        grad_b_qv,
        grad_w_o,
        grad_b_o,
        grad_ln2_gain,
        grad_ln2_bias,
        grad_w_up,
        grad_b_up,
        grad_w_down,
        grad_b_down,
    )
    summed = lax.psum(
        (
            grads[0],
            grads[1],
            grads[2],
            grads[3],
            grads[4],
            grads[5],
            grads[6],
            grads[7],
            grads[8],
            grads[9],
            grads[10],
            grads[11],
        ),
        ("rows", "blk"),
    )
    return (
        output,
        input_grad,
        summed[0],
        summed[1],
        summed[2],
        summed[3],
        summed[4],
        summed[5],
        summed[6],
        summed[7],
        summed[8],
        summed[9],
        summed[10],
        summed[11],
    )


def device_function(tokens, *rest):
    d = tokens.shape[2]
    whole_rows = (
        lax.axis_size("blk") == tokens.shape[0] == 4
        and lax.axis_size("rows") == 8
        and tokens.shape[1] == TILE
        and d == 512
    )
    return (row_device if whole_rows else general_device)(tokens, *rest)


def solution(mesh):
    in_specs = (
        P("rows", "blk", None),
        P("rows", None),
        P(),
        P(),
        P(),
        P(),
        P(),
        P(),
        P(),
        P(),
        P(),
        P(),
        P(),
        P(),
        P("rows", "blk", None),
    )
    out_specs = (
        P("rows", "blk", None),
        P("rows", "blk", None),
        P(),
        P(),
        P(),
        P(),
        P(),
        P(),
        P(),
        P(),
        P(),
        P(),
        P(),
        P(),
    )
    return jax.shard_map(
        device_function, mesh=mesh, in_specs=in_specs, out_specs=out_specs, check_vma=False
    )
```

```python
import functools

import jax
import jax.numpy as jnp
from jax import lax
from jax.experimental import pallas as pl
from jax.experimental.pallas import tpu as pltpu
from jax.sharding import PartitionSpec as P

HEADS = 8
norm_eps = 1e-05
neg_big = -1e30
BOTH = ("rows", "blk")
F32 = jnp.float32
BF16 = jnp.bfloat16
TILE = 256
LANES = 128
MIB = 1024 * 1024
B_FLOPS = 1e9
L_FLOPS = 1e9
MID_TILE = 512
MID_MIB = 28
LAST_MIB = 26


def mm(lhs, rhs):
    return lax.dot_general(lhs, rhs, (((1,), (0,)), ((), ())), preferred_element_type=F32)


def mm_nt(lhs, rhs):
    return lax.dot_general(lhs, rhs, (((1,), (1,)), ((), ())), preferred_element_type=F32)


def mm_tn(lhs, rhs):
    return lax.dot_general(lhs, rhs, (((0,), (0,)), ((), ())), preferred_element_type=F32)


def cell_start(ends_ref, positions):
    start = jnp.zeros_like(positions)
    for c in range(ends_ref.shape[0]):
        start = jnp.where(ends_ref[c] <= positions, ends_ref[c], start)
    return start


def norm_parts(values):
    average = jnp.mean(values, axis=-1, keepdims=True)
    centered = values - average
    variance = jnp.mean(centered * centered, axis=-1, keepdims=True)
    scale = lax.rsqrt(variance + norm_eps)
    return centered * scale, scale


def norm_pull(e, n, scale, gain):
    f = e * gain
    return (
        f
        - jnp.mean(f, axis=-1, keepdims=True)
        - n * jnp.mean(f * n, axis=-1, keepdims=True)
    ) * scale


def head_lanes(shape, half):
    lane = lax.broadcasted_iota(jnp.int32, shape, len(shape) - 1)
    return (lane < LANES // 2) if half == 0 else (lane >= LANES // 2)


def only_head(values, half):
    return jnp.where(head_lanes(values.shape, half), values, jnp.zeros_like(values))


def in_order(blk_ref, pieces, whole_ref):
    size = pieces[0].shape[0]
    for flip, piece_ref in enumerate(pieces):
        at = jnp.bitwise_xor(blk_ref[0], flip) * size
        whole_ref[pl.ds(pl.multiple_of(at, size), size), :] = piece_ref[...]


def forward_kernel(
    ends_ref, blk_ref, x0_ref, x1_ref, x2_ref, x3_ref, gain_ref, bias_ref, w_ref, b_ref,
    x_ref, q_ref, k_ref, v_ref, n1_ref, att_ref, lse_ref,
    mask_ref,
):
    in_order(blk_ref, (x0_ref, x1_ref, x2_ref, x3_ref), x_ref)
    t, width = x_ref.shape
    pairs = width // LANES
    scale_qk = (width // HEADS) ** (-0.5)
    for low in range(0, t, 512):
        rows = slice(low, low + 512)
        n, _ = norm_parts(x_ref[rows].astype(F32))
        n1 = (n * gain_ref[...] + bias_ref[...]).astype(BF16)
        n1_ref[rows] = n1
        q = mm(n1, w_ref[:, :width]) + b_ref[:, :width]
        q = (q.astype(BF16).astype(F32) * scale_qk).astype(BF16)
        k = mm(n1, w_ref[:, width : 2 * width]).astype(BF16)
        v = (mm(n1, w_ref[:, 2 * width :]) + b_ref[:, width:]).astype(BF16)
        for g in range(pairs):
            cols = slice(g * LANES, (g + 1) * LANES)
            q_ref[g, rows, :] = q[:, cols]
            k_ref[g, rows, :] = k[:, cols]
            v_ref[g, rows, :] = v[:, cols]
    for low in range(0, t, TILE):
        reach = low + TILE
        rows = slice(low, reach)
        q_pos = low + lax.broadcasted_iota(jnp.int32, (TILE, 1), 0)
        k_pos = lax.broadcasted_iota(jnp.int32, (TILE, reach), 1)
        start = cell_start(ends_ref, q_pos)
        mask_ref[:, :reach] = jnp.where((k_pos <= q_pos) & (k_pos >= start), 0.0, neg_big)
        lse_all = jnp.zeros((TILE, LANES), F32)
        lane = lax.broadcasted_iota(jnp.int32, lse_all.shape, 1)
        for g in range(pairs):
            qp = q_ref[g, rows, :]
            kp = k_ref[g, :reach, :]
            vp = v_ref[g, :reach, :]
            outs = []
            for half in range(2):
                s = mm_nt(only_head(qp, half), kp) + mask_ref[:, :reach]
                top = jnp.max(s, axis=-1, keepdims=True)
                p = jnp.exp(s - top)
                total = jnp.sum(p, axis=-1, keepdims=True)
                outs.append(mm(p.astype(BF16), vp) / total)
                lse_all = jnp.where(lane == 2 * g + half, top + jnp.log(total), lse_all)
            att_ref[g, rows, :] = jnp.where(head_lanes(outs[0].shape, 0), outs[0], outs[1])
        lse_ref[:, rows] = jnp.transpose(lse_all)[:HEADS]


def whole(shape):
    return pl.BlockSpec(shape, lambda i: (0,) * len(shape))


def by_row(cols, tile=TILE):
    return pl.BlockSpec((tile, cols), lambda i: (i, 0))


def by_pair(pairs, tile=TILE):
    return pl.BlockSpec((pairs, tile, LANES), lambda i: (0, i, 0))


def heads_row(tile=TILE):
    return pl.BlockSpec((HEADS, tile), lambda i: (0, i))


SMEM_SPEC = pl.BlockSpec(memory_space=pltpu.SMEM)


def in_hbm(*arrays):
    return [pltpu.with_memory_space_constraint(a, pltpu.HBM) for a in arrays]


def params(mib):
    return pltpu.CompilerParams(dimension_semantics=("arbitrary",), vmem_limit_bytes=mib * MIB)


def cost(flops, moved):
    return pl.CostEstimate(flops=int(flops), bytes_accessed=int(moved), transcendentals=0)


def forward_call(ends, blk, pieces, gain, bias, w_qkv, b_qv):
    size, d = pieces[0].shape
    t = size * len(pieces)
    pairs = d // LANES
    return pl.pallas_call(
        forward_kernel,
        grid=(1,),
        in_specs=[SMEM_SPEC, SMEM_SPEC]
        + [whole((size, d))] * len(pieces)
        + [whole((1, d)), whole((1, d)), whole(w_qkv.shape), whole((1, 2 * d))],
        out_specs=[
            whole((t, d)), whole((pairs, t, LANES)), whole((pairs, t, LANES)), whole((pairs, t, LANES)), whole((t, d)),
            whole((pairs, t, LANES)), whole((HEADS, t)),
        ],
        out_shape=[
            jax.ShapeDtypeStruct((t, d), BF16),
            pltpu.HBM((pairs, t, LANES), BF16),
            pltpu.HBM((pairs, t, LANES), BF16),
            pltpu.HBM((pairs, t, LANES), BF16),
            pltpu.HBM((t, d), BF16),
            jax.ShapeDtypeStruct((pairs, t, LANES), F32),
            jax.ShapeDtypeStruct((HEADS, t), F32),
        ],
        scratch_shapes=[pltpu.VMEM((TILE, t), F32)],
        compiler_params=params(34),
        cost_estimate=cost(20e9, 10e6),
        name="forward",
    )(ends, blk, *pieces, gain[None], bias[None], w_qkv, b_qv[None])


def leave(blk_ref, whole_ref, own_ref, near_ref, far_ref):
    size = own_ref.shape[0]
    for flip, dest in ((0, own_ref), (1, near_ref), (2, far_ref.at[:size]), (3, far_ref.at[size:])):
        at = jnp.bitwise_xor(blk_ref[0], flip) * size
        dest[...] = whole_ref[pl.ds(pl.multiple_of(at, size), size), :]


def relay_kernel(near_ref, far_ref, out_ref):
    size = near_ref.shape[0]
    out_ref[:size] = near_ref[...]
    out_ref[size:] = far_ref[size:]


def relay_call(near, far):
    return pl.pallas_call(
        relay_kernel,
        grid=(1,),
        in_specs=[whole(near.shape), whole(far.shape)],
        out_specs=whole(far.shape),
        out_shape=jax.ShapeDtypeStruct(far.shape, far.dtype),
        compiler_params=params(8),
        cost_estimate=cost(1e7, 1e5),
        name="relay",
    )(near, far)


def arrive_kernel(blk_ref, own_ref, near_ref, far_ref, out_ref):
    size = own_ref.shape[0]
    pieces = (own_ref[...], near_ref[:size], far_ref[:size], near_ref[size:])
    for flip, piece in enumerate(pieces):
        out_ref[jnp.bitwise_xor(blk_ref[0], flip)] = piece.astype(out_ref.dtype)


def arrive_call(blk, own, near, far, dtype):
    shape = (4,) + own.shape
    return pl.pallas_call(
        arrive_kernel,
        grid=(1,),
        in_specs=[SMEM_SPEC, whole(own.shape), whole(near.shape), whole(far.shape)],
        out_specs=whole(shape),
        out_shape=jax.ShapeDtypeStruct(shape, dtype),
        compiler_params=params(12),
        cost_estimate=cost(1e7, 1e5),
        name="arrive",
    )(blk, own, near, far)


def split_halves(core_ref, whole_ref, keep_ref, send_ref):
    half = keep_ref.shape[0]
    core = core_ref[0]
    keep_ref[...] = whole_ref[pl.ds(pl.multiple_of(core * half, half), half), :]
    send_ref[...] = whole_ref[pl.ds(pl.multiple_of((1 - core) * half, half), half), :].astype(BF16)


def middle_kernel(
    core_ref, blk_ref, att_ref, x_ref, c0_ref, c1_ref, c2_ref, c3_ref, wo_ref, bo_ref, gain_ref, bias_ref, wup_ref, bup_ref, wdown_ref, bdown_ref,
    o0_ref, o1_ref, o2_ref, gmid_ref, gatt_ref, delta_ref, keep_ref, send_ref, vec_ref,
    cot_ref, out_ref, gw_ref, hidden_ref, gpre_ref, n2_ref, attb_ref, gbr_ref,
):
    pairs = att_ref.shape[0]
    t, d = x_ref.shape
    ff = wup_ref.shape[-1]
    c0 = 0.7978845608028654
    c1 = 0.044715

    def col(values):
        return jnp.sum(values, axis=0, keepdims=True)

    in_order(blk_ref, (c0_ref, c1_ref, c2_ref, c3_ref), cot_ref)
    vec_ref[...] = jnp.zeros_like(vec_ref)
    head = lax.broadcasted_iota(jnp.int32, (HEADS, d), 0)
    lane = lax.broadcasted_iota(jnp.int32, (HEADS, d), 1)
    ones = jnp.where(lane // (d // HEADS) == head, 1.0, 0.0).astype(BF16)
    def tile(step, carry):
        rows = pl.ds(pl.multiple_of(step * MID_TILE, MID_TILE), MID_TILE)
        att = jnp.concatenate([att_ref[g, rows, :] for g in range(pairs)], axis=-1)
        att_b = att.astype(BF16)
        attb_ref[rows, :] = att_b
        middle = x_ref[rows, :].astype(F32) + mm(att_b, wo_ref[...]) + bo_ref[...]
        n, scale = norm_parts(middle)
        n2 = (n * gain_ref[...] + bias_ref[...]).astype(BF16)
        n2_ref[rows, :] = n2
        pre = mm(n2, wup_ref[...]) + bup_ref[...]
        sq = pre * pre
        th = jnp.tanh(c0 * (pre + c1 * (sq * pre)))
        half_one = 0.5 * (1.0 + th)
        hidden = (pre * half_one).astype(BF16)
        hidden_ref[rows, :] = hidden
        slope = half_one + (0.5 * pre) * (1.0 - th * th) * (c0 + (3.0 * c0 * c1) * sq)
        out_ref[rows, :] = (middle + mm(hidden, wdown_ref[...]) + bdown_ref[...]).astype(BF16)
        cot = cot_ref[rows, :]
        cot_f = cot.astype(F32)
        gpre = (mm_nt(cot, wdown_ref[...]) * slope).astype(BF16)
        gpre_ref[rows, :] = gpre
        e = mm_nt(gpre, wup_ref[...])
        gmid = cot_f + norm_pull(e, n, scale, gain_ref[...])
        gmid_ref[rows, :] = gmid
        gbr = gmid.astype(BF16)
        gbr_ref[rows, :] = gbr
        gatt = mm_nt(gbr, wo_ref[...]).astype(BF16)
        for g in range(pairs):
            gatt_ref[g, rows, :] = gatt[:, g * LANES : (g + 1) * LANES]
        prod = gatt.astype(F32) * att
        hi = prod.astype(BF16)
        lo = (prod - hi.astype(F32)).astype(BF16)
        delta_ref[:, rows] = mm_nt(ones, hi) + mm_nt(ones, lo)
        gsum = col(gpre.astype(F32))
        vec_ref[0:1] += col(cot_f)
        vec_ref[1:2] += gsum[:, :d]
        vec_ref[2:3] += gsum[:, d:]
        vec_ref[3:4] += col(e * n)
        vec_ref[4:5] += col(e)
        vec_ref[5:6] += col(gbr.astype(F32))
        return carry

    lax.fori_loop(0, t // MID_TILE, tile, 0)
    leave(blk_ref, out_ref, o0_ref, o1_ref, o2_ref)
    gw_ref[:ff] = mm_tn(hidden_ref[...], cot_ref[...])
    gw_ref[ff : ff + d] = mm_tn(n2_ref[...], gpre_ref[:, :d])
    gw_ref[ff + d : ff + 2 * d] = mm_tn(n2_ref[...], gpre_ref[:, d:])
    gw_ref[ff + 2 * d :] = mm_tn(attb_ref[...], gbr_ref[...])
    split_halves(core_ref, gw_ref, keep_ref, send_ref)


def middle_call(core, blk, att, x, cots, w_o, b_o, gain, bias, w_up, b_up, w_down, b_down):
    t, d = x.shape
    pairs = d // LANES
    ff = w_up.shape[1]
    half = (ff + 3 * d) // 2
    return pl.pallas_call(
        middle_kernel,
        grid=(1,),
        in_specs=[
            SMEM_SPEC, SMEM_SPEC,
            by_pair(pairs, t), by_row(d, t), *[whole(c.shape) for c in cots], whole((d, d)), whole((1, d)), whole((1, d)), whole((1, d)),
            whole((d, ff)), whole((1, ff)), whole((ff, d)), whole((1, d)),
        ],
        out_specs=[
            whole((t // 4, d)), whole((t // 4, d)), whole((t // 2, d)), by_row(d, t), by_pair(pairs, t), heads_row(t), whole((half, d)), whole((half, d)),
            whole((8, d)),
        ],
        out_shape=[
            pltpu.HBM((t // 4, d), BF16),
            pltpu.HBM((t // 4, d), BF16),
            pltpu.HBM((t // 2, d), BF16),
            pltpu.HBM((t, d), F32),
            pltpu.HBM((pairs, t, LANES), BF16),
            jax.ShapeDtypeStruct((HEADS, t), F32),
            jax.ShapeDtypeStruct((half, d), F32),
            jax.ShapeDtypeStruct((half, d), BF16),
            jax.ShapeDtypeStruct((8, d), F32),
        ],
        scratch_shapes=[
            pltpu.VMEM((t, d), BF16),
            pltpu.VMEM((t, d), BF16),
            pltpu.VMEM((2 * half, d), F32),
            pltpu.VMEM((t, ff), BF16),
            pltpu.VMEM((t, ff), BF16),
            pltpu.VMEM((t, d), BF16),
            pltpu.VMEM((t, d), BF16),
            pltpu.VMEM((t, d), BF16),
        ],
        compiler_params=params(30),
        cost_estimate=cost(15e9, 20e6),
        name="middle",
    )(core, blk, att, x, *cots, w_o, b_o[None], gain[None], bias[None], w_up, b_up[None], w_down, b_down[None])


def backward_kernel(first, ends_ref, q_ref, k_ref, v_ref, g_ref, lse_ref, delta_ref, dq_ref, dk_ref, dv_ref, acc_ref):
    pair = pl.program_id(0) + first
    t = q_ref.shape[1]
    scale_qk = (LANES // 2) ** (-0.5)
    pos_row = lax.broadcasted_iota(jnp.int32, (1, t), 1)
    start_row = cell_start(ends_ref, pos_row)
    acc_ref[...] = jnp.zeros_like(acc_ref)
    jobs = [(j, half) for j in range(t // TILE) for half in range(2)]
    lses = [lse_ref[pl.ds(2 * pair + half, 1), :] for half in range(2)]
    deltas = [delta_ref[pl.ds(2 * pair + half, 1), :] for half in range(2)]
    kts = {}
    outs = {}

    def scores(job):
        j, half = job
        low = j * TILE
        km = only_head(k_ref[0, low : low + TILE, :], half)
        vm = only_head(v_ref[0, low : low + TILE, :], half)
        return mm_nt(km, q_ref[0, low:, :]), mm_nt(vm, g_ref[0, low:, :])

    def rest(job, s, dp):
        j, half = job
        low = j * TILE
        k_pos = low + lax.broadcasted_iota(jnp.int32, (TILE, t - low), 0)
        high = low + TILE
        diag = (k_pos[:, :TILE] >= start_row[:, low:high]) & (k_pos[:, :TILE] <= pos_row[:, low:high])
        p = jnp.exp(jnp.where(diag, s[:, :TILE] - lses[half][:, low:high], neg_big))
        if high < t:
            far = k_pos[:, TILE:] >= start_row[:, high:]
            p = jnp.concatenate([p, jnp.exp(jnp.where(far, s[:, TILE:] - lses[half][:, high:], neg_big))], axis=1)
        ds = (p * (dp - deltas[half][:, low:])).astype(BF16)
        dv = mm(p.astype(BF16), g_ref[0, low:, :])
        dk = mm(ds, q_ref[0, low:, :])
        kt = jnp.transpose(k_ref[0, low : low + TILE, :])
        rows = slice(half * 64, half * 64 + 64)
        acc_ref[rows, low:] += mm(kt[rows], ds)
        if half == 0:
            outs[j] = (dk, dv)
        else:
            first_lanes = head_lanes(dk.shape, 0)
            dk_ref[0, low : low + TILE, :] = jnp.where(first_lanes, outs[j][0], dk).astype(BF16)
            dv_ref[0, low : low + TILE, :] = jnp.where(first_lanes, outs[j][1], dv).astype(BF16)

    ready = scores(jobs[0])
    for at, job in enumerate(jobs):
        now = ready
        if at + 1 < len(jobs):
            ready = scores(jobs[at + 1])
        rest(job, *now)
    dq_ref[0] = jnp.transpose((acc_ref[...] * scale_qk)).astype(BF16)


def backward_call(ends, q, k, v, gatt, lse, delta, first, count):
    pairs, t, _ = q.shape
    spec = pl.BlockSpec((1, t, LANES), lambda i: (i + first, 0, 0))
    out = pl.BlockSpec((1, t, LANES), lambda i: (i, 0, 0))
    return pl.pallas_call(
        functools.partial(backward_kernel, first),
        grid=(count,),
        in_specs=[SMEM_SPEC, spec, spec, spec, spec, whole((HEADS, t)), whole((HEADS, t))],
        out_specs=[out, out, out],
        out_shape=[pltpu.HBM((count, t, LANES), BF16)] * 3,
        scratch_shapes=[pltpu.VMEM((LANES, t), F32)],
        compiler_params=params(28),
        cost_estimate=cost(count * B_FLOPS, count * 1e5),
        name="backward",
    )(ends, *in_hbm(q, k, v, gatt), lse, delta)


VEC_ROWS = 128


def last_kernel(*refs):
    core_ref, blk_ref = refs[:2]
    grads = refs[2:5]
    n1_ref, x_ref, gmid_ref, gain_ref, w_ref, vecmid_ref = refs[5:11]
    g0_ref, g1_ref, g2_ref, keep_ref, send_ref, gw_ref, gin_ref = refs[11:]
    pairs = grads[0].shape[0]
    d = x_ref.shape[-1]
    half = keep_ref.shape[0]
    gqkv = jnp.concatenate([grads[part][g] for part in range(3) for g in range(pairs)], axis=-1)
    gw = mm_tn(n1_ref[...], gqkv)
    blocks = 3 * pairs
    for p in range(blocks):
        at = (p // (blocks // 2)) * half + (p % (blocks // 2)) * d
        gw_ref[at : at + d] = gw[:, p * LANES : (p + 1) * LANES]
    e = mm_nt(gqkv, w_ref[...])
    n, scale = norm_parts(x_ref[...].astype(F32))
    gin_ref[...] = (gmid_ref[...] + norm_pull(e, n, scale, gain_ref[...])).astype(BF16)
    leave(blk_ref, gin_ref, g0_ref, g1_ref, g2_ref)

    def col(values):
        return jnp.sum(values, axis=0, keepdims=True)

    rows = [vecmid_ref[r : r + 1] for r in range(6)]
    rows += [col(e * n), col(e), col(gqkv[:, :d].astype(F32)), col(gqkv[:, 2 * d :].astype(F32))]
    base = half - VEC_ROWS
    gw_ref[base:half] = jnp.zeros((VEC_ROWS, LANES), F32)
    gw_ref[half + base :] = jnp.zeros((VEC_ROWS, LANES), F32)
    for r, row in enumerate(rows):
        for g in range(d // LANES):
            at = base + r * (d // LANES) + g
            gw_ref[at : at + 1] = row[:, g * LANES : (g + 1) * LANES]
    split_halves(core_ref, gw_ref, keep_ref, send_ref)


def last_call(core, blk, grads, n1, x, gmid, gain, w_qkv, vec_mid):
    t, d = x.shape
    half = 3 * d * d // LANES // 2 + VEC_ROWS
    return pl.pallas_call(
        last_kernel,
        grid=(1,),
        in_specs=[SMEM_SPEC, SMEM_SPEC]
        + [whole(a.shape) for a in grads]
        + [by_row(d, t), by_row(d, t), by_row(d, t), whole((1, d)), whole(w_qkv.shape), whole((8, d))],
        out_specs=[whole((t // 4, d)), whole((t // 4, d)), whole((t // 2, d)), whole((half, LANES)), whole((half, LANES))],
        out_shape=[
            pltpu.HBM((t // 4, d), BF16),
            pltpu.HBM((t // 4, d), BF16),
            pltpu.HBM((t // 2, d), BF16),
            jax.ShapeDtypeStruct((half, LANES), F32),
            jax.ShapeDtypeStruct((half, LANES), BF16),
        ],
        scratch_shapes=[pltpu.VMEM((2 * half, LANES), F32), pltpu.VMEM((t, d), BF16)],
        compiler_params=params(28),
        cost_estimate=cost(L_FLOPS, 1e5),
        name="last",
    )(core, blk, *in_hbm(*grads), n1, x, gmid, gain[None], w_qkv, vec_mid)


def ordered_halves(core_ref, own_ref, got_ref, write):
    pl.when(core_ref[0] == 0)(functools.partial(write, own_ref, got_ref))
    pl.when(core_ref[0] == 1)(functools.partial(write, got_ref, own_ref))


def finish_mid_kernel(core_ref, own_ref, got_ref, down_ref, up_ref, wo_ref):
    ff, d = down_ref.shape
    half = own_ref.shape[0]

    def write(low_ref, high_ref):
        def take(first, last):
            if last <= half:
                return low_ref[first:last].astype(F32)
            if first >= half:
                return high_ref[first - half : last - half].astype(F32)
            return jnp.concatenate([take(first, half), take(half, last)], axis=0)

        down_ref[...] = take(0, ff)
        up_ref[:, :d] = take(ff, ff + d)
        up_ref[:, d:] = take(ff + d, ff + 2 * d)
        wo_ref[...] = take(ff + 2 * d, ff + 3 * d)

    ordered_halves(core_ref, own_ref, got_ref, write)


def finish_last_kernel(core_ref, own_ref, got_ref, qkv_ref, *vec_refs):
    d = qkv_ref.shape[0]
    half = own_ref.shape[0]
    blocks = qkv_ref.shape[1] // LANES

    def write(low_ref, high_ref):
        for p in range(blocks):
            ref = (low_ref, high_ref)[p // (blocks // 2)]
            at = (p % (blocks // 2)) * d
            qkv_ref[:, p * LANES : (p + 1) * LANES] = ref[at : at + d].astype(F32)
        at = half - VEC_ROWS
        for ref in vec_refs:
            for g in range(ref.shape[1] // LANES):
                ref[:, g * LANES : (g + 1) * LANES] = low_ref[at : at + 1].astype(F32)
                at += 1

    ordered_halves(core_ref, own_ref, got_ref, write)


def finish_call(kernel, core, own, got, shapes, name):
    return pl.pallas_call(
        kernel,
        grid=(1,),
        in_specs=[SMEM_SPEC, whole(own.shape), whole(got.shape)],
        out_specs=[whole(shape) for shape in shapes],
        out_shape=[jax.ShapeDtypeStruct(shape, F32) for shape in shapes],
        compiler_params=params(28),
        cost_estimate=cost(1e8, 8e6),
        name=name,
    )(core, own, got)


def send_xor(values, flip):
    count = lax.axis_size(BOTH)
    return lax.ppermute(values, BOTH, [(i, i ^ flip) for i in range(count)])


def add_kernel(place_ref, *refs):
    outs = place_ref.shape[0]
    terms, results = refs[:-outs], refs[-outs:]
    size = results[0].shape[0]
    for flip, result in enumerate(results):
        rows = pl.ds(pl.multiple_of(jnp.bitwise_xor(place_ref[0], flip) * size, size), size)
        total = terms[0][rows, :].astype(F32)
        for term in terms[1:]:
            total = total + term[rows, :].astype(F32)
        result[...] = total.astype(result.dtype)


def add_call(place, parts, terms, own_dtype):
    rows, lanes = terms[0].shape
    shape = (rows // parts, lanes)
    places = jnp.broadcast_to(place, (parts,)).astype(jnp.int32)
    return pl.pallas_call(
        add_kernel,
        grid=(1,),
        in_specs=[SMEM_SPEC] + [whole(a.shape) for a in terms],
        out_specs=[whole(shape)] * parts,
        out_shape=[jax.ShapeDtypeStruct(shape, own_dtype if p == 0 else BF16) for p in range(parts)],
        compiler_params=params(28),
        cost_estimate=cost(1e8, 4e6),
        name="add",
    )(places, *terms)


def join_kernel(place_ref, *refs):
    out_ref = refs[-1]
    for flip, ref in enumerate(refs[:-1]):
        size = ref.shape[0]
        rows = pl.ds(pl.multiple_of(jnp.bitwise_xor(place_ref[0], flip) * size, size), size)
        out_ref[rows, :] = ref[...]


def join_call(place, pieces):
    rows, lanes = pieces[0].shape
    shape = (rows * len(pieces), lanes)
    return pl.pallas_call(
        join_kernel,
        grid=(1,),
        in_specs=[SMEM_SPEC] + [whole(p.shape) for p in pieces],
        out_specs=whole(shape),
        out_shape=jax.ShapeDtypeStruct(shape, pieces[0].dtype),
        compiler_params=params(28),
        cost_estimate=cost(1e8, 2e6),
        name="join",
    )(place[None].astype(jnp.int32), *pieces)


def swap_parts(parts, shift):
    return [send_xor(part, (flip + 1) << shift) for flip, part in enumerate(parts)]


def spread(part, shift, parts):
    return [send_xor(part, flip << shift) for flip in range(1, parts)]


def after(values, *others):
    return lax.optimization_barrier((values,) + others)[0]


def row_device(
    tokens, seg_lengths, ln1_gain, ln1_bias, w_qkv, b_qv, w_o, b_o, ln2_gain, ln2_bias,
    w_up, b_up, w_down, b_down, cotangent,
):
    row_count, slice_len, d = tokens.shape
    row = lax.axis_index("blk")
    me = lax.axis_index("rows") * lax.axis_size("blk") + row
    place_core = me & 1
    place_plane = (me >> 1) & 3
    place_deep = me >> 3
    core = place_core[None].astype(jnp.int32)
    blk = row[None].astype(jnp.int32)
    ends = jnp.cumsum(seg_lengths, axis=1)
    ends = lax.dynamic_index_in_dim(ends, row, 0, keepdims=False).astype(jnp.int32)

    def cut(values):
        return [lax.dynamic_index_in_dim(values, row ^ flip, 0, keepdims=False) for flip in range(row_count)]

    def swap(pieces):
        return [pieces[0]] + swap_parts(pieces[1:], 0)

    x = swap(cut(tokens))
    cot = cut(cotangent)
    cot = lax.optimization_barrier(tuple(cot) + tuple(x))[:row_count]
    cot = swap(list(cot))
    x, q, k, v, n1, att, lse = forward_call(ends, blk, x, ln1_gain, ln1_bias, w_qkv, b_qv)
    out, out_near, out_far, gmid, gatt, delta, keep, send, vec_mid = middle_call(
        core, blk, att, x, cot, w_o, b_o, ln2_gain, ln2_bias, w_up, b_up, w_down, b_down
    )
    own, *parts = add_call(place_plane, 4, [keep, send_xor(send, 1)], F32)
    grads = backward_call(after(ends, own), q, k, v, gatt, lse, delta, 0, d // LANES)
    own, *parts = add_call(after(place_deep, grads[0]), 4, [own] + swap_parts(parts, 1), F32)
    out_far = send_xor(after(out_far, own), 2)
    first = [own] + swap_parts(parts, 3)
    gin, gin_near, gin_far, keep, send = last_call(
        after(core, own), blk, grads, n1, x, gmid, ln1_gain, w_qkv, vec_mid
    )
    (first,) = add_call(0, 1, first, BF16)
    send, first, out_far = lax.optimization_barrier((send, first, out_far))
    first_z = spread(first, 3, 2)
    own, *parts = add_call(place_plane, 4, [keep, send_xor(send, 1)], F32)
    first = join_call(after(place_deep & 1, own), [first] + first_z)
    first_z = spread(first, 4, 2)
    second = swap_parts(parts, 1)
    out_near = send_xor(relay_call(after(out_near, own), out_far), 1)
    output = arrive_call(blk, out, out_near, out_far, BF16)
    own, *parts = add_call(after(place_deep, output), 4, [own] + second, F32)
    first = join_call(place_deep >> 1, [first] + first_z)
    first, gin_far = lax.optimization_barrier((first, gin_far, own))[:2]
    gin_far = send_xor(gin_far, 2)
    (second,) = add_call(0, 1, [own] + swap_parts(parts, 3), BF16)
    first = join_call(after(place_plane & 1, second), [first] + spread(first, 1, 2))
    second = join_call(after(place_deep, gin_far), [second] + spread(second, 3, 4))
    first = join_call(after(place_plane >> 1, second), [first] + spread(first, 2, 2))
    gin_near = send_xor(relay_call(after(gin_near, second), gin_far), 1)
    input_grad = arrive_call(blk, gin, gin_near, gin_far, F32)
    second = join_call(after(place_plane, input_grad), [second] + spread(second, 1, 4))
    gw_down, gw_up, gw_o = finish_call(
        finish_mid_kernel, core, first, send_xor(first, 1), [w_down.shape, w_up.shape, w_o.shape], "finish_mid"
    )
    gw_qkv, *vecs = finish_call(
        finish_last_kernel, after(core, gw_down), second, send_xor(second, 1),
        [w_qkv.shape] + [(1, size) for size in (d, 2 * d, d, d, d, d, d, 2 * d)], "finish_last",
    )
    vecs = [vec.reshape(-1) for vec in vecs]
    g_down_b, g_up_b, g_ln2_gain, g_ln2_bias, g_o_b, g_ln1_gain, g_ln1_bias, g_qv_b = vecs
    return (
        output, input_grad, g_ln1_gain, g_ln1_bias, gw_qkv, g_qv_b, gw_o, g_o_b, g_ln2_gain, g_ln2_bias,
        gw_up, g_up_b, gw_down, g_down_b,
    )


def layer_norm(values, gain_vec, bias_vec):
    average = jnp.mean(values, axis=-1, keepdims=True)
    centered = values - average
    variance = jnp.mean(centered * centered, axis=-1, keepdims=True)
    return centered * lax.rsqrt(variance + norm_eps) * gain_vec + bias_vec


def segment_of(cell_ends, positions):
    return jnp.sum((cell_ends[:, None, :] <= positions[None, :, None]).astype(jnp.int32), axis=-1)


def block_scores(query_heads, key_heads, query_pos, key_pos, query_seg, key_seg, scale_qk):
    raw_scores = (
        jnp.einsum("rqhd,rkhd->rqhk", query_heads, key_heads, preferred_element_type=jnp.float32)
        * scale_qk
    )
    causal = key_pos[None, :] <= query_pos[:, None]
    same_cell = query_seg[:, :, None] == key_seg[:, None, :]
    allowed = (causal[None] & same_cell)[:, :, None, :]
    return (jnp.where(allowed, raw_scores, neg_big), allowed)


def block_active(query_pos, key_pos, query_seg, key_seg):
    return (key_pos[0] <= query_pos[-1]) & jnp.any(key_seg[:, -1] >= query_seg[:, 0])


def backward_block(
    query_heads,
    grad_heads,
    log_total,
    delta_sum,
    key_heads,
    value_heads,
    query_pos,
    key_pos,
    query_seg,
    key_seg,
    scale_qk,
):
    scores, allowed = block_scores(
        query_heads, key_heads, query_pos, key_pos, query_seg, key_seg, scale_qk
    )
    softmaxed = jnp.where(allowed, jnp.exp(scores - log_total[..., None]), 0.0)
    grad_probs = jnp.einsum(
        "rqhd,rkhd->rqhk", grad_heads, value_heads, preferred_element_type=jnp.float32
    )
    grad_scores = (softmaxed * (grad_probs - delta_sum[..., None])).astype(jnp.bfloat16)
    grad_query = (
        jnp.einsum("rqhk,rkhd->rqhd", grad_scores, key_heads, preferred_element_type=jnp.float32)
        * scale_qk
    )
    grad_key = (
        jnp.einsum("rqhk,rqhd->rkhd", grad_scores, query_heads, preferred_element_type=jnp.float32)
        * scale_qk
    )
    grad_value = jnp.einsum(
        "rqhk,rqhd->rkhd",
        softmaxed.astype(jnp.bfloat16),
        grad_heads,
        preferred_element_type=jnp.float32,
    )
    return (grad_query, grad_key, grad_value)


def unchanged(old_state):
    return old_state


def general_device(
    tokens,
    seg_lengths,
    ln1_gain,
    ln1_bias,
    w_qkv,
    b_qv,
    w_o,
    b_o,
    ln2_gain,
    ln2_bias,
    w_up,
    b_up,
    w_down,
    b_down,
    cotangent,
):
    row_count, slice_len, width_all = tokens.shape
    head_size = width_all // HEADS
    scale_qk = head_size ** (-0.5)
    head_shape = (row_count, slice_len, HEADS, head_size)
    stat_shape = (row_count, slice_len, HEADS)
    full_length = lax.axis_size("blk") * slice_len
    offsets = jnp.arange(slice_len, dtype=jnp.int32)
    query_pos = lax.axis_index("blk") * slice_len + offsets
    cell_ends = jnp.cumsum(seg_lengths, axis=1)
    query_seg = segment_of(cell_ends, query_pos)

    def take_block(piece, block_index):
        return lax.dynamic_slice_in_dim(piece, block_index * slice_len, slice_len, 1).reshape(
            head_shape
        )

    inputs = tokens.astype(jnp.float32)
    normed_val, first_pull = jax.vjp(layer_norm, inputs, ln1_gain, ln1_bias)
    normed_one = normed_val.astype(jnp.bfloat16)
    projected = jnp.dot(normed_one, w_qkv, preferred_element_type=jnp.float32)
    query_b = (projected[..., :width_all] + b_qv[:width_all]).astype(jnp.bfloat16)
    key_b = projected[..., width_all : 2 * width_all].astype(jnp.bfloat16)
    value_b = (projected[..., 2 * width_all :] + b_qv[width_all:]).astype(jnp.bfloat16)
    query_heads = query_b.reshape(head_shape)
    start_state = (
        jnp.full(stat_shape, neg_big, jnp.float32),
        jnp.zeros(stat_shape, jnp.float32),
        jnp.zeros(head_shape, jnp.float32),
    )
    key_piece = lax.all_gather(key_b, "blk", axis=1, tiled=True)
    value_piece = lax.all_gather(value_b, "blk", axis=1, tiled=True)

    def forward_block_step(block_index, inner_state):
        key_pos = block_index * slice_len + offsets
        key_seg = segment_of(cell_ends, key_pos)
        key_heads = take_block(key_piece, block_index)
        value_heads = take_block(value_piece, block_index)

        def forward_update(old_state):
            running_top, running_total, running_sum = old_state
            scores, allowed = block_scores(
                query_heads, key_heads, query_pos, key_pos, query_seg, key_seg, scale_qk
            )
            new_top = jnp.maximum(running_top, jnp.max(scores, axis=-1))
            factor = jnp.exp(running_top - new_top)
            weights_now = jnp.where(allowed, jnp.exp(scores - new_top[..., None]), 0.0)
            new_total = running_total * factor + jnp.sum(weights_now, axis=-1)
            new_sum = running_sum * factor[..., None] + jnp.einsum(
                "rqhk,rkhd->rqhd",
                weights_now.astype(jnp.bfloat16),
                value_heads,
                preferred_element_type=jnp.float32,
            )
            return (new_top, new_total, new_sum)

        return lax.cond(
            block_active(query_pos, key_pos, query_seg, key_seg),
            forward_update,
            unchanged,
            inner_state,
        )

    running_top, running_total, running_sum = lax.fori_loop(
        0, key_piece.shape[1] // slice_len, forward_block_step, start_state
    )
    attn_f32 = (running_sum / running_total[..., None]).reshape(row_count, slice_len, width_all)
    log_total = running_top + jnp.log(running_total)
    attn_b = attn_f32.astype(jnp.bfloat16)
    middle = inputs + jnp.dot(attn_b, w_o, preferred_element_type=jnp.float32) + b_o
    normed_two_val, second_pull = jax.vjp(layer_norm, middle, ln2_gain, ln2_bias)
    normed_two = normed_two_val.astype(jnp.bfloat16)
    hidden_pre = jnp.dot(normed_two, w_up, preferred_element_type=jnp.float32) + b_up
    hidden_val, gelu_pull = jax.vjp(jax.nn.gelu, hidden_pre)
    hidden_b = hidden_val.astype(jnp.bfloat16)
    output = (
        middle + jnp.dot(hidden_b, w_down, preferred_element_type=jnp.float32) + b_down
    ).astype(jnp.bfloat16)
    grad_out = cotangent.astype(jnp.float32)
    grad_w_down = jnp.einsum("rcf,rcd->fd", hidden_b, cotangent, preferred_element_type=jnp.float32)
    grad_b_down = jnp.sum(grad_out, axis=(0, 1))
    grad_hidden = jnp.einsum("rcd,fd->rcf", cotangent, w_down, preferred_element_type=jnp.float32)
    (grad_pre,) = gelu_pull(grad_hidden)
    grad_pre_b = grad_pre.astype(jnp.bfloat16)
    grad_w_up = jnp.einsum(
        "rcd,rcf->df", normed_two, grad_pre_b, preferred_element_type=jnp.float32
    )
    grad_b_up = jnp.sum(grad_pre_b.astype(jnp.float32), axis=(0, 1))
    grad_normed_two = jnp.einsum(
        "rcf,df->rcd", grad_pre_b, w_up, preferred_element_type=jnp.float32
    )
    grad_mid_norm, grad_ln2_gain, grad_ln2_bias = second_pull(grad_normed_two)
    grad_middle = grad_out + grad_mid_norm
    grad_branch_b = grad_middle.astype(jnp.bfloat16)
    grad_w_o = jnp.einsum("rce,rcd->ed", attn_b, grad_branch_b, preferred_element_type=jnp.float32)
    grad_b_o = jnp.sum(grad_branch_b.astype(jnp.float32), axis=(0, 1))
    grad_attn_b = jnp.einsum(
        "rcd,ed->rce", grad_branch_b, w_o, preferred_element_type=jnp.float32
    ).astype(jnp.bfloat16)
    delta_sum = jnp.sum((grad_attn_b.astype(jnp.float32) * attn_f32).reshape(head_shape), axis=-1)
    grad_heads = grad_attn_b.reshape(head_shape)
    whole_shape = (row_count, full_length, HEADS, head_size)
    back_state = (
        jnp.zeros(head_shape, jnp.float32),
        jnp.zeros(whole_shape, jnp.float32),
        jnp.zeros(whole_shape, jnp.float32),
    )
    backward_key_piece = lax.all_gather(key_b, "blk", axis=1, tiled=True)
    backward_value_piece = lax.all_gather(value_b, "blk", axis=1, tiled=True)

    def backward_block_step(block_index, inner_state):
        key_pos = block_index * slice_len + offsets
        key_seg = segment_of(cell_ends, key_pos)
        key_heads = take_block(backward_key_piece, block_index)
        value_heads = take_block(backward_value_piece, block_index)

        def backward_update(old_state):
            grad_query, grad_key, grad_value = backward_block(
                query_heads,
                grad_heads,
                log_total,
                delta_sum,
                key_heads,
                value_heads,
                query_pos,
                key_pos,
                query_seg,
                key_seg,
                scale_qk,
            )
            at_row = block_index * slice_len
            return (
                old_state[0] + grad_query,
                lax.dynamic_update_slice_in_dim(old_state[1], grad_key, at_row, 1),
                lax.dynamic_update_slice_in_dim(old_state[2], grad_value, at_row, 1),
            )

        return lax.cond(
            block_active(query_pos, key_pos, query_seg, key_seg),
            backward_update,
            unchanged,
            inner_state,
        )

    back_result = lax.fori_loop(
        0, backward_key_piece.shape[1] // slice_len, backward_block_step, back_state
    )
    grad_query_sum = back_result[0]
    grad_key_sum, grad_value_sum = (
        lax.psum_scatter(
            back_result[1].astype(jnp.bfloat16), "blk", scatter_dimension=1, tiled=True
        ).astype(jnp.float32),
        lax.psum_scatter(
            back_result[2].astype(jnp.bfloat16), "blk", scatter_dimension=1, tiled=True
        ).astype(jnp.float32),
    )
    flat_shape = (row_count, slice_len, width_all)
    grad_qkv_b = jnp.concatenate(
        [
            grad_query_sum.reshape(flat_shape),
            grad_key_sum.reshape(flat_shape),
            grad_value_sum.reshape(flat_shape),
        ],
        axis=-1,
    ).astype(jnp.bfloat16)
    grad_w_qkv = jnp.einsum(
        "rcd,rce->de", normed_one, grad_qkv_b, preferred_element_type=jnp.float32
    )
    column_sums = jnp.sum(grad_qkv_b.astype(jnp.float32), axis=(0, 1))
    grad_b_qv = jnp.concatenate([column_sums[:width_all], column_sums[2 * width_all :]])
    grad_normed_one = jnp.einsum(
        "rce,de->rcd", grad_qkv_b, w_qkv, preferred_element_type=jnp.float32
    )
    grad_in_norm, grad_ln1_gain, grad_ln1_bias = first_pull(grad_normed_one)
    input_grad = grad_middle + grad_in_norm
    grads = (
        grad_ln1_gain,
        grad_ln1_bias,
        grad_w_qkv,
        grad_b_qv,
        grad_w_o,
        grad_b_o,
        grad_ln2_gain,
        grad_ln2_bias,
        grad_w_up,
        grad_b_up,
        grad_w_down,
        grad_b_down,
    )
    summed = lax.psum(
        (
            grads[0],
            grads[1],
            grads[2],
            grads[3],
            grads[4],
            grads[5],
            grads[6],
            grads[7],
            grads[8],
            grads[9],
            grads[10],
            grads[11],
        ),
        ("rows", "blk"),
    )
    return (
        output,
        input_grad,
        summed[0],
        summed[1],
        summed[2],
        summed[3],
        summed[4],
        summed[5],
        summed[6],
        summed[7],
        summed[8],
        summed[9],
        summed[10],
        summed[11],
    )


def device_function(tokens, *rest):
    d = tokens.shape[2]
    whole_rows = (
        lax.axis_size("blk") == tokens.shape[0] == 4
        and lax.axis_size("rows") == 8
        and tokens.shape[1] == TILE
        and d == 512
    )
    return (row_device if whole_rows else general_device)(tokens, *rest)


def solution(mesh):
    in_specs = (
        P("rows", "blk", None),
        P("rows", None),
        P(),
        P(),
        P(),
        P(),
        P(),
        P(),
        P(),
        P(),
        P(),
        P(),
        P(),
        P(),
        P("rows", "blk", None),
    )
    out_specs = (
        P("rows", "blk", None),
        P("rows", "blk", None),
        P(),
        P(),
        P(),
        P(),
        P(),
        P(),
        P(),
        P(),
        P(),
        P(),
        P(),
        P(),
    )
    return jax.shard_map(
        device_function, mesh=mesh, in_specs=in_specs, out_specs=out_specs, check_vma=False
    )
```

```python
import functools

import jax
import jax.numpy as jnp
from jax import lax
from jax.experimental import pallas as pl
from jax.experimental.pallas import tpu as pltpu
from jax.sharding import PartitionSpec as P

HEADS = 8
norm_eps = 1e-05
neg_big = -1e30
BOTH = ("rows", "blk")
F32 = jnp.float32
BF16 = jnp.bfloat16
TILE = 256
LANES = 128
MIB = 1024 * 1024
B_FLOPS = 1e9
L_FLOPS = 1e9
MID_TILE = 512
MID_MIB = 28
LAST_MIB = 26


def mm(lhs, rhs):
    return lax.dot_general(lhs, rhs, (((1,), (0,)), ((), ())), preferred_element_type=F32)


def mm_nt(lhs, rhs):
    return lax.dot_general(lhs, rhs, (((1,), (1,)), ((), ())), preferred_element_type=F32)


def mm_tn(lhs, rhs):
    return lax.dot_general(lhs, rhs, (((0,), (0,)), ((), ())), preferred_element_type=F32)


def cell_start(ends_ref, positions):
    start = jnp.zeros_like(positions)
    for c in range(ends_ref.shape[0]):
        start = jnp.where(ends_ref[c] <= positions, ends_ref[c], start)
    return start


def norm_parts(values):
    average = jnp.mean(values, axis=-1, keepdims=True)
    centered = values - average
    variance = jnp.mean(centered * centered, axis=-1, keepdims=True)
    scale = lax.rsqrt(variance + norm_eps)
    return centered * scale, scale


def norm_pull(e, n, scale, gain):
    f = e * gain
    return (
        f
        - jnp.mean(f, axis=-1, keepdims=True)
        - n * jnp.mean(f * n, axis=-1, keepdims=True)
    ) * scale


def head_lanes(shape, half):
    lane = lax.broadcasted_iota(jnp.int32, shape, len(shape) - 1)
    return (lane < LANES // 2) if half == 0 else (lane >= LANES // 2)


def only_head(values, half):
    return jnp.where(head_lanes(values.shape, half), values, jnp.zeros_like(values))


def in_order(blk_ref, pieces, whole_ref):
    size = pieces[0].shape[0]
    for flip, piece_ref in enumerate(pieces):
        at = jnp.bitwise_xor(blk_ref[0], flip) * size
        whole_ref[pl.ds(pl.multiple_of(at, size), size), :] = piece_ref[...]


def forward_kernel(
    ends_ref, blk_ref, x0_ref, x1_ref, x2_ref, x3_ref, gain_ref, bias_ref, w_ref, b_ref,
    x_ref, q_ref, k_ref, v_ref, n1_ref, att_ref, lse_ref,
    mask_ref,
):
    in_order(blk_ref, (x0_ref, x1_ref, x2_ref, x3_ref), x_ref)
    t, width = x_ref.shape
    pairs = width // LANES
    scale_qk = (width // HEADS) ** (-0.5)
    for low in range(0, t, 512):
        rows = slice(low, low + 512)
        n, _ = norm_parts(x_ref[rows].astype(F32))
        n1 = (n * gain_ref[...] + bias_ref[...]).astype(BF16)
        n1_ref[rows] = n1
        q = mm(n1, w_ref[:, :width]) + b_ref[:, :width]
        q = (q.astype(BF16).astype(F32) * scale_qk).astype(BF16)
        k = mm(n1, w_ref[:, width : 2 * width]).astype(BF16)
        v = (mm(n1, w_ref[:, 2 * width :]) + b_ref[:, width:]).astype(BF16)
        for g in range(pairs):
            cols = slice(g * LANES, (g + 1) * LANES)
            q_ref[g, rows, :] = q[:, cols]
            k_ref[g, rows, :] = k[:, cols]
            v_ref[g, rows, :] = v[:, cols]
    for low in range(0, t, TILE):
        reach = low + TILE
        rows = slice(low, reach)
        q_pos = low + lax.broadcasted_iota(jnp.int32, (TILE, 1), 0)
        k_pos = lax.broadcasted_iota(jnp.int32, (TILE, reach), 1)
        start = cell_start(ends_ref, q_pos)
        mask_ref[:, :reach] = jnp.where((k_pos <= q_pos) & (k_pos >= start), 0.0, neg_big)
        lse_all = jnp.zeros((TILE, LANES), F32)
        lane = lax.broadcasted_iota(jnp.int32, lse_all.shape, 1)
        for g in range(pairs):
            qp = q_ref[g, rows, :]
            kp = k_ref[g, :reach, :]
            vp = v_ref[g, :reach, :]
            outs = []
            for half in range(2):
                s = mm_nt(only_head(qp, half), kp) + mask_ref[:, :reach]
                top = jnp.max(s, axis=-1, keepdims=True)
                p = jnp.exp(s - top)
                total = jnp.sum(p, axis=-1, keepdims=True)
                outs.append(mm(p.astype(BF16), vp) / total)
                lse_all = jnp.where(lane == 2 * g + half, top + jnp.log(total), lse_all)
            att_ref[g, rows, :] = jnp.where(head_lanes(outs[0].shape, 0), outs[0], outs[1])
        lse_ref[:, rows] = jnp.transpose(lse_all)[:HEADS]


def whole(shape):
    return pl.BlockSpec(shape, lambda i: (0,) * len(shape))


def by_row(cols, tile=TILE):
    return pl.BlockSpec((tile, cols), lambda i: (i, 0))


def by_pair(pairs, tile=TILE):
    return pl.BlockSpec((pairs, tile, LANES), lambda i: (0, i, 0))


def heads_row(tile=TILE):
    return pl.BlockSpec((HEADS, tile), lambda i: (0, i))


SMEM_SPEC = pl.BlockSpec(memory_space=pltpu.SMEM)


def in_hbm(*arrays):
    return [pltpu.with_memory_space_constraint(a, pltpu.HBM) for a in arrays]


def params(mib):
    return pltpu.CompilerParams(dimension_semantics=("arbitrary",), vmem_limit_bytes=mib * MIB)


def cost(flops, moved):
    return pl.CostEstimate(flops=int(flops), bytes_accessed=int(moved), transcendentals=0)


def forward_call(ends, blk, pieces, gain, bias, w_qkv, b_qv):
    size, d = pieces[0].shape
    t = size * len(pieces)
    pairs = d // LANES
    return pl.pallas_call(
        forward_kernel,
        grid=(1,),
        in_specs=[SMEM_SPEC, SMEM_SPEC]
        + [whole((size, d))] * len(pieces)
        + [whole((1, d)), whole((1, d)), whole(w_qkv.shape), whole((1, 2 * d))],
        out_specs=[
            whole((t, d)), whole((pairs, t, LANES)), whole((pairs, t, LANES)), whole((pairs, t, LANES)), whole((t, d)),
            whole((pairs, t, LANES)), whole((HEADS, t)),
        ],
        out_shape=[
            jax.ShapeDtypeStruct((t, d), BF16),
            pltpu.HBM((pairs, t, LANES), BF16),
            pltpu.HBM((pairs, t, LANES), BF16),
            pltpu.HBM((pairs, t, LANES), BF16),
            pltpu.HBM((t, d), BF16),
            jax.ShapeDtypeStruct((pairs, t, LANES), F32),
            jax.ShapeDtypeStruct((HEADS, t), F32),
        ],
        scratch_shapes=[pltpu.VMEM((TILE, t), F32)],
        compiler_params=params(34),
        cost_estimate=cost(20e9, 10e6),
        name="forward",
    )(ends, blk, *pieces, gain[None], bias[None], w_qkv, b_qv[None])


def leave(blk_ref, whole_ref, own_ref, near_ref, far_ref):
    size = own_ref.shape[0]
    for flip, dest in ((0, own_ref), (1, near_ref), (2, far_ref.at[:size]), (3, far_ref.at[size:])):
        at = jnp.bitwise_xor(blk_ref[0], flip) * size
        dest[...] = whole_ref[pl.ds(pl.multiple_of(at, size), size), :]


def relay_kernel(near_ref, far_ref, out_ref):
    size = near_ref.shape[0]
    out_ref[:size] = near_ref[...]
    out_ref[size:] = far_ref[size:]


def relay_call(near, far):
    return pl.pallas_call(
        relay_kernel,
        grid=(1,),
        in_specs=[whole(near.shape), whole(far.shape)],
        out_specs=whole(far.shape),
        out_shape=jax.ShapeDtypeStruct(far.shape, far.dtype),
        compiler_params=params(8),
        cost_estimate=cost(1e7, 1e5),
        name="relay",
    )(near, far)


def arrive_kernel(blk_ref, own_ref, near_ref, far_ref, out_ref):
    size = own_ref.shape[0]
    pieces = (own_ref[...], near_ref[:size], far_ref[:size], near_ref[size:])
    for flip, piece in enumerate(pieces):
        out_ref[jnp.bitwise_xor(blk_ref[0], flip)] = piece.astype(out_ref.dtype)


def arrive_call(blk, own, near, far, dtype):
    shape = (4,) + own.shape
    return pl.pallas_call(
        arrive_kernel,
        grid=(1,),
        in_specs=[SMEM_SPEC, whole(own.shape), whole(near.shape), whole(far.shape)],
        out_specs=whole(shape),
        out_shape=jax.ShapeDtypeStruct(shape, dtype),
        compiler_params=params(12),
        cost_estimate=cost(1e7, 1e5),
        name="arrive",
    )(blk, own, near, far)


def split_halves(core_ref, whole_ref, keep_ref, send_ref):
    half = keep_ref.shape[0]
    core = core_ref[0]
    keep_ref[...] = whole_ref[pl.ds(pl.multiple_of(core * half, half), half), :]
    send_ref[...] = whole_ref[pl.ds(pl.multiple_of((1 - core) * half, half), half), :].astype(BF16)


def middle_kernel(
    core_ref, blk_ref, att_ref, x_ref, c0_ref, c1_ref, c2_ref, c3_ref, wo_ref, bo_ref, gain_ref, bias_ref, wup_ref, bup_ref, wdown_ref, bdown_ref,
    o0_ref, o1_ref, o2_ref, gmid_ref, gatt_ref, delta_ref, keep_ref, send_ref, vec_ref,
    cot_ref, out_ref, gw_ref, hidden_ref, gpre_ref, n2_ref, attb_ref, gbr_ref,
):
    pairs = att_ref.shape[0]
    t, d = x_ref.shape
    ff = wup_ref.shape[-1]
    c0 = 0.7978845608028654
    c1 = 0.044715

    def col(values):
        return jnp.sum(values, axis=0, keepdims=True)

    in_order(blk_ref, (c0_ref, c1_ref, c2_ref, c3_ref), cot_ref)
    vec_ref[...] = jnp.zeros_like(vec_ref)
    head = lax.broadcasted_iota(jnp.int32, (HEADS, d), 0)
    lane = lax.broadcasted_iota(jnp.int32, (HEADS, d), 1)
    ones = jnp.where(lane // (d // HEADS) == head, 1.0, 0.0).astype(BF16)
    def tile(step, carry):
        rows = pl.ds(pl.multiple_of(step * MID_TILE, MID_TILE), MID_TILE)
        att = jnp.concatenate([att_ref[g, rows, :] for g in range(pairs)], axis=-1)
        att_b = att.astype(BF16)
        attb_ref[rows, :] = att_b
        middle = x_ref[rows, :].astype(F32) + mm(att_b, wo_ref[...]) + bo_ref[...]
        n, scale = norm_parts(middle)
        n2 = (n * gain_ref[...] + bias_ref[...]).astype(BF16)
        n2_ref[rows, :] = n2
        pre = mm(n2, wup_ref[...]) + bup_ref[...]
        sq = pre * pre
        th = jnp.tanh(c0 * (pre + c1 * (sq * pre)))
        half_one = 0.5 * (1.0 + th)
        hidden = (pre * half_one).astype(BF16)
        hidden_ref[rows, :] = hidden
        slope = half_one + (0.5 * pre) * (1.0 - th * th) * (c0 + (3.0 * c0 * c1) * sq)
        out_ref[rows, :] = (middle + mm(hidden, wdown_ref[...]) + bdown_ref[...]).astype(BF16)
        cot = cot_ref[rows, :]
        cot_f = cot.astype(F32)
        gpre = (mm_nt(cot, wdown_ref[...]) * slope).astype(BF16)
        gpre_ref[rows, :] = gpre
        e = mm_nt(gpre, wup_ref[...])
        gmid = cot_f + norm_pull(e, n, scale, gain_ref[...])
        gmid_ref[rows, :] = gmid
        gbr = gmid.astype(BF16)
        gbr_ref[rows, :] = gbr
        gatt = mm_nt(gbr, wo_ref[...]).astype(BF16)
        for g in range(pairs):
            gatt_ref[g, rows, :] = gatt[:, g * LANES : (g + 1) * LANES]
        prod = gatt.astype(F32) * att
        hi = prod.astype(BF16)
        lo = (prod - hi.astype(F32)).astype(BF16)
        delta_ref[:, rows] = mm_nt(ones, hi) + mm_nt(ones, lo)
        gsum = col(gpre.astype(F32))
        vec_ref[0:1] += col(cot_f)
        vec_ref[1:2] += gsum[:, :d]
        vec_ref[2:3] += gsum[:, d:]
        vec_ref[3:4] += col(e * n)
        vec_ref[4:5] += col(e)
        vec_ref[5:6] += col(gbr.astype(F32))
        return carry

    lax.fori_loop(0, t // MID_TILE, tile, 0)
    leave(blk_ref, out_ref, o0_ref, o1_ref, o2_ref)
    gw_ref[:ff] = mm_tn(hidden_ref[...], cot_ref[...])
    gw_ref[ff : ff + d] = mm_tn(n2_ref[...], gpre_ref[:, :d])
    gw_ref[ff + d : ff + 2 * d] = mm_tn(n2_ref[...], gpre_ref[:, d:])
    gw_ref[ff + 2 * d :] = mm_tn(attb_ref[...], gbr_ref[...])
    split_halves(core_ref, gw_ref, keep_ref, send_ref)


def middle_call(core, blk, att, x, cots, w_o, b_o, gain, bias, w_up, b_up, w_down, b_down):
    t, d = x.shape
    pairs = d // LANES
    ff = w_up.shape[1]
    half = (ff + 3 * d) // 2
    return pl.pallas_call(
        middle_kernel,
        grid=(1,),
        in_specs=[
            SMEM_SPEC, SMEM_SPEC,
            by_pair(pairs, t), by_row(d, t), *[whole(c.shape) for c in cots], whole((d, d)), whole((1, d)), whole((1, d)), whole((1, d)),
            whole((d, ff)), whole((1, ff)), whole((ff, d)), whole((1, d)),
        ],
        out_specs=[
            whole((t // 4, d)), whole((t // 4, d)), whole((t // 2, d)), by_row(d, t), by_pair(pairs, t), heads_row(t), whole((half, d)), whole((half, d)),
            whole((8, d)),
        ],
        out_shape=[
            pltpu.HBM((t // 4, d), BF16),
            pltpu.HBM((t // 4, d), BF16),
            pltpu.HBM((t // 2, d), BF16),
            pltpu.HBM((t, d), F32),
            pltpu.HBM((pairs, t, LANES), BF16),
            jax.ShapeDtypeStruct((HEADS, t), F32),
            jax.ShapeDtypeStruct((half, d), F32),
            jax.ShapeDtypeStruct((half, d), BF16),
            jax.ShapeDtypeStruct((8, d), F32),
        ],
        scratch_shapes=[
            pltpu.VMEM((t, d), BF16),
            pltpu.VMEM((t, d), BF16),
            pltpu.VMEM((2 * half, d), F32),
            pltpu.VMEM((t, ff), BF16),
            pltpu.VMEM((t, ff), BF16),
            pltpu.VMEM((t, d), BF16),
            pltpu.VMEM((t, d), BF16),
            pltpu.VMEM((t, d), BF16),
        ],
        compiler_params=params(30),
        cost_estimate=cost(15e9, 20e6),
        name="middle",
    )(core, blk, att, x, *cots, w_o, b_o[None], gain[None], bias[None], w_up, b_up[None], w_down, b_down[None])


def backward_kernel(first, ends_ref, q_ref, k_ref, v_ref, g_ref, lse_ref, delta_ref, dq_ref, dk_ref, dv_ref, acc_ref):
    pair = pl.program_id(0) + first
    t = q_ref.shape[1]
    scale_qk = (LANES // 2) ** (-0.5)
    pos_row = lax.broadcasted_iota(jnp.int32, (1, t), 1)
    start_row = cell_start(ends_ref, pos_row)
    acc_ref[...] = jnp.zeros_like(acc_ref)
    jobs = [(j, half) for j in range(t // TILE) for half in range(2)]
    lses = [lse_ref[pl.ds(2 * pair + half, 1), :] for half in range(2)]
    deltas = [delta_ref[pl.ds(2 * pair + half, 1), :] for half in range(2)]
    kts = {}
    outs = {}

    def scores(job):
        j, half = job
        low = j * TILE
        km = only_head(k_ref[0, low : low + TILE, :], half)
        vm = only_head(v_ref[0, low : low + TILE, :], half)
        return mm_nt(km, q_ref[0, low:, :]), mm_nt(vm, g_ref[0, low:, :])

    def rest(job, s, dp):
        j, half = job
        low = j * TILE
        k_pos = low + lax.broadcasted_iota(jnp.int32, (TILE, t - low), 0)
        high = low + TILE
        diag = (k_pos[:, :TILE] >= start_row[:, low:high]) & (k_pos[:, :TILE] <= pos_row[:, low:high])
        p = jnp.exp(jnp.where(diag, s[:, :TILE] - lses[half][:, low:high], neg_big))
        if high < t:
            far = k_pos[:, TILE:] >= start_row[:, high:]
            p = jnp.concatenate([p, jnp.exp(jnp.where(far, s[:, TILE:] - lses[half][:, high:], neg_big))], axis=1)
        ds = (p * (dp - deltas[half][:, low:])).astype(BF16)
        dv = mm(p.astype(BF16), g_ref[0, low:, :])
        dk = mm(ds, q_ref[0, low:, :])
        kt = jnp.transpose(k_ref[0, low : low + TILE, :])
        rows = slice(half * 64, half * 64 + 64)
        acc_ref[rows, low:] += mm(kt[rows], ds)
        if half == 0:
            outs[j] = (dk, dv)
        else:
            first_lanes = head_lanes(dk.shape, 0)
            dk_ref[0, low : low + TILE, :] = jnp.where(first_lanes, outs[j][0], dk).astype(BF16)
            dv_ref[0, low : low + TILE, :] = jnp.where(first_lanes, outs[j][1], dv).astype(BF16)

    ready = scores(jobs[0])
    for at, job in enumerate(jobs):
        now = ready
        if at + 1 < len(jobs):
            ready = scores(jobs[at + 1])
        rest(job, *now)
    dq_ref[0] = jnp.transpose((acc_ref[...] * scale_qk)).astype(BF16)


def backward_call(ends, q, k, v, gatt, lse, delta, first, count):
    pairs, t, _ = q.shape
    spec = pl.BlockSpec((1, t, LANES), lambda i: (i + first, 0, 0))
    out = pl.BlockSpec((1, t, LANES), lambda i: (i, 0, 0))
    return pl.pallas_call(
        functools.partial(backward_kernel, first),
        grid=(count,),
        in_specs=[SMEM_SPEC, spec, spec, spec, spec, whole((HEADS, t)), whole((HEADS, t))],
        out_specs=[out, out, out],
        out_shape=[pltpu.HBM((count, t, LANES), BF16)] * 3,
        scratch_shapes=[pltpu.VMEM((LANES, t), F32)],
        compiler_params=params(28),
        cost_estimate=cost(count * B_FLOPS, count * 1e5),
        name="backward",
    )(ends, *in_hbm(q, k, v, gatt), lse, delta)


VEC_ROWS = 128


def last_kernel(*refs):
    core_ref, blk_ref = refs[:2]
    grads = refs[2:5]
    n1_ref, x_ref, gmid_ref, gain_ref, w_ref, vecmid_ref = refs[5:11]
    g0_ref, g1_ref, g2_ref, keep_ref, send_ref, gw_ref, gin_ref = refs[11:]
    pairs = grads[0].shape[0]
    d = x_ref.shape[-1]
    half = keep_ref.shape[0]
    gqkv = jnp.concatenate([grads[part][g] for part in range(3) for g in range(pairs)], axis=-1)
    gw = mm_tn(n1_ref[...], gqkv)
    blocks = 3 * pairs
    for p in range(blocks):
        at = (p // (blocks // 2)) * half + (p % (blocks // 2)) * d
        gw_ref[at : at + d] = gw[:, p * LANES : (p + 1) * LANES]
    e = mm_nt(gqkv, w_ref[...])
    n, scale = norm_parts(x_ref[...].astype(F32))
    gin_ref[...] = (gmid_ref[...] + norm_pull(e, n, scale, gain_ref[...])).astype(BF16)
    leave(blk_ref, gin_ref, g0_ref, g1_ref, g2_ref)

    def col(values):
        return jnp.sum(values, axis=0, keepdims=True)

    rows = [vecmid_ref[r : r + 1] for r in range(6)]
    rows += [col(e * n), col(e), col(gqkv[:, :d].astype(F32)), col(gqkv[:, 2 * d :].astype(F32))]
    base = half - VEC_ROWS
    gw_ref[base:half] = jnp.zeros((VEC_ROWS, LANES), F32)
    gw_ref[half + base :] = jnp.zeros((VEC_ROWS, LANES), F32)
    for r, row in enumerate(rows):
        for g in range(d // LANES):
            at = base + r * (d // LANES) + g
            gw_ref[at : at + 1] = row[:, g * LANES : (g + 1) * LANES]
    split_halves(core_ref, gw_ref, keep_ref, send_ref)


def last_call(core, blk, grads, n1, x, gmid, gain, w_qkv, vec_mid):
    t, d = x.shape
    half = 3 * d * d // LANES // 2 + VEC_ROWS
    return pl.pallas_call(
        last_kernel,
        grid=(1,),
        in_specs=[SMEM_SPEC, SMEM_SPEC]
        + [whole(a.shape) for a in grads]
        + [by_row(d, t), by_row(d, t), by_row(d, t), whole((1, d)), whole(w_qkv.shape), whole((8, d))],
        out_specs=[whole((t // 4, d)), whole((t // 4, d)), whole((t // 2, d)), whole((half, LANES)), whole((half, LANES))],
        out_shape=[
            pltpu.HBM((t // 4, d), BF16),
            pltpu.HBM((t // 4, d), BF16),
            pltpu.HBM((t // 2, d), BF16),
            jax.ShapeDtypeStruct((half, LANES), F32),
            jax.ShapeDtypeStruct((half, LANES), BF16),
        ],
        scratch_shapes=[pltpu.VMEM((2 * half, LANES), F32), pltpu.VMEM((t, d), BF16)],
        compiler_params=params(28),
        cost_estimate=cost(L_FLOPS, 1e5),
        name="last",
    )(core, blk, *in_hbm(*grads), n1, x, gmid, gain[None], w_qkv, vec_mid)


def ordered_halves(core_ref, own_ref, got_ref, write):
    pl.when(core_ref[0] == 0)(functools.partial(write, own_ref, got_ref))
    pl.when(core_ref[0] == 1)(functools.partial(write, got_ref, own_ref))


def finish_mid_kernel(core_ref, own_ref, got_ref, down_ref, up_ref, wo_ref):
    ff, d = down_ref.shape
    half = own_ref.shape[0]

    def write(low_ref, high_ref):
        def take(first, last):
            if last <= half:
                return low_ref[first:last].astype(F32)
            if first >= half:
                return high_ref[first - half : last - half].astype(F32)
            return jnp.concatenate([take(first, half), take(half, last)], axis=0)

        down_ref[...] = take(0, ff)
        up_ref[:, :d] = take(ff, ff + d)
        up_ref[:, d:] = take(ff + d, ff + 2 * d)
        wo_ref[...] = take(ff + 2 * d, ff + 3 * d)

    ordered_halves(core_ref, own_ref, got_ref, write)


def finish_last_kernel(core_ref, own_ref, got_ref, qkv_ref, *vec_refs):
    d = qkv_ref.shape[0]
    half = own_ref.shape[0]
    blocks = qkv_ref.shape[1] // LANES

    def write(low_ref, high_ref):
        for p in range(blocks):
            ref = (low_ref, high_ref)[p // (blocks // 2)]
            at = (p % (blocks // 2)) * d
            qkv_ref[:, p * LANES : (p + 1) * LANES] = ref[at : at + d].astype(F32)
        at = half - VEC_ROWS
        for ref in vec_refs:
            for g in range(ref.shape[1] // LANES):
                ref[:, g * LANES : (g + 1) * LANES] = low_ref[at : at + 1].astype(F32)
                at += 1

    ordered_halves(core_ref, own_ref, got_ref, write)


def finish_call(kernel, core, own, got, shapes, name):
    return pl.pallas_call(
        kernel,
        grid=(1,),
        in_specs=[SMEM_SPEC, whole(own.shape), whole(got.shape)],
        out_specs=[whole(shape) for shape in shapes],
        out_shape=[jax.ShapeDtypeStruct(shape, F32) for shape in shapes],
        compiler_params=params(28),
        cost_estimate=cost(1e8, 8e6),
        name=name,
    )(core, own, got)


def send_xor(values, flip):
    count = lax.axis_size(BOTH)
    return lax.ppermute(values, BOTH, [(i, i ^ flip) for i in range(count)])


def add_kernel(place_ref, *refs):
    outs = place_ref.shape[0]
    terms, results = refs[:-outs], refs[-outs:]
    size = results[0].shape[0]
    for flip, result in enumerate(results):
        rows = pl.ds(pl.multiple_of(jnp.bitwise_xor(place_ref[0], flip) * size, size), size)
        total = terms[0][rows, :].astype(F32)
        for term in terms[1:]:
            total = total + term[rows, :].astype(F32)
        result[...] = total.astype(result.dtype)


def add_call(place, parts, terms, own_dtype):
    rows, lanes = terms[0].shape
    shape = (rows // parts, lanes)
    places = jnp.broadcast_to(place, (parts,)).astype(jnp.int32)
    return pl.pallas_call(
        add_kernel,
        grid=(1,),
        in_specs=[SMEM_SPEC] + [whole(a.shape) for a in terms],
        out_specs=[whole(shape)] * parts,
        out_shape=[jax.ShapeDtypeStruct(shape, own_dtype if p == 0 else BF16) for p in range(parts)],
        compiler_params=params(28),
        cost_estimate=cost(1e8, 4e6),
        name="add",
    )(places, *terms)


def join_kernel(place_ref, *refs):
    out_ref = refs[-1]
    for flip, ref in enumerate(refs[:-1]):
        size = ref.shape[0]
        rows = pl.ds(pl.multiple_of(jnp.bitwise_xor(place_ref[0], flip) * size, size), size)
        out_ref[rows, :] = ref[...]


def join_call(place, pieces):
    rows, lanes = pieces[0].shape
    shape = (rows * len(pieces), lanes)
    return pl.pallas_call(
        join_kernel,
        grid=(1,),
        in_specs=[SMEM_SPEC] + [whole(p.shape) for p in pieces],
        out_specs=whole(shape),
        out_shape=jax.ShapeDtypeStruct(shape, pieces[0].dtype),
        compiler_params=params(28),
        cost_estimate=cost(1e8, 2e6),
        name="join",
    )(place[None].astype(jnp.int32), *pieces)


def swap_parts(parts, shift):
    return [send_xor(part, (flip + 1) << shift) for flip, part in enumerate(parts)]


def spread(part, shift, parts):
    return [send_xor(part, flip << shift) for flip in range(1, parts)]


def after(values, *others):
    return lax.optimization_barrier((values,) + others)[0]


def row_device(
    tokens, seg_lengths, ln1_gain, ln1_bias, w_qkv, b_qv, w_o, b_o, ln2_gain, ln2_bias,
    w_up, b_up, w_down, b_down, cotangent,
):
    row_count, slice_len, d = tokens.shape
    row = lax.axis_index("blk")
    me = lax.axis_index("rows") * lax.axis_size("blk") + row
    place_core = me & 1
    place_plane = (me >> 1) & 3
    place_deep = me >> 3
    core = place_core[None].astype(jnp.int32)
    blk = row[None].astype(jnp.int32)
    ends = jnp.cumsum(seg_lengths, axis=1)
    ends = lax.dynamic_index_in_dim(ends, row, 0, keepdims=False).astype(jnp.int32)

    def cut(values):
        return [lax.dynamic_index_in_dim(values, row ^ flip, 0, keepdims=False) for flip in range(row_count)]

    def swap(pieces):
        return [pieces[0]] + swap_parts(pieces[1:], 0)

    x = swap(cut(tokens))
    cot = cut(cotangent)
    cot = lax.optimization_barrier(tuple(cot) + tuple(x))[:row_count]
    cot = swap(list(cot))
    x, q, k, v, n1, att, lse = forward_call(ends, blk, x, ln1_gain, ln1_bias, w_qkv, b_qv)
    out, out_near, out_far, gmid, gatt, delta, keep, send, vec_mid = middle_call(
        core, blk, att, x, cot, w_o, b_o, ln2_gain, ln2_bias, w_up, b_up, w_down, b_down
    )
    own, *parts = add_call(place_plane, 4, [keep, send_xor(send, 1)], F32)
    grads = backward_call(after(ends, own), q, k, v, gatt, lse, delta, 0, d // LANES)
    own, *parts = add_call(after(place_deep, grads[0]), 4, [own] + swap_parts(parts, 1), F32)
    out_far = send_xor(after(out_far, own), 2)
    first = [own] + swap_parts(parts, 3)
    gin, gin_near, gin_far, keep, send = last_call(
        after(core, own), blk, grads, n1, x, gmid, ln1_gain, w_qkv, vec_mid
    )
    (first,) = add_call(0, 1, first, BF16)
    send, first, out_far = lax.optimization_barrier((send, first, out_far))
    first_z = spread(first, 3, 2)
    own, *parts = add_call(place_plane, 4, [keep, send_xor(send, 1)], F32)
    first = join_call(after(place_deep & 1, own), [first] + first_z)
    first_z = spread(first, 4, 2)
    second = swap_parts(parts, 1)
    own, *parts = add_call(place_deep, 4, [own] + second, F32)
    out_near = send_xor(relay_call(after(out_near, own), out_far), 1)
    first = join_call(place_deep >> 1, [first] + first_z)
    first, gin_far = lax.optimization_barrier((first, gin_far, own))[:2]
    gin_far = send_xor(gin_far, 2)
    (second,) = add_call(0, 1, [own] + swap_parts(parts, 3), BF16)
    first = join_call(after(place_plane & 1, second), [first] + spread(first, 1, 2))
    second = join_call(place_deep, [second] + spread(second, 3, 4))
    first = join_call(after(place_plane >> 1, second), [first] + spread(first, 2, 2))
    gin_near = send_xor(relay_call(after(gin_near, second), gin_far), 1)
    output = arrive_call(after(blk, second), out, out_near, out_far, BF16)
    input_grad = arrive_call(blk, gin, gin_near, gin_far, F32)
    second = join_call(after(place_plane, output, input_grad), [second] + spread(second, 1, 4))
    gw_down, gw_up, gw_o = finish_call(
        finish_mid_kernel, core, first, send_xor(first, 1), [w_down.shape, w_up.shape, w_o.shape], "finish_mid"
    )
    gw_qkv, *vecs = finish_call(
        finish_last_kernel, after(core, gw_down), second, send_xor(second, 1),
        [w_qkv.shape] + [(1, size) for size in (d, 2 * d, d, d, d, d, d, 2 * d)], "finish_last",
    )
    vecs = [vec.reshape(-1) for vec in vecs]
    g_down_b, g_up_b, g_ln2_gain, g_ln2_bias, g_o_b, g_ln1_gain, g_ln1_bias, g_qv_b = vecs
    return (
        output, input_grad, g_ln1_gain, g_ln1_bias, gw_qkv, g_qv_b, gw_o, g_o_b, g_ln2_gain, g_ln2_bias,
        gw_up, g_up_b, gw_down, g_down_b,
    )


def layer_norm(values, gain_vec, bias_vec):
    average = jnp.mean(values, axis=-1, keepdims=True)
    centered = values - average
    variance = jnp.mean(centered * centered, axis=-1, keepdims=True)
    return centered * lax.rsqrt(variance + norm_eps) * gain_vec + bias_vec


def segment_of(cell_ends, positions):
    return jnp.sum((cell_ends[:, None, :] <= positions[None, :, None]).astype(jnp.int32), axis=-1)


def block_scores(query_heads, key_heads, query_pos, key_pos, query_seg, key_seg, scale_qk):
    raw_scores = (
        jnp.einsum("rqhd,rkhd->rqhk", query_heads, key_heads, preferred_element_type=jnp.float32)
        * scale_qk
    )
    causal = key_pos[None, :] <= query_pos[:, None]
    same_cell = query_seg[:, :, None] == key_seg[:, None, :]
    allowed = (causal[None] & same_cell)[:, :, None, :]
    return (jnp.where(allowed, raw_scores, neg_big), allowed)


def block_active(query_pos, key_pos, query_seg, key_seg):
    return (key_pos[0] <= query_pos[-1]) & jnp.any(key_seg[:, -1] >= query_seg[:, 0])


def backward_block(
    query_heads,
    grad_heads,
    log_total,
    delta_sum,
    key_heads,
    value_heads,
    query_pos,
    key_pos,
    query_seg,
    key_seg,
    scale_qk,
):
    scores, allowed = block_scores(
        query_heads, key_heads, query_pos, key_pos, query_seg, key_seg, scale_qk
    )
    softmaxed = jnp.where(allowed, jnp.exp(scores - log_total[..., None]), 0.0)
    grad_probs = jnp.einsum(
        "rqhd,rkhd->rqhk", grad_heads, value_heads, preferred_element_type=jnp.float32
    )
    grad_scores = (softmaxed * (grad_probs - delta_sum[..., None])).astype(jnp.bfloat16)
    grad_query = (
        jnp.einsum("rqhk,rkhd->rqhd", grad_scores, key_heads, preferred_element_type=jnp.float32)
        * scale_qk
    )
    grad_key = (
        jnp.einsum("rqhk,rqhd->rkhd", grad_scores, query_heads, preferred_element_type=jnp.float32)
        * scale_qk
    )
    grad_value = jnp.einsum(
        "rqhk,rqhd->rkhd",
        softmaxed.astype(jnp.bfloat16),
        grad_heads,
        preferred_element_type=jnp.float32,
    )
    return (grad_query, grad_key, grad_value)


def unchanged(old_state):
    return old_state


def general_device(
    tokens,
    seg_lengths,
    ln1_gain,
    ln1_bias,
    w_qkv,
    b_qv,
    w_o,
    b_o,
    ln2_gain,
    ln2_bias,
    w_up,
    b_up,
    w_down,
    b_down,
    cotangent,
):
    row_count, slice_len, width_all = tokens.shape
    head_size = width_all // HEADS
    scale_qk = head_size ** (-0.5)
    head_shape = (row_count, slice_len, HEADS, head_size)
    stat_shape = (row_count, slice_len, HEADS)
    full_length = lax.axis_size("blk") * slice_len
    offsets = jnp.arange(slice_len, dtype=jnp.int32)
    query_pos = lax.axis_index("blk") * slice_len + offsets
    cell_ends = jnp.cumsum(seg_lengths, axis=1)
    query_seg = segment_of(cell_ends, query_pos)

    def take_block(piece, block_index):
        return lax.dynamic_slice_in_dim(piece, block_index * slice_len, slice_len, 1).reshape(
            head_shape
        )

    inputs = tokens.astype(jnp.float32)
    normed_val, first_pull = jax.vjp(layer_norm, inputs, ln1_gain, ln1_bias)
    normed_one = normed_val.astype(jnp.bfloat16)
    projected = jnp.dot(normed_one, w_qkv, preferred_element_type=jnp.float32)
    query_b = (projected[..., :width_all] + b_qv[:width_all]).astype(jnp.bfloat16)
    key_b = projected[..., width_all : 2 * width_all].astype(jnp.bfloat16)
    value_b = (projected[..., 2 * width_all :] + b_qv[width_all:]).astype(jnp.bfloat16)
    query_heads = query_b.reshape(head_shape)
    start_state = (
        jnp.full(stat_shape, neg_big, jnp.float32),
        jnp.zeros(stat_shape, jnp.float32),
        jnp.zeros(head_shape, jnp.float32),
    )
    key_piece = lax.all_gather(key_b, "blk", axis=1, tiled=True)
    value_piece = lax.all_gather(value_b, "blk", axis=1, tiled=True)

    def forward_block_step(block_index, inner_state):
        key_pos = block_index * slice_len + offsets
        key_seg = segment_of(cell_ends, key_pos)
        key_heads = take_block(key_piece, block_index)
        value_heads = take_block(value_piece, block_index)

        def forward_update(old_state):
            running_top, running_total, running_sum = old_state
            scores, allowed = block_scores(
                query_heads, key_heads, query_pos, key_pos, query_seg, key_seg, scale_qk
            )
            new_top = jnp.maximum(running_top, jnp.max(scores, axis=-1))
            factor = jnp.exp(running_top - new_top)
            weights_now = jnp.where(allowed, jnp.exp(scores - new_top[..., None]), 0.0)
            new_total = running_total * factor + jnp.sum(weights_now, axis=-1)
            new_sum = running_sum * factor[..., None] + jnp.einsum(
                "rqhk,rkhd->rqhd",
                weights_now.astype(jnp.bfloat16),
                value_heads,
                preferred_element_type=jnp.float32,
            )
            return (new_top, new_total, new_sum)

        return lax.cond(
            block_active(query_pos, key_pos, query_seg, key_seg),
            forward_update,
            unchanged,
            inner_state,
        )

    running_top, running_total, running_sum = lax.fori_loop(
        0, key_piece.shape[1] // slice_len, forward_block_step, start_state
    )
    attn_f32 = (running_sum / running_total[..., None]).reshape(row_count, slice_len, width_all)
    log_total = running_top + jnp.log(running_total)
    attn_b = attn_f32.astype(jnp.bfloat16)
    middle = inputs + jnp.dot(attn_b, w_o, preferred_element_type=jnp.float32) + b_o
    normed_two_val, second_pull = jax.vjp(layer_norm, middle, ln2_gain, ln2_bias)
    normed_two = normed_two_val.astype(jnp.bfloat16)
    hidden_pre = jnp.dot(normed_two, w_up, preferred_element_type=jnp.float32) + b_up
    hidden_val, gelu_pull = jax.vjp(jax.nn.gelu, hidden_pre)
    hidden_b = hidden_val.astype(jnp.bfloat16)
    output = (
        middle + jnp.dot(hidden_b, w_down, preferred_element_type=jnp.float32) + b_down
    ).astype(jnp.bfloat16)
    grad_out = cotangent.astype(jnp.float32)
    grad_w_down = jnp.einsum("rcf,rcd->fd", hidden_b, cotangent, preferred_element_type=jnp.float32)
    grad_b_down = jnp.sum(grad_out, axis=(0, 1))
    grad_hidden = jnp.einsum("rcd,fd->rcf", cotangent, w_down, preferred_element_type=jnp.float32)
    (grad_pre,) = gelu_pull(grad_hidden)
    grad_pre_b = grad_pre.astype(jnp.bfloat16)
    grad_w_up = jnp.einsum(
        "rcd,rcf->df", normed_two, grad_pre_b, preferred_element_type=jnp.float32
    )
    grad_b_up = jnp.sum(grad_pre_b.astype(jnp.float32), axis=(0, 1))
    grad_normed_two = jnp.einsum(
        "rcf,df->rcd", grad_pre_b, w_up, preferred_element_type=jnp.float32
    )
    grad_mid_norm, grad_ln2_gain, grad_ln2_bias = second_pull(grad_normed_two)
    grad_middle = grad_out + grad_mid_norm
    grad_branch_b = grad_middle.astype(jnp.bfloat16)
    grad_w_o = jnp.einsum("rce,rcd->ed", attn_b, grad_branch_b, preferred_element_type=jnp.float32)
    grad_b_o = jnp.sum(grad_branch_b.astype(jnp.float32), axis=(0, 1))
    grad_attn_b = jnp.einsum(
        "rcd,ed->rce", grad_branch_b, w_o, preferred_element_type=jnp.float32
    ).astype(jnp.bfloat16)
    delta_sum = jnp.sum((grad_attn_b.astype(jnp.float32) * attn_f32).reshape(head_shape), axis=-1)
    grad_heads = grad_attn_b.reshape(head_shape)
    whole_shape = (row_count, full_length, HEADS, head_size)
    back_state = (
        jnp.zeros(head_shape, jnp.float32),
        jnp.zeros(whole_shape, jnp.float32),
        jnp.zeros(whole_shape, jnp.float32),
    )
    backward_key_piece = lax.all_gather(key_b, "blk", axis=1, tiled=True)
    backward_value_piece = lax.all_gather(value_b, "blk", axis=1, tiled=True)

    def backward_block_step(block_index, inner_state):
        key_pos = block_index * slice_len + offsets
        key_seg = segment_of(cell_ends, key_pos)
        key_heads = take_block(backward_key_piece, block_index)
        value_heads = take_block(backward_value_piece, block_index)

        def backward_update(old_state):
            grad_query, grad_key, grad_value = backward_block(
                query_heads,
                grad_heads,
                log_total,
                delta_sum,
                key_heads,
                value_heads,
                query_pos,
                key_pos,
                query_seg,
                key_seg,
                scale_qk,
            )
            at_row = block_index * slice_len
            return (
                old_state[0] + grad_query,
                lax.dynamic_update_slice_in_dim(old_state[1], grad_key, at_row, 1),
                lax.dynamic_update_slice_in_dim(old_state[2], grad_value, at_row, 1),
            )

        return lax.cond(
            block_active(query_pos, key_pos, query_seg, key_seg),
            backward_update,
            unchanged,
            inner_state,
        )

    back_result = lax.fori_loop(
        0, backward_key_piece.shape[1] // slice_len, backward_block_step, back_state
    )
    grad_query_sum = back_result[0]
    grad_key_sum, grad_value_sum = (
        lax.psum_scatter(
            back_result[1].astype(jnp.bfloat16), "blk", scatter_dimension=1, tiled=True
        ).astype(jnp.float32),
        lax.psum_scatter(
            back_result[2].astype(jnp.bfloat16), "blk", scatter_dimension=1, tiled=True
        ).astype(jnp.float32),
    )
    flat_shape = (row_count, slice_len, width_all)
    grad_qkv_b = jnp.concatenate(
        [
            grad_query_sum.reshape(flat_shape),
            grad_key_sum.reshape(flat_shape),
            grad_value_sum.reshape(flat_shape),
        ],
        axis=-1,
    ).astype(jnp.bfloat16)
    grad_w_qkv = jnp.einsum(
        "rcd,rce->de", normed_one, grad_qkv_b, preferred_element_type=jnp.float32
    )
    column_sums = jnp.sum(grad_qkv_b.astype(jnp.float32), axis=(0, 1))
    grad_b_qv = jnp.concatenate([column_sums[:width_all], column_sums[2 * width_all :]])
    grad_normed_one = jnp.einsum(
        "rce,de->rcd", grad_qkv_b, w_qkv, preferred_element_type=jnp.float32
    )
    grad_in_norm, grad_ln1_gain, grad_ln1_bias = first_pull(grad_normed_one)
    input_grad = grad_middle + grad_in_norm
    grads = (
        grad_ln1_gain,
        grad_ln1_bias,
        grad_w_qkv,
        grad_b_qv,
        grad_w_o,
        grad_b_o,
        grad_ln2_gain,
        grad_ln2_bias,
        grad_w_up,
        grad_b_up,
        grad_w_down,
        grad_b_down,
    )
    summed = lax.psum(
        (
            grads[0],
            grads[1],
            grads[2],
            grads[3],
            grads[4],
            grads[5],
            grads[6],
            grads[7],
            grads[8],
            grads[9],
            grads[10],
            grads[11],
        ),
        ("rows", "blk"),
    )
    return (
        output,
        input_grad,
        summed[0],
        summed[1],
        summed[2],
        summed[3],
        summed[4],
        summed[5],
        summed[6],
        summed[7],
        summed[8],
        summed[9],
        summed[10],
        summed[11],
    )


def device_function(tokens, *rest):
    d = tokens.shape[2]
    whole_rows = (
        lax.axis_size("blk") == tokens.shape[0] == 4
        and lax.axis_size("rows") == 8
        and tokens.shape[1] == TILE
        and d == 512
    )
    return (row_device if whole_rows else general_device)(tokens, *rest)


def solution(mesh):
    in_specs = (
        P("rows", "blk", None),
        P("rows", None),
        P(),
        P(),
        P(),
        P(),
        P(),
        P(),
        P(),
        P(),
        P(),
        P(),
        P(),
        P(),
        P("rows", "blk", None),
    )
    out_specs = (
        P("rows", "blk", None),
        P("rows", "blk", None),
        P(),
        P(),
        P(),
        P(),
        P(),
        P(),
        P(),
        P(),
        P(),
        P(),
        P(),
        P(),
    )
    return jax.shard_map(
        device_function, mesh=mesh, in_specs=in_specs, out_specs=out_specs, check_vma=False
    )
```

```python
import functools

import jax
import jax.numpy as jnp
from jax import lax
from jax.experimental import pallas as pl
from jax.experimental.pallas import tpu as pltpu
from jax.sharding import PartitionSpec as P

HEADS = 8
norm_eps = 1e-05
neg_big = -1e30
BOTH = ("rows", "blk")
F32 = jnp.float32
BF16 = jnp.bfloat16
TILE = 256
LANES = 128
MIB = 1024 * 1024
B_FLOPS = 1e9
L_FLOPS = 1e9
MID_TILE = 512
MID_MIB = 28
LAST_MIB = 26


def mm(lhs, rhs):
    return lax.dot_general(lhs, rhs, (((1,), (0,)), ((), ())), preferred_element_type=F32)


def mm_nt(lhs, rhs):
    return lax.dot_general(lhs, rhs, (((1,), (1,)), ((), ())), preferred_element_type=F32)


def mm_tn(lhs, rhs):
    return lax.dot_general(lhs, rhs, (((0,), (0,)), ((), ())), preferred_element_type=F32)


def cell_start(ends_ref, positions):
    start = jnp.zeros_like(positions)
    for c in range(ends_ref.shape[0]):
        start = jnp.where(ends_ref[c] <= positions, ends_ref[c], start)
    return start


def norm_parts(values):
    average = jnp.mean(values, axis=-1, keepdims=True)
    centered = values - average
    variance = jnp.mean(centered * centered, axis=-1, keepdims=True)
    scale = lax.rsqrt(variance + norm_eps)
    return centered * scale, scale


def norm_pull(e, n, scale, gain):
    f = e * gain
    return (
        f
        - jnp.mean(f, axis=-1, keepdims=True)
        - n * jnp.mean(f * n, axis=-1, keepdims=True)
    ) * scale


def head_lanes(shape, half):
    lane = lax.broadcasted_iota(jnp.int32, shape, len(shape) - 1)
    return (lane < LANES // 2) if half == 0 else (lane >= LANES // 2)


def only_head(values, half):
    return jnp.where(head_lanes(values.shape, half), values, jnp.zeros_like(values))


def in_order(blk_ref, pieces, whole_ref):
    size = pieces[0].shape[0]
    for flip, piece_ref in enumerate(pieces):
        at = jnp.bitwise_xor(blk_ref[0], flip) * size
        whole_ref[pl.ds(pl.multiple_of(at, size), size), :] = piece_ref[...]


def forward_kernel(
    ends_ref, blk_ref, x0_ref, x1_ref, x2_ref, x3_ref, gain_ref, bias_ref, w_ref, b_ref,
    x_ref, q_ref, k_ref, v_ref, n1_ref, att_ref, lse_ref,
    mask_ref,
):
    in_order(blk_ref, (x0_ref, x1_ref, x2_ref, x3_ref), x_ref)
    t, width = x_ref.shape
    pairs = width // LANES
    scale_qk = (width // HEADS) ** (-0.5)
    for low in range(0, t, 512):
        rows = slice(low, low + 512)
        n, _ = norm_parts(x_ref[rows].astype(F32))
        n1 = (n * gain_ref[...] + bias_ref[...]).astype(BF16)
        n1_ref[rows] = n1
        q = mm(n1, w_ref[:, :width]) + b_ref[:, :width]
        q = (q.astype(BF16).astype(F32) * scale_qk).astype(BF16)
        k = mm(n1, w_ref[:, width : 2 * width]).astype(BF16)
        v = (mm(n1, w_ref[:, 2 * width :]) + b_ref[:, width:]).astype(BF16)
        for g in range(pairs):
            cols = slice(g * LANES, (g + 1) * LANES)
            q_ref[g, rows, :] = q[:, cols]
            k_ref[g, rows, :] = k[:, cols]
            v_ref[g, rows, :] = v[:, cols]
    for low in range(0, t, TILE):
        reach = low + TILE
        rows = slice(low, reach)
        q_pos = low + lax.broadcasted_iota(jnp.int32, (TILE, 1), 0)
        k_pos = lax.broadcasted_iota(jnp.int32, (TILE, reach), 1)
        start = cell_start(ends_ref, q_pos)
        mask_ref[:, :reach] = jnp.where((k_pos <= q_pos) & (k_pos >= start), 0.0, neg_big)
        lse_all = jnp.zeros((TILE, LANES), F32)
        lane = lax.broadcasted_iota(jnp.int32, lse_all.shape, 1)
        for g in range(pairs):
            qp = q_ref[g, rows, :]
            kp = k_ref[g, :reach, :]
            vp = v_ref[g, :reach, :]
            outs = []
            for half in range(2):
                s = mm_nt(only_head(qp, half), kp) + mask_ref[:, :reach]
                top = jnp.max(s, axis=-1, keepdims=True)
                p = jnp.exp(s - top)
                total = jnp.sum(p, axis=-1, keepdims=True)
                outs.append(mm(p.astype(BF16), vp) / total)
                lse_all = jnp.where(lane == 2 * g + half, top + jnp.log(total), lse_all)
            att_ref[g, rows, :] = jnp.where(head_lanes(outs[0].shape, 0), outs[0], outs[1])
        lse_ref[:, rows] = jnp.transpose(lse_all)[:HEADS]


def whole(shape):
    return pl.BlockSpec(shape, lambda i: (0,) * len(shape))


def by_row(cols, tile=TILE):
    return pl.BlockSpec((tile, cols), lambda i: (i, 0))


def by_pair(pairs, tile=TILE):
    return pl.BlockSpec((pairs, tile, LANES), lambda i: (0, i, 0))


def heads_row(tile=TILE):
    return pl.BlockSpec((HEADS, tile), lambda i: (0, i))


SMEM_SPEC = pl.BlockSpec(memory_space=pltpu.SMEM)


def in_hbm(*arrays):
    return [pltpu.with_memory_space_constraint(a, pltpu.HBM) for a in arrays]


def params(mib):
    return pltpu.CompilerParams(dimension_semantics=("arbitrary",), vmem_limit_bytes=mib * MIB)


def cost(flops, moved):
    return pl.CostEstimate(flops=int(flops), bytes_accessed=int(moved), transcendentals=0)


def forward_call(ends, blk, pieces, gain, bias, w_qkv, b_qv):
    size, d = pieces[0].shape
    t = size * len(pieces)
    pairs = d // LANES
    return pl.pallas_call(
        forward_kernel,
        grid=(1,),
        in_specs=[SMEM_SPEC, SMEM_SPEC]
        + [whole((size, d))] * len(pieces)
        + [whole((1, d)), whole((1, d)), whole(w_qkv.shape), whole((1, 2 * d))],
        out_specs=[
            whole((t, d)), whole((pairs, t, LANES)), whole((pairs, t, LANES)), whole((pairs, t, LANES)), whole((t, d)),
            whole((pairs, t, LANES)), whole((HEADS, t)),
        ],
        out_shape=[
            jax.ShapeDtypeStruct((t, d), BF16),
            pltpu.HBM((pairs, t, LANES), BF16),
            pltpu.HBM((pairs, t, LANES), BF16),
            pltpu.HBM((pairs, t, LANES), BF16),
            pltpu.HBM((t, d), BF16),
            jax.ShapeDtypeStruct((pairs, t, LANES), F32),
            jax.ShapeDtypeStruct((HEADS, t), F32),
        ],
        scratch_shapes=[pltpu.VMEM((TILE, t), F32)],
        compiler_params=params(34),
        cost_estimate=cost(20e9, 10e6),
        name="forward",
    )(ends, blk, *pieces, gain[None], bias[None], w_qkv, b_qv[None])


def leave(blk_ref, whole_ref, own_ref, near_ref, far_ref):
    size = own_ref.shape[0]
    for flip, dest in ((0, own_ref), (1, near_ref), (2, far_ref.at[:size]), (3, far_ref.at[size:])):
        at = jnp.bitwise_xor(blk_ref[0], flip) * size
        dest[...] = whole_ref[pl.ds(pl.multiple_of(at, size), size), :]


def relay_kernel(near_ref, far_ref, out_ref):
    size = near_ref.shape[0]
    out_ref[:size] = near_ref[...]
    out_ref[size:] = far_ref[size:]


def relay_call(near, far):
    return pl.pallas_call(
        relay_kernel,
        grid=(1,),
        in_specs=[whole(near.shape), whole(far.shape)],
        out_specs=whole(far.shape),
        out_shape=jax.ShapeDtypeStruct(far.shape, far.dtype),
        compiler_params=params(8),
        cost_estimate=cost(1e7, 1e5),
        name="relay",
    )(near, far)


def arrive_kernel(blk_ref, own_ref, near_ref, far_ref, out_ref):
    size = own_ref.shape[0]
    pieces = (own_ref[...], near_ref[:size], far_ref[:size], near_ref[size:])
    for flip, piece in enumerate(pieces):
        out_ref[jnp.bitwise_xor(blk_ref[0], flip)] = piece.astype(out_ref.dtype)


def arrive_call(blk, own, near, far, dtype):
    shape = (4,) + own.shape
    return pl.pallas_call(
        arrive_kernel,
        grid=(1,),
        in_specs=[SMEM_SPEC, whole(own.shape), whole(near.shape), whole(far.shape)],
        out_specs=whole(shape),
        out_shape=jax.ShapeDtypeStruct(shape, dtype),
        compiler_params=params(12),
        cost_estimate=cost(1e7, 1e5),
        name="arrive",
    )(blk, own, near, far)


def split_halves(core_ref, whole_ref, keep_ref, send_ref):
    half = keep_ref.shape[0]
    core = core_ref[0]
    keep_ref[...] = whole_ref[pl.ds(pl.multiple_of(core * half, half), half), :]
    send_ref[...] = whole_ref[pl.ds(pl.multiple_of((1 - core) * half, half), half), :].astype(BF16)


def middle_kernel(
    core_ref, blk_ref, att_ref, x_ref, c0_ref, c1_ref, c2_ref, c3_ref, wo_ref, bo_ref, gain_ref, bias_ref, wup_ref, bup_ref, wdown_ref, bdown_ref,
    o0_ref, o1_ref, o2_ref, gmid_ref, gatt_ref, delta_ref, keep_ref, send_ref, vec_ref,
    cot_ref, out_ref, gw_ref, hidden_ref, gpre_ref, n2_ref, attb_ref, gbr_ref,
):
    pairs = att_ref.shape[0]
    t, d = x_ref.shape
    ff = wup_ref.shape[-1]
    c0 = 0.7978845608028654
    c1 = 0.044715

    def col(values):
        return jnp.sum(values, axis=0, keepdims=True)

    in_order(blk_ref, (c0_ref, c1_ref, c2_ref, c3_ref), cot_ref)
    vec_ref[...] = jnp.zeros_like(vec_ref)
    head = lax.broadcasted_iota(jnp.int32, (HEADS, d), 0)
    lane = lax.broadcasted_iota(jnp.int32, (HEADS, d), 1)
    ones = jnp.where(lane // (d // HEADS) == head, 1.0, 0.0).astype(BF16)
    def tile(step, carry):
        rows = pl.ds(pl.multiple_of(step * MID_TILE, MID_TILE), MID_TILE)
        att = jnp.concatenate([att_ref[g, rows, :] for g in range(pairs)], axis=-1)
        att_b = att.astype(BF16)
        attb_ref[rows, :] = att_b
        middle = x_ref[rows, :].astype(F32) + mm(att_b, wo_ref[...]) + bo_ref[...]
        n, scale = norm_parts(middle)
        n2 = (n * gain_ref[...] + bias_ref[...]).astype(BF16)
        n2_ref[rows, :] = n2
        pre = mm(n2, wup_ref[...]) + bup_ref[...]
        sq = pre * pre
        th = jnp.tanh(c0 * (pre + c1 * (sq * pre)))
        half_one = 0.5 * (1.0 + th)
        hidden = (pre * half_one).astype(BF16)
        hidden_ref[rows, :] = hidden
        slope = half_one + (0.5 * pre) * (1.0 - th * th) * (c0 + (3.0 * c0 * c1) * sq)
        out_ref[rows, :] = (middle + mm(hidden, wdown_ref[...]) + bdown_ref[...]).astype(BF16)
        cot = cot_ref[rows, :]
        cot_f = cot.astype(F32)
        gpre = (mm_nt(cot, wdown_ref[...]) * slope).astype(BF16)
        gpre_ref[rows, :] = gpre
        e = mm_nt(gpre, wup_ref[...])
        gmid = cot_f + norm_pull(e, n, scale, gain_ref[...])
        gmid_ref[rows, :] = gmid
        gbr = gmid.astype(BF16)
        gbr_ref[rows, :] = gbr
        gatt = mm_nt(gbr, wo_ref[...]).astype(BF16)
        for g in range(pairs):
            gatt_ref[g, rows, :] = gatt[:, g * LANES : (g + 1) * LANES]
        prod = gatt.astype(F32) * att
        hi = prod.astype(BF16)
        lo = (prod - hi.astype(F32)).astype(BF16)
        delta_ref[:, rows] = mm_nt(ones, hi) + mm_nt(ones, lo)
        gsum = col(gpre.astype(F32))
        vec_ref[0:1] += col(cot_f)
        vec_ref[1:2] += gsum[:, :d]
        vec_ref[2:3] += gsum[:, d:]
        vec_ref[3:4] += col(e * n)
        vec_ref[4:5] += col(e)
        vec_ref[5:6] += col(gbr.astype(F32))
        return carry

    lax.fori_loop(0, t // MID_TILE, tile, 0)
    leave(blk_ref, out_ref, o0_ref, o1_ref, o2_ref)
    gw_ref[:ff] = mm_tn(hidden_ref[...], cot_ref[...])
    gw_ref[ff : ff + d] = mm_tn(n2_ref[...], gpre_ref[:, :d])
    gw_ref[ff + d : ff + 2 * d] = mm_tn(n2_ref[...], gpre_ref[:, d:])
    gw_ref[ff + 2 * d :] = mm_tn(attb_ref[...], gbr_ref[...])
    split_halves(core_ref, gw_ref, keep_ref, send_ref)


def middle_call(core, blk, att, x, cots, w_o, b_o, gain, bias, w_up, b_up, w_down, b_down):
    t, d = x.shape
    pairs = d // LANES
    ff = w_up.shape[1]
    half = (ff + 3 * d) // 2
    return pl.pallas_call(
        middle_kernel,
        grid=(1,),
        in_specs=[
            SMEM_SPEC, SMEM_SPEC,
            by_pair(pairs, t), by_row(d, t), *[whole(c.shape) for c in cots], whole((d, d)), whole((1, d)), whole((1, d)), whole((1, d)),
            whole((d, ff)), whole((1, ff)), whole((ff, d)), whole((1, d)),
        ],
        out_specs=[
            whole((t // 4, d)), whole((t // 4, d)), whole((t // 2, d)), by_row(d, t), by_pair(pairs, t), heads_row(t), whole((half, d)), whole((half, d)),
            whole((8, d)),
        ],
        out_shape=[
            pltpu.HBM((t // 4, d), BF16),
            pltpu.HBM((t // 4, d), BF16),
            pltpu.HBM((t // 2, d), BF16),
            pltpu.HBM((t, d), F32),
            pltpu.HBM((pairs, t, LANES), BF16),
            jax.ShapeDtypeStruct((HEADS, t), F32),
            jax.ShapeDtypeStruct((half, d), F32),
            jax.ShapeDtypeStruct((half, d), BF16),
            jax.ShapeDtypeStruct((8, d), F32),
        ],
        scratch_shapes=[
            pltpu.VMEM((t, d), BF16),
            pltpu.VMEM((t, d), BF16),
            pltpu.VMEM((2 * half, d), F32),
            pltpu.VMEM((t, ff), BF16),
            pltpu.VMEM((t, ff), BF16),
            pltpu.VMEM((t, d), BF16),
            pltpu.VMEM((t, d), BF16),
            pltpu.VMEM((t, d), BF16),
        ],
        compiler_params=params(30),
        cost_estimate=cost(15e9, 20e6),
        name="middle",
    )(core, blk, att, x, *cots, w_o, b_o[None], gain[None], bias[None], w_up, b_up[None], w_down, b_down[None])


def backward_kernel(first, ends_ref, q_ref, k_ref, v_ref, g_ref, lse_ref, delta_ref, dq_ref, dk_ref, dv_ref, acc_ref):
    pair = pl.program_id(0) + first
    t = q_ref.shape[1]
    scale_qk = (LANES // 2) ** (-0.5)
    pos_row = lax.broadcasted_iota(jnp.int32, (1, t), 1)
    start_row = cell_start(ends_ref, pos_row)
    acc_ref[...] = jnp.zeros_like(acc_ref)
    jobs = [(j, half) for j in range(t // TILE) for half in range(2)]
    lses = [lse_ref[pl.ds(2 * pair + half, 1), :] for half in range(2)]
    deltas = [delta_ref[pl.ds(2 * pair + half, 1), :] for half in range(2)]
    kts = {}
    outs = {}

    def scores(job):
        j, half = job
        low = j * TILE
        km = only_head(k_ref[0, low : low + TILE, :], half)
        vm = only_head(v_ref[0, low : low + TILE, :], half)
        return mm_nt(km, q_ref[0, low:, :]), mm_nt(vm, g_ref[0, low:, :])

    def rest(job, s, dp):
        j, half = job
        low = j * TILE
        k_pos = low + lax.broadcasted_iota(jnp.int32, (TILE, t - low), 0)
        high = low + TILE
        diag = (k_pos[:, :TILE] >= start_row[:, low:high]) & (k_pos[:, :TILE] <= pos_row[:, low:high])
        p = jnp.exp(jnp.where(diag, s[:, :TILE] - lses[half][:, low:high], neg_big))
        if high < t:
            far = k_pos[:, TILE:] >= start_row[:, high:]
            p = jnp.concatenate([p, jnp.exp(jnp.where(far, s[:, TILE:] - lses[half][:, high:], neg_big))], axis=1)
        ds = (p * (dp - deltas[half][:, low:])).astype(BF16)
        dv = mm(p.astype(BF16), g_ref[0, low:, :])
        dk = mm(ds, q_ref[0, low:, :])
        kt = jnp.transpose(k_ref[0, low : low + TILE, :])
        rows = slice(half * 64, half * 64 + 64)
        acc_ref[rows, low:] += mm(kt[rows], ds)
        if half == 0:
            outs[j] = (dk, dv)
        else:
            first_lanes = head_lanes(dk.shape, 0)
            dk_ref[0, low : low + TILE, :] = jnp.where(first_lanes, outs[j][0], dk).astype(BF16)
            dv_ref[0, low : low + TILE, :] = jnp.where(first_lanes, outs[j][1], dv).astype(BF16)

    ready = scores(jobs[0])
    for at, job in enumerate(jobs):
        now = ready
        if at + 1 < len(jobs):
            ready = scores(jobs[at + 1])
        rest(job, *now)
    dq_ref[0] = jnp.transpose((acc_ref[...] * scale_qk)).astype(BF16)


def backward_call(ends, q, k, v, gatt, lse, delta, first, count):
    pairs, t, _ = q.shape
    spec = pl.BlockSpec((1, t, LANES), lambda i: (i + first, 0, 0))
    out = pl.BlockSpec((1, t, LANES), lambda i: (i, 0, 0))
    return pl.pallas_call(
        functools.partial(backward_kernel, first),
        grid=(count,),
        in_specs=[SMEM_SPEC, spec, spec, spec, spec, whole((HEADS, t)), whole((HEADS, t))],
        out_specs=[out, out, out],
        out_shape=[jax.ShapeDtypeStruct((count, t, LANES), BF16)] * 3,
        scratch_shapes=[pltpu.VMEM((LANES, t), F32)],
        compiler_params=params(28),
        cost_estimate=cost(count * B_FLOPS, count * 1e5),
        name="backward",
    )(ends, *in_hbm(q, k, v, gatt), lse, delta)


VEC_ROWS = 128


def last_kernel(*refs):
    core_ref, blk_ref = refs[:2]
    grads = refs[2:5]
    n1_ref, x_ref, gmid_ref, gain_ref, w_ref, vecmid_ref = refs[5:11]
    g0_ref, g1_ref, g2_ref, keep_ref, send_ref, gw_ref, gin_ref = refs[11:]
    pairs = grads[0].shape[0]
    d = x_ref.shape[-1]
    half = keep_ref.shape[0]
    gqkv = jnp.concatenate([grads[part][g] for part in range(3) for g in range(pairs)], axis=-1)
    gw = mm_tn(n1_ref[...], gqkv)
    blocks = 3 * pairs
    for p in range(blocks):
        at = (p // (blocks // 2)) * half + (p % (blocks // 2)) * d
        gw_ref[at : at + d] = gw[:, p * LANES : (p + 1) * LANES]
    e = mm_nt(gqkv, w_ref[...])
    n, scale = norm_parts(x_ref[...].astype(F32))
    gin_ref[...] = (gmid_ref[...] + norm_pull(e, n, scale, gain_ref[...])).astype(BF16)
    leave(blk_ref, gin_ref, g0_ref, g1_ref, g2_ref)

    def col(values):
        return jnp.sum(values, axis=0, keepdims=True)

    rows = [vecmid_ref[r : r + 1] for r in range(6)]
    rows += [col(e * n), col(e), col(gqkv[:, :d].astype(F32)), col(gqkv[:, 2 * d :].astype(F32))]
    base = half - VEC_ROWS
    gw_ref[base:half] = jnp.zeros((VEC_ROWS, LANES), F32)
    gw_ref[half + base :] = jnp.zeros((VEC_ROWS, LANES), F32)
    for r, row in enumerate(rows):
        for g in range(d // LANES):
            at = base + r * (d // LANES) + g
            gw_ref[at : at + 1] = row[:, g * LANES : (g + 1) * LANES]
    split_halves(core_ref, gw_ref, keep_ref, send_ref)


def last_call(core, blk, grads, n1, x, gmid, gain, w_qkv, vec_mid):
    t, d = x.shape
    half = 3 * d * d // LANES // 2 + VEC_ROWS
    return pl.pallas_call(
        last_kernel,
        grid=(1,),
        in_specs=[SMEM_SPEC, SMEM_SPEC]
        + [whole(a.shape) for a in grads]
        + [by_row(d, t), by_row(d, t), by_row(d, t), whole((1, d)), whole(w_qkv.shape), whole((8, d))],
        out_specs=[whole((t // 4, d)), whole((t // 4, d)), whole((t // 2, d)), whole((half, LANES)), whole((half, LANES))],
        out_shape=[
            pltpu.HBM((t // 4, d), BF16),
            pltpu.HBM((t // 4, d), BF16),
            pltpu.HBM((t // 2, d), BF16),
            jax.ShapeDtypeStruct((half, LANES), F32),
            jax.ShapeDtypeStruct((half, LANES), BF16),
        ],
        scratch_shapes=[pltpu.VMEM((2 * half, LANES), F32), pltpu.VMEM((t, d), BF16)],
        compiler_params=params(28),
        cost_estimate=cost(L_FLOPS, 1e5),
        name="last",
    )(core, blk, *grads, n1, x, gmid, gain[None], w_qkv, vec_mid)


def ordered_halves(core_ref, own_ref, got_ref, write):
    pl.when(core_ref[0] == 0)(functools.partial(write, own_ref, got_ref))
    pl.when(core_ref[0] == 1)(functools.partial(write, got_ref, own_ref))


def finish_mid_kernel(core_ref, own_ref, got_ref, down_ref, up_ref, wo_ref):
    ff, d = down_ref.shape
    half = own_ref.shape[0]

    def write(low_ref, high_ref):
        def take(first, last):
            if last <= half:
                return low_ref[first:last].astype(F32)
            if first >= half:
                return high_ref[first - half : last - half].astype(F32)
            return jnp.concatenate([take(first, half), take(half, last)], axis=0)

        down_ref[...] = take(0, ff)
        up_ref[:, :d] = take(ff, ff + d)
        up_ref[:, d:] = take(ff + d, ff + 2 * d)
        wo_ref[...] = take(ff + 2 * d, ff + 3 * d)

    ordered_halves(core_ref, own_ref, got_ref, write)


def finish_last_kernel(core_ref, own_ref, got_ref, qkv_ref, *vec_refs):
    d = qkv_ref.shape[0]
    half = own_ref.shape[0]
    blocks = qkv_ref.shape[1] // LANES

    def write(low_ref, high_ref):
        for p in range(blocks):
            ref = (low_ref, high_ref)[p // (blocks // 2)]
            at = (p % (blocks // 2)) * d
            qkv_ref[:, p * LANES : (p + 1) * LANES] = ref[at : at + d].astype(F32)
        at = half - VEC_ROWS
        for ref in vec_refs:
            for g in range(ref.shape[1] // LANES):
                ref[:, g * LANES : (g + 1) * LANES] = low_ref[at : at + 1].astype(F32)
                at += 1

    ordered_halves(core_ref, own_ref, got_ref, write)


def finish_call(kernel, core, own, got, shapes, name):
    return pl.pallas_call(
        kernel,
        grid=(1,),
        in_specs=[SMEM_SPEC, whole(own.shape), whole(got.shape)],
        out_specs=[whole(shape) for shape in shapes],
        out_shape=[jax.ShapeDtypeStruct(shape, F32) for shape in shapes],
        compiler_params=params(28),
        cost_estimate=cost(1e8, 8e6),
        name=name,
    )(core, own, got)


def send_xor(values, flip):
    count = lax.axis_size(BOTH)
    return lax.ppermute(values, BOTH, [(i, i ^ flip) for i in range(count)])


def add_kernel(place_ref, *refs):
    outs = place_ref.shape[0]
    terms, results = refs[:-outs], refs[-outs:]
    size = results[0].shape[0]
    for flip, result in enumerate(results):
        rows = pl.ds(pl.multiple_of(jnp.bitwise_xor(place_ref[0], flip) * size, size), size)
        total = terms[0][rows, :].astype(F32)
        for term in terms[1:]:
            total = total + term[rows, :].astype(F32)
        result[...] = total.astype(result.dtype)


def add_call(place, parts, terms, own_dtype):
    rows, lanes = terms[0].shape
    shape = (rows // parts, lanes)
    places = jnp.broadcast_to(place, (parts,)).astype(jnp.int32)
    return pl.pallas_call(
        add_kernel,
        grid=(1,),
        in_specs=[SMEM_SPEC] + [whole(a.shape) for a in terms],
        out_specs=[whole(shape)] * parts,
        out_shape=[jax.ShapeDtypeStruct(shape, own_dtype if p == 0 else BF16) for p in range(parts)],
        compiler_params=params(28),
        cost_estimate=cost(1e8, 4e6),
        name="add",
    )(places, *terms)


def join_kernel(place_ref, *refs):
    out_ref = refs[-1]
    for flip, ref in enumerate(refs[:-1]):
        size = ref.shape[0]
        rows = pl.ds(pl.multiple_of(jnp.bitwise_xor(place_ref[0], flip) * size, size), size)
        out_ref[rows, :] = ref[...]


def join_call(place, pieces):
    rows, lanes = pieces[0].shape
    shape = (rows * len(pieces), lanes)
    return pl.pallas_call(
        join_kernel,
        grid=(1,),
        in_specs=[SMEM_SPEC] + [whole(p.shape) for p in pieces],
        out_specs=whole(shape),
        out_shape=jax.ShapeDtypeStruct(shape, pieces[0].dtype),
        compiler_params=params(28),
        cost_estimate=cost(1e8, 2e6),
        name="join",
    )(place[None].astype(jnp.int32), *pieces)


def swap_parts(parts, shift):
    return [send_xor(part, (flip + 1) << shift) for flip, part in enumerate(parts)]


def spread(part, shift, parts):
    return [send_xor(part, flip << shift) for flip in range(1, parts)]


def after(values, *others):
    return lax.optimization_barrier((values,) + others)[0]


def row_device(
    tokens, seg_lengths, ln1_gain, ln1_bias, w_qkv, b_qv, w_o, b_o, ln2_gain, ln2_bias,
    w_up, b_up, w_down, b_down, cotangent,
):
    row_count, slice_len, d = tokens.shape
    row = lax.axis_index("blk")
    me = lax.axis_index("rows") * lax.axis_size("blk") + row
    place_core = me & 1
    place_plane = (me >> 1) & 3
    place_deep = me >> 3
    core = place_core[None].astype(jnp.int32)
    blk = row[None].astype(jnp.int32)
    ends = jnp.cumsum(seg_lengths, axis=1)
    ends = lax.dynamic_index_in_dim(ends, row, 0, keepdims=False).astype(jnp.int32)

    def cut(values):
        return [lax.dynamic_index_in_dim(values, row ^ flip, 0, keepdims=False) for flip in range(row_count)]

    def swap(pieces):
        return [pieces[0]] + swap_parts(pieces[1:], 0)

    x = swap(cut(tokens))
    cot = cut(cotangent)
    cot = lax.optimization_barrier(tuple(cot) + tuple(x))[:row_count]
    cot = swap(list(cot))
    x, q, k, v, n1, att, lse = forward_call(ends, blk, x, ln1_gain, ln1_bias, w_qkv, b_qv)
    out, out_near, out_far, gmid, gatt, delta, keep, send, vec_mid = middle_call(
        core, blk, att, x, cot, w_o, b_o, ln2_gain, ln2_bias, w_up, b_up, w_down, b_down
    )
    own, *parts = add_call(place_plane, 4, [keep, send_xor(send, 1)], F32)
    grads = backward_call(after(ends, own), q, k, v, gatt, lse, delta, 0, d // LANES)
    own, *parts = add_call(after(place_deep, grads[0]), 4, [own] + swap_parts(parts, 1), F32)
    out_far = send_xor(after(out_far, own), 2)
    first = [own] + swap_parts(parts, 3)
    gin, gin_near, gin_far, keep, send = last_call(
        after(core, own), blk, grads, n1, x, gmid, ln1_gain, w_qkv, vec_mid
    )
    (first,) = add_call(0, 1, first, BF16)
    send, first, out_far = lax.optimization_barrier((send, first, out_far))
    first_z = spread(first, 3, 2)
    own, *parts = add_call(place_plane, 4, [keep, send_xor(send, 1)], F32)
    first = join_call(after(place_deep & 1, own), [first] + first_z)
    first_z = spread(first, 4, 2)
    second = swap_parts(parts, 1)
    own, *parts = add_call(place_deep, 4, [own] + second, F32)
    out_near = send_xor(relay_call(after(out_near, own), out_far), 1)
    first = join_call(place_deep >> 1, [first] + first_z)
    first, gin_far = lax.optimization_barrier((first, gin_far, own))[:2]
    gin_far = send_xor(gin_far, 2)
    (second,) = add_call(0, 1, [own] + swap_parts(parts, 3), BF16)
    first = join_call(after(place_plane & 1, second), [first] + spread(first, 1, 2))
    second = join_call(place_deep, [second] + spread(second, 3, 4))
    first = join_call(after(place_plane >> 1, second), [first] + spread(first, 2, 2))
    gin_near = send_xor(relay_call(after(gin_near, second), gin_far), 1)
    output = arrive_call(after(blk, second), out, out_near, out_far, BF16)
    input_grad = arrive_call(blk, gin, gin_near, gin_far, F32)
    second = join_call(after(place_plane, output, input_grad), [second] + spread(second, 1, 4))
    gw_down, gw_up, gw_o = finish_call(
        finish_mid_kernel, core, first, send_xor(first, 1), [w_down.shape, w_up.shape, w_o.shape], "finish_mid"
    )
    gw_qkv, *vecs = finish_call(
        finish_last_kernel, after(core, gw_down), second, send_xor(second, 1),
        [w_qkv.shape] + [(1, size) for size in (d, 2 * d, d, d, d, d, d, 2 * d)], "finish_last",
    )
    vecs = [vec.reshape(-1) for vec in vecs]
    g_down_b, g_up_b, g_ln2_gain, g_ln2_bias, g_o_b, g_ln1_gain, g_ln1_bias, g_qv_b = vecs
    return (
        output, input_grad, g_ln1_gain, g_ln1_bias, gw_qkv, g_qv_b, gw_o, g_o_b, g_ln2_gain, g_ln2_bias,
        gw_up, g_up_b, gw_down, g_down_b,
    )


def layer_norm(values, gain_vec, bias_vec):
    average = jnp.mean(values, axis=-1, keepdims=True)
    centered = values - average
    variance = jnp.mean(centered * centered, axis=-1, keepdims=True)
    return centered * lax.rsqrt(variance + norm_eps) * gain_vec + bias_vec


def segment_of(cell_ends, positions):
    return jnp.sum((cell_ends[:, None, :] <= positions[None, :, None]).astype(jnp.int32), axis=-1)


def block_scores(query_heads, key_heads, query_pos, key_pos, query_seg, key_seg, scale_qk):
    raw_scores = (
        jnp.einsum("rqhd,rkhd->rqhk", query_heads, key_heads, preferred_element_type=jnp.float32)
        * scale_qk
    )
    causal = key_pos[None, :] <= query_pos[:, None]
    same_cell = query_seg[:, :, None] == key_seg[:, None, :]
    allowed = (causal[None] & same_cell)[:, :, None, :]
    return (jnp.where(allowed, raw_scores, neg_big), allowed)


def block_active(query_pos, key_pos, query_seg, key_seg):
    return (key_pos[0] <= query_pos[-1]) & jnp.any(key_seg[:, -1] >= query_seg[:, 0])


def backward_block(
    query_heads,
    grad_heads,
    log_total,
    delta_sum,
    key_heads,
    value_heads,
    query_pos,
    key_pos,
    query_seg,
    key_seg,
    scale_qk,
):
    scores, allowed = block_scores(
        query_heads, key_heads, query_pos, key_pos, query_seg, key_seg, scale_qk
    )
    softmaxed = jnp.where(allowed, jnp.exp(scores - log_total[..., None]), 0.0)
    grad_probs = jnp.einsum(
        "rqhd,rkhd->rqhk", grad_heads, value_heads, preferred_element_type=jnp.float32
    )
    grad_scores = (softmaxed * (grad_probs - delta_sum[..., None])).astype(jnp.bfloat16)
    grad_query = (
        jnp.einsum("rqhk,rkhd->rqhd", grad_scores, key_heads, preferred_element_type=jnp.float32)
        * scale_qk
    )
    grad_key = (
        jnp.einsum("rqhk,rqhd->rkhd", grad_scores, query_heads, preferred_element_type=jnp.float32)
        * scale_qk
    )
    grad_value = jnp.einsum(
        "rqhk,rqhd->rkhd",
        softmaxed.astype(jnp.bfloat16),
        grad_heads,
        preferred_element_type=jnp.float32,
    )
    return (grad_query, grad_key, grad_value)


def unchanged(old_state):
    return old_state


def general_device(
    tokens,
    seg_lengths,
    ln1_gain,
    ln1_bias,
    w_qkv,
    b_qv,
    w_o,
    b_o,
    ln2_gain,
    ln2_bias,
    w_up,
    b_up,
    w_down,
    b_down,
    cotangent,
):
    row_count, slice_len, width_all = tokens.shape
    head_size = width_all // HEADS
    scale_qk = head_size ** (-0.5)
    head_shape = (row_count, slice_len, HEADS, head_size)
    stat_shape = (row_count, slice_len, HEADS)
    full_length = lax.axis_size("blk") * slice_len
    offsets = jnp.arange(slice_len, dtype=jnp.int32)
    query_pos = lax.axis_index("blk") * slice_len + offsets
    cell_ends = jnp.cumsum(seg_lengths, axis=1)
    query_seg = segment_of(cell_ends, query_pos)

    def take_block(piece, block_index):
        return lax.dynamic_slice_in_dim(piece, block_index * slice_len, slice_len, 1).reshape(
            head_shape
        )

    inputs = tokens.astype(jnp.float32)
    normed_val, first_pull = jax.vjp(layer_norm, inputs, ln1_gain, ln1_bias)
    normed_one = normed_val.astype(jnp.bfloat16)
    projected = jnp.dot(normed_one, w_qkv, preferred_element_type=jnp.float32)
    query_b = (projected[..., :width_all] + b_qv[:width_all]).astype(jnp.bfloat16)
    key_b = projected[..., width_all : 2 * width_all].astype(jnp.bfloat16)
    value_b = (projected[..., 2 * width_all :] + b_qv[width_all:]).astype(jnp.bfloat16)
    query_heads = query_b.reshape(head_shape)
    start_state = (
        jnp.full(stat_shape, neg_big, jnp.float32),
        jnp.zeros(stat_shape, jnp.float32),
        jnp.zeros(head_shape, jnp.float32),
    )
    key_piece = lax.all_gather(key_b, "blk", axis=1, tiled=True)
    value_piece = lax.all_gather(value_b, "blk", axis=1, tiled=True)

    def forward_block_step(block_index, inner_state):
        key_pos = block_index * slice_len + offsets
        key_seg = segment_of(cell_ends, key_pos)
        key_heads = take_block(key_piece, block_index)
        value_heads = take_block(value_piece, block_index)

        def forward_update(old_state):
            running_top, running_total, running_sum = old_state
            scores, allowed = block_scores(
                query_heads, key_heads, query_pos, key_pos, query_seg, key_seg, scale_qk
            )
            new_top = jnp.maximum(running_top, jnp.max(scores, axis=-1))
            factor = jnp.exp(running_top - new_top)
            weights_now = jnp.where(allowed, jnp.exp(scores - new_top[..., None]), 0.0)
            new_total = running_total * factor + jnp.sum(weights_now, axis=-1)
            new_sum = running_sum * factor[..., None] + jnp.einsum(
                "rqhk,rkhd->rqhd",
                weights_now.astype(jnp.bfloat16),
                value_heads,
                preferred_element_type=jnp.float32,
            )
            return (new_top, new_total, new_sum)

        return lax.cond(
            block_active(query_pos, key_pos, query_seg, key_seg),
            forward_update,
            unchanged,
            inner_state,
        )

    running_top, running_total, running_sum = lax.fori_loop(
        0, key_piece.shape[1] // slice_len, forward_block_step, start_state
    )
    attn_f32 = (running_sum / running_total[..., None]).reshape(row_count, slice_len, width_all)
    log_total = running_top + jnp.log(running_total)
    attn_b = attn_f32.astype(jnp.bfloat16)
    middle = inputs + jnp.dot(attn_b, w_o, preferred_element_type=jnp.float32) + b_o
    normed_two_val, second_pull = jax.vjp(layer_norm, middle, ln2_gain, ln2_bias)
    normed_two = normed_two_val.astype(jnp.bfloat16)
    hidden_pre = jnp.dot(normed_two, w_up, preferred_element_type=jnp.float32) + b_up
    hidden_val, gelu_pull = jax.vjp(jax.nn.gelu, hidden_pre)
    hidden_b = hidden_val.astype(jnp.bfloat16)
    output = (
        middle + jnp.dot(hidden_b, w_down, preferred_element_type=jnp.float32) + b_down
    ).astype(jnp.bfloat16)
    grad_out = cotangent.astype(jnp.float32)
    grad_w_down = jnp.einsum("rcf,rcd->fd", hidden_b, cotangent, preferred_element_type=jnp.float32)
    grad_b_down = jnp.sum(grad_out, axis=(0, 1))
    grad_hidden = jnp.einsum("rcd,fd->rcf", cotangent, w_down, preferred_element_type=jnp.float32)
    (grad_pre,) = gelu_pull(grad_hidden)
    grad_pre_b = grad_pre.astype(jnp.bfloat16)
    grad_w_up = jnp.einsum(
        "rcd,rcf->df", normed_two, grad_pre_b, preferred_element_type=jnp.float32
    )
    grad_b_up = jnp.sum(grad_pre_b.astype(jnp.float32), axis=(0, 1))
    grad_normed_two = jnp.einsum(
        "rcf,df->rcd", grad_pre_b, w_up, preferred_element_type=jnp.float32
    )
    grad_mid_norm, grad_ln2_gain, grad_ln2_bias = second_pull(grad_normed_two)
    grad_middle = grad_out + grad_mid_norm
    grad_branch_b = grad_middle.astype(jnp.bfloat16)
    grad_w_o = jnp.einsum("rce,rcd->ed", attn_b, grad_branch_b, preferred_element_type=jnp.float32)
    grad_b_o = jnp.sum(grad_branch_b.astype(jnp.float32), axis=(0, 1))
    grad_attn_b = jnp.einsum(
        "rcd,ed->rce", grad_branch_b, w_o, preferred_element_type=jnp.float32
    ).astype(jnp.bfloat16)
    delta_sum = jnp.sum((grad_attn_b.astype(jnp.float32) * attn_f32).reshape(head_shape), axis=-1)
    grad_heads = grad_attn_b.reshape(head_shape)
    whole_shape = (row_count, full_length, HEADS, head_size)
    back_state = (
        jnp.zeros(head_shape, jnp.float32),
        jnp.zeros(whole_shape, jnp.float32),
        jnp.zeros(whole_shape, jnp.float32),
    )
    backward_key_piece = lax.all_gather(key_b, "blk", axis=1, tiled=True)
    backward_value_piece = lax.all_gather(value_b, "blk", axis=1, tiled=True)

    def backward_block_step(block_index, inner_state):
        key_pos = block_index * slice_len + offsets
        key_seg = segment_of(cell_ends, key_pos)
        key_heads = take_block(backward_key_piece, block_index)
        value_heads = take_block(backward_value_piece, block_index)

        def backward_update(old_state):
            grad_query, grad_key, grad_value = backward_block(
                query_heads,
                grad_heads,
                log_total,
                delta_sum,
                key_heads,
                value_heads,
                query_pos,
                key_pos,
                query_seg,
                key_seg,
                scale_qk,
            )
            at_row = block_index * slice_len
            return (
                old_state[0] + grad_query,
                lax.dynamic_update_slice_in_dim(old_state[1], grad_key, at_row, 1),
                lax.dynamic_update_slice_in_dim(old_state[2], grad_value, at_row, 1),
            )

        return lax.cond(
            block_active(query_pos, key_pos, query_seg, key_seg),
            backward_update,
            unchanged,
            inner_state,
        )

    back_result = lax.fori_loop(
        0, backward_key_piece.shape[1] // slice_len, backward_block_step, back_state
    )
    grad_query_sum = back_result[0]
    grad_key_sum, grad_value_sum = (
        lax.psum_scatter(
            back_result[1].astype(jnp.bfloat16), "blk", scatter_dimension=1, tiled=True
        ).astype(jnp.float32),
        lax.psum_scatter(
            back_result[2].astype(jnp.bfloat16), "blk", scatter_dimension=1, tiled=True
        ).astype(jnp.float32),
    )
    flat_shape = (row_count, slice_len, width_all)
    grad_qkv_b = jnp.concatenate(
        [
            grad_query_sum.reshape(flat_shape),
            grad_key_sum.reshape(flat_shape),
            grad_value_sum.reshape(flat_shape),
        ],
        axis=-1,
    ).astype(jnp.bfloat16)
    grad_w_qkv = jnp.einsum(
        "rcd,rce->de", normed_one, grad_qkv_b, preferred_element_type=jnp.float32
    )
    column_sums = jnp.sum(grad_qkv_b.astype(jnp.float32), axis=(0, 1))
    grad_b_qv = jnp.concatenate([column_sums[:width_all], column_sums[2 * width_all :]])
    grad_normed_one = jnp.einsum(
        "rce,de->rcd", grad_qkv_b, w_qkv, preferred_element_type=jnp.float32
    )
    grad_in_norm, grad_ln1_gain, grad_ln1_bias = first_pull(grad_normed_one)
    input_grad = grad_middle + grad_in_norm
    grads = (
        grad_ln1_gain,
        grad_ln1_bias,
        grad_w_qkv,
        grad_b_qv,
        grad_w_o,
        grad_b_o,
        grad_ln2_gain,
        grad_ln2_bias,
        grad_w_up,
        grad_b_up,
        grad_w_down,
        grad_b_down,
    )
    summed = lax.psum(
        (
            grads[0],
            grads[1],
            grads[2],
            grads[3],
            grads[4],
            grads[5],
            grads[6],
            grads[7],
            grads[8],
            grads[9],
            grads[10],
            grads[11],
        ),
        ("rows", "blk"),
    )
    return (
        output,
        input_grad,
        summed[0],
        summed[1],
        summed[2],
        summed[3],
        summed[4],
        summed[5],
        summed[6],
        summed[7],
        summed[8],
        summed[9],
        summed[10],
        summed[11],
    )


def device_function(tokens, *rest):
    d = tokens.shape[2]
    whole_rows = (
        lax.axis_size("blk") == tokens.shape[0] == 4
        and lax.axis_size("rows") == 8
        and tokens.shape[1] == TILE
        and d == 512
    )
    return (row_device if whole_rows else general_device)(tokens, *rest)


def solution(mesh):
    in_specs = (
        P("rows", "blk", None),
        P("rows", None),
        P(),
        P(),
        P(),
        P(),
        P(),
        P(),
        P(),
        P(),
        P(),
        P(),
        P(),
        P(),
        P("rows", "blk", None),
    )
    out_specs = (
        P("rows", "blk", None),
        P("rows", "blk", None),
        P(),
        P(),
        P(),
        P(),
        P(),
        P(),
        P(),
        P(),
        P(),
        P(),
        P(),
        P(),
    )
    return jax.shard_map(
        device_function, mesh=mesh, in_specs=in_specs, out_specs=out_specs, check_vma=False
    )
```

```python
import functools

import jax
import jax.numpy as jnp
from jax import lax
from jax.experimental import pallas as pl
from jax.experimental.pallas import tpu as pltpu
from jax.sharding import PartitionSpec as P

HEADS = 8
norm_eps = 1e-05
neg_big = -1e30
BOTH = ("rows", "blk")
F32 = jnp.float32
BF16 = jnp.bfloat16
TILE = 256
LANES = 128
MIB = 1024 * 1024
B_FLOPS = 1e9
L_FLOPS = 1e9
MID_TILE = 512
MID_MIB = 28
LAST_MIB = 26


def mm(lhs, rhs):
    return lax.dot_general(lhs, rhs, (((1,), (0,)), ((), ())), preferred_element_type=F32)


def mm_nt(lhs, rhs):
    return lax.dot_general(lhs, rhs, (((1,), (1,)), ((), ())), preferred_element_type=F32)


def mm_tn(lhs, rhs):
    return lax.dot_general(lhs, rhs, (((0,), (0,)), ((), ())), preferred_element_type=F32)


def cell_start(ends_ref, positions):
    start = jnp.zeros_like(positions)
    for c in range(ends_ref.shape[0]):
        start = jnp.where(ends_ref[c] <= positions, ends_ref[c], start)
    return start


def norm_parts(values):
    average = jnp.mean(values, axis=-1, keepdims=True)
    centered = values - average
    variance = jnp.mean(centered * centered, axis=-1, keepdims=True)
    scale = lax.rsqrt(variance + norm_eps)
    return centered * scale, scale


def norm_pull(e, n, scale, gain):
    f = e * gain
    return (
        f
        - jnp.mean(f, axis=-1, keepdims=True)
        - n * jnp.mean(f * n, axis=-1, keepdims=True)
    ) * scale


def head_lanes(shape, half):
    lane = lax.broadcasted_iota(jnp.int32, shape, len(shape) - 1)
    return (lane < LANES // 2) if half == 0 else (lane >= LANES // 2)


def only_head(values, half):
    return jnp.where(head_lanes(values.shape, half), values, jnp.zeros_like(values))


def in_order(blk_ref, pieces, whole_ref):
    size = pieces[0].shape[0]
    for flip, piece_ref in enumerate(pieces):
        at = jnp.bitwise_xor(blk_ref[0], flip) * size
        whole_ref[pl.ds(pl.multiple_of(at, size), size), :] = piece_ref[...]


def forward_kernel(
    ends_ref, blk_ref, x0_ref, x1_ref, x2_ref, x3_ref, gain_ref, bias_ref, w_ref, b_ref,
    x_ref, q_ref, k_ref, v_ref, n1_ref, att_ref, lse_ref,
    mask_ref,
):
    in_order(blk_ref, (x0_ref, x1_ref, x2_ref, x3_ref), x_ref)
    t, width = x_ref.shape
    pairs = width // LANES
    scale_qk = (width // HEADS) ** (-0.5)
    for low in range(0, t, 512):
        rows = slice(low, low + 512)
        n, _ = norm_parts(x_ref[rows].astype(F32))
        n1 = (n * gain_ref[...] + bias_ref[...]).astype(BF16)
        n1_ref[rows] = n1
        q = mm(n1, w_ref[:, :width]) + b_ref[:, :width]
        q = (q.astype(BF16).astype(F32) * scale_qk).astype(BF16)
        k = mm(n1, w_ref[:, width : 2 * width]).astype(BF16)
        v = (mm(n1, w_ref[:, 2 * width :]) + b_ref[:, width:]).astype(BF16)
        for g in range(pairs):
            cols = slice(g * LANES, (g + 1) * LANES)
            q_ref[g, rows, :] = q[:, cols]
            k_ref[g, rows, :] = k[:, cols]
            v_ref[g, rows, :] = v[:, cols]
    for low in range(0, t, TILE):
        reach = low + TILE
        rows = slice(low, reach)
        q_pos = low + lax.broadcasted_iota(jnp.int32, (TILE, 1), 0)
        k_pos = lax.broadcasted_iota(jnp.int32, (TILE, reach), 1)
        start = cell_start(ends_ref, q_pos)
        mask_ref[:, :reach] = jnp.where((k_pos <= q_pos) & (k_pos >= start), 0.0, neg_big)
        lse_all = jnp.zeros((TILE, LANES), F32)
        lane = lax.broadcasted_iota(jnp.int32, lse_all.shape, 1)
        for g in range(pairs):
            qp = q_ref[g, rows, :]
            kp = k_ref[g, :reach, :]
            vp = v_ref[g, :reach, :]
            outs = []
            for half in range(2):
                s = mm_nt(only_head(qp, half), kp) + mask_ref[:, :reach]
                top = jnp.max(s, axis=-1, keepdims=True)
                p = jnp.exp(s - top)
                total = jnp.sum(p, axis=-1, keepdims=True)
                outs.append(mm(p.astype(BF16), vp) / total)
                lse_all = jnp.where(lane == 2 * g + half, top + jnp.log(total), lse_all)
            att_ref[g, rows, :] = jnp.where(head_lanes(outs[0].shape, 0), outs[0], outs[1])
        lse_ref[:, rows] = jnp.transpose(lse_all)[:HEADS]


def whole(shape):
    return pl.BlockSpec(shape, lambda i: (0,) * len(shape))


def by_row(cols, tile=TILE):
    return pl.BlockSpec((tile, cols), lambda i: (i, 0))


def by_pair(pairs, tile=TILE):
    return pl.BlockSpec((pairs, tile, LANES), lambda i: (0, i, 0))


def heads_row(tile=TILE):
    return pl.BlockSpec((HEADS, tile), lambda i: (0, i))


SMEM_SPEC = pl.BlockSpec(memory_space=pltpu.SMEM)


def in_hbm(*arrays):
    return [pltpu.with_memory_space_constraint(a, pltpu.HBM) for a in arrays]


def params(mib):
    return pltpu.CompilerParams(dimension_semantics=("arbitrary",), vmem_limit_bytes=mib * MIB)


def cost(flops, moved):
    return pl.CostEstimate(flops=int(flops), bytes_accessed=int(moved), transcendentals=0)


def forward_call(ends, blk, pieces, gain, bias, w_qkv, b_qv):
    size, d = pieces[0].shape
    t = size * len(pieces)
    pairs = d // LANES
    return pl.pallas_call(
        forward_kernel,
        grid=(1,),
        in_specs=[SMEM_SPEC, SMEM_SPEC]
        + [whole((size, d))] * len(pieces)
        + [whole((1, d)), whole((1, d)), whole(w_qkv.shape), whole((1, 2 * d))],
        out_specs=[
            whole((t, d)), whole((pairs, t, LANES)), whole((pairs, t, LANES)), whole((pairs, t, LANES)), whole((t, d)),
            whole((pairs, t, LANES)), whole((HEADS, t)),
        ],
        out_shape=[
            jax.ShapeDtypeStruct((t, d), BF16),
            pltpu.HBM((pairs, t, LANES), BF16),
            pltpu.HBM((pairs, t, LANES), BF16),
            pltpu.HBM((pairs, t, LANES), BF16),
            pltpu.HBM((t, d), BF16),
            jax.ShapeDtypeStruct((pairs, t, LANES), F32),
            jax.ShapeDtypeStruct((HEADS, t), F32),
        ],
        scratch_shapes=[pltpu.VMEM((TILE, t), F32)],
        compiler_params=params(34),
        cost_estimate=cost(20e9, 10e6),
        name="forward",
    )(ends, blk, *pieces, gain[None], bias[None], w_qkv, b_qv[None])


def leave(blk_ref, whole_ref, own_ref, near_ref, far_ref):
    size = own_ref.shape[0]
    for flip, dest in ((0, own_ref), (1, near_ref), (2, far_ref.at[:size]), (3, far_ref.at[size:])):
        at = jnp.bitwise_xor(blk_ref[0], flip) * size
        dest[...] = whole_ref[pl.ds(pl.multiple_of(at, size), size), :]


def relay_kernel(near_ref, far_ref, out_ref):
    size = near_ref.shape[0]
    out_ref[:size] = near_ref[...]
    out_ref[size:] = far_ref[size:]


def relay_call(near, far):
    return pl.pallas_call(
        relay_kernel,
        grid=(1,),
        in_specs=[whole(near.shape), whole(far.shape)],
        out_specs=whole(far.shape),
        out_shape=jax.ShapeDtypeStruct(far.shape, far.dtype),
        compiler_params=params(8),
        cost_estimate=cost(1e7, 1e5),
        name="relay",
    )(near, far)


def arrive_kernel(blk_ref, own_ref, near_ref, far_ref, out_ref):
    size = own_ref.shape[0]
    pieces = (own_ref[...], near_ref[:size], far_ref[:size], near_ref[size:])
    for flip, piece in enumerate(pieces):
        out_ref[jnp.bitwise_xor(blk_ref[0], flip)] = piece.astype(out_ref.dtype)


def arrive_call(blk, own, near, far, dtype):
    shape = (4,) + own.shape
    return pl.pallas_call(
        arrive_kernel,
        grid=(1,),
        in_specs=[SMEM_SPEC, whole(own.shape), whole(near.shape), whole(far.shape)],
        out_specs=whole(shape),
        out_shape=jax.ShapeDtypeStruct(shape, dtype),
        compiler_params=params(12),
        cost_estimate=cost(1e7, 1e5),
        name="arrive",
    )(blk, own, near, far)


def split_halves(core_ref, whole_ref, keep_ref, send_ref):
    half = keep_ref.shape[0]
    core = core_ref[0]
    keep_ref[...] = whole_ref[pl.ds(pl.multiple_of(core * half, half), half), :].astype(BF16)
    send_ref[...] = whole_ref[pl.ds(pl.multiple_of((1 - core) * half, half), half), :].astype(BF16)


def middle_kernel(
    core_ref, blk_ref, att_ref, x_ref, c0_ref, c1_ref, c2_ref, c3_ref, wo_ref, bo_ref, gain_ref, bias_ref, wup_ref, bup_ref, wdown_ref, bdown_ref,
    o0_ref, o1_ref, o2_ref, gmid_ref, gatt_ref, delta_ref, keep_ref, send_ref, vec_ref,
    cot_ref, out_ref, gw_ref, hidden_ref, gpre_ref, n2_ref, attb_ref, gbr_ref,
):
    pairs = att_ref.shape[0]
    t, d = x_ref.shape
    ff = wup_ref.shape[-1]
    c0 = 0.7978845608028654
    c1 = 0.044715

    def col(values):
        return jnp.sum(values, axis=0, keepdims=True)

    in_order(blk_ref, (c0_ref, c1_ref, c2_ref, c3_ref), cot_ref)
    vec_ref[...] = jnp.zeros_like(vec_ref)
    head = lax.broadcasted_iota(jnp.int32, (HEADS, d), 0)
    lane = lax.broadcasted_iota(jnp.int32, (HEADS, d), 1)
    ones = jnp.where(lane // (d // HEADS) == head, 1.0, 0.0).astype(BF16)
    def tile(step, carry):
        rows = pl.ds(pl.multiple_of(step * MID_TILE, MID_TILE), MID_TILE)
        att = jnp.concatenate([att_ref[g, rows, :] for g in range(pairs)], axis=-1)
        att_b = att.astype(BF16)
        attb_ref[rows, :] = att_b
        middle = x_ref[rows, :].astype(F32) + mm(att_b, wo_ref[...]) + bo_ref[...]
        n, scale = norm_parts(middle)
        n2 = (n * gain_ref[...] + bias_ref[...]).astype(BF16)
        n2_ref[rows, :] = n2
        pre = mm(n2, wup_ref[...]) + bup_ref[...]
        sq = pre * pre
        th = jnp.tanh(c0 * (pre + c1 * (sq * pre)))
        half_one = 0.5 * (1.0 + th)
        hidden = (pre * half_one).astype(BF16)
        hidden_ref[rows, :] = hidden
        slope = half_one + (0.5 * pre) * (1.0 - th * th) * (c0 + (3.0 * c0 * c1) * sq)
        out_ref[rows, :] = (middle + mm(hidden, wdown_ref[...]) + bdown_ref[...]).astype(BF16)
        cot = cot_ref[rows, :]
        cot_f = cot.astype(F32)
        gpre = (mm_nt(cot, wdown_ref[...]) * slope).astype(BF16)
        gpre_ref[rows, :] = gpre
        e = mm_nt(gpre, wup_ref[...])
        gmid = cot_f + norm_pull(e, n, scale, gain_ref[...])
        gmid_ref[rows, :] = gmid
        gbr = gmid.astype(BF16)
        gbr_ref[rows, :] = gbr
        gatt = mm_nt(gbr, wo_ref[...]).astype(BF16)
        for g in range(pairs):
            gatt_ref[g, rows, :] = gatt[:, g * LANES : (g + 1) * LANES]
        prod = gatt.astype(F32) * att
        hi = prod.astype(BF16)
        lo = (prod - hi.astype(F32)).astype(BF16)
        delta_ref[:, rows] = mm_nt(ones, hi) + mm_nt(ones, lo)
        gsum = col(gpre.astype(F32))
        vec_ref[0:1] += col(cot_f)
        vec_ref[1:2] += gsum[:, :d]
        vec_ref[2:3] += gsum[:, d:]
        vec_ref[3:4] += col(e * n)
        vec_ref[4:5] += col(e)
        vec_ref[5:6] += col(gbr.astype(F32))
        return carry

    lax.fori_loop(0, t // MID_TILE, tile, 0)
    leave(blk_ref, out_ref, o0_ref, o1_ref, o2_ref)
    gw_ref[:ff] = mm_tn(hidden_ref[...], cot_ref[...])
    gw_ref[ff : ff + d] = mm_tn(n2_ref[...], gpre_ref[:, :d])
    gw_ref[ff + d : ff + 2 * d] = mm_tn(n2_ref[...], gpre_ref[:, d:])
    gw_ref[ff + 2 * d :] = mm_tn(attb_ref[...], gbr_ref[...])
    split_halves(core_ref, gw_ref, keep_ref, send_ref)


def middle_call(core, blk, att, x, cots, w_o, b_o, gain, bias, w_up, b_up, w_down, b_down):
    t, d = x.shape
    pairs = d // LANES
    ff = w_up.shape[1]
    half = (ff + 3 * d) // 2
    return pl.pallas_call(
        middle_kernel,
        grid=(1,),
        in_specs=[
            SMEM_SPEC, SMEM_SPEC,
            by_pair(pairs, t), by_row(d, t), *[whole(c.shape) for c in cots], whole((d, d)), whole((1, d)), whole((1, d)), whole((1, d)),
            whole((d, ff)), whole((1, ff)), whole((ff, d)), whole((1, d)),
        ],
        out_specs=[
            whole((t // 4, d)), whole((t // 4, d)), whole((t // 2, d)), by_row(d, t), by_pair(pairs, t), heads_row(t), whole((half, d)), whole((half, d)),
            whole((8, d)),
        ],
        out_shape=[
            pltpu.HBM((t // 4, d), BF16),
            pltpu.HBM((t // 4, d), BF16),
            pltpu.HBM((t // 2, d), BF16),
            pltpu.HBM((t, d), F32),
            pltpu.HBM((pairs, t, LANES), BF16),
            jax.ShapeDtypeStruct((HEADS, t), F32),
            jax.ShapeDtypeStruct((half, d), BF16),
            jax.ShapeDtypeStruct((half, d), BF16),
            jax.ShapeDtypeStruct((8, d), F32),
        ],
        scratch_shapes=[
            pltpu.VMEM((t, d), BF16),
            pltpu.VMEM((t, d), BF16),
            pltpu.VMEM((2 * half, d), F32),
            pltpu.VMEM((t, ff), BF16),
            pltpu.VMEM((t, ff), BF16),
            pltpu.VMEM((t, d), BF16),
            pltpu.VMEM((t, d), BF16),
            pltpu.VMEM((t, d), BF16),
        ],
        compiler_params=params(30),
        cost_estimate=cost(15e9, 20e6),
        name="middle",
    )(core, blk, att, x, *cots, w_o, b_o[None], gain[None], bias[None], w_up, b_up[None], w_down, b_down[None])


def backward_kernel(first, ends_ref, q_ref, k_ref, v_ref, g_ref, lse_ref, delta_ref, dq_ref, dk_ref, dv_ref, acc_ref):
    pair = pl.program_id(0) + first
    t = q_ref.shape[1]
    scale_qk = (LANES // 2) ** (-0.5)
    pos_row = lax.broadcasted_iota(jnp.int32, (1, t), 1)
    start_row = cell_start(ends_ref, pos_row)
    acc_ref[...] = jnp.zeros_like(acc_ref)
    jobs = [(j, half) for j in range(t // TILE) for half in range(2)]
    lses = [lse_ref[pl.ds(2 * pair + half, 1), :] for half in range(2)]
    deltas = [delta_ref[pl.ds(2 * pair + half, 1), :] for half in range(2)]
    kts = {}
    outs = {}

    def scores(job):
        j, half = job
        low = j * TILE
        km = only_head(k_ref[0, low : low + TILE, :], half)
        vm = only_head(v_ref[0, low : low + TILE, :], half)
        return mm_nt(km, q_ref[0, low:, :]), mm_nt(vm, g_ref[0, low:, :])

    def rest(job, s, dp):
        j, half = job
        low = j * TILE
        k_pos = low + lax.broadcasted_iota(jnp.int32, (TILE, t - low), 0)
        high = low + TILE
        diag = (k_pos[:, :TILE] >= start_row[:, low:high]) & (k_pos[:, :TILE] <= pos_row[:, low:high])
        p = jnp.exp(jnp.where(diag, s[:, :TILE] - lses[half][:, low:high], neg_big))
        if high < t:
            far = k_pos[:, TILE:] >= start_row[:, high:]
            p = jnp.concatenate([p, jnp.exp(jnp.where(far, s[:, TILE:] - lses[half][:, high:], neg_big))], axis=1)
        ds = (p * (dp - deltas[half][:, low:])).astype(BF16)
        dv = mm(p.astype(BF16), g_ref[0, low:, :])
        dk = mm(ds, q_ref[0, low:, :])
        kt = jnp.transpose(k_ref[0, low : low + TILE, :])
        rows = slice(half * 64, half * 64 + 64)
        acc_ref[rows, low:] += mm(kt[rows], ds)
        if half == 0:
            outs[j] = (dk, dv)
        else:
            first_lanes = head_lanes(dk.shape, 0)
            dk_ref[0, low : low + TILE, :] = jnp.where(first_lanes, outs[j][0], dk).astype(BF16)
            dv_ref[0, low : low + TILE, :] = jnp.where(first_lanes, outs[j][1], dv).astype(BF16)

    ready = scores(jobs[0])
    for at, job in enumerate(jobs):
        now = ready
        if at + 1 < len(jobs):
            ready = scores(jobs[at + 1])
        rest(job, *now)
    dq_ref[0] = jnp.transpose((acc_ref[...] * scale_qk)).astype(BF16)


def backward_call(ends, q, k, v, gatt, lse, delta, first, count):
    pairs, t, _ = q.shape
    spec = pl.BlockSpec((1, t, LANES), lambda i: (i + first, 0, 0))
    out = pl.BlockSpec((1, t, LANES), lambda i: (i, 0, 0))
    return pl.pallas_call(
        functools.partial(backward_kernel, first),
        grid=(count,),
        in_specs=[SMEM_SPEC, spec, spec, spec, spec, whole((HEADS, t)), whole((HEADS, t))],
        out_specs=[out, out, out],
        out_shape=[jax.ShapeDtypeStruct((count, t, LANES), BF16)] * 3,
        scratch_shapes=[pltpu.VMEM((LANES, t), F32)],
        compiler_params=params(28),
        cost_estimate=cost(count * B_FLOPS, count * 1e5),
        name="backward",
    )(ends, *in_hbm(q, k, v, gatt), lse, delta)


VEC_ROWS = 128


def last_kernel(*refs):
    core_ref, blk_ref = refs[:2]
    grads = refs[2:5]
    n1_ref, x_ref, gmid_ref, gain_ref, w_ref, vecmid_ref = refs[5:11]
    g0_ref, g1_ref, g2_ref, keep_ref, send_ref, gw_ref, gin_ref = refs[11:]
    pairs = grads[0].shape[0]
    d = x_ref.shape[-1]
    half = keep_ref.shape[0]
    gqkv = jnp.concatenate([grads[part][g] for part in range(3) for g in range(pairs)], axis=-1)
    gw = mm_tn(n1_ref[...], gqkv)
    blocks = 3 * pairs
    for p in range(blocks):
        at = (p // (blocks // 2)) * half + (p % (blocks // 2)) * d
        gw_ref[at : at + d] = gw[:, p * LANES : (p + 1) * LANES]
    e = mm_nt(gqkv, w_ref[...])
    n, scale = norm_parts(x_ref[...].astype(F32))
    gin_ref[...] = (gmid_ref[...] + norm_pull(e, n, scale, gain_ref[...])).astype(BF16)
    leave(blk_ref, gin_ref, g0_ref, g1_ref, g2_ref)

    def col(values):
        return jnp.sum(values, axis=0, keepdims=True)

    rows = [vecmid_ref[r : r + 1] for r in range(6)]
    rows += [col(e * n), col(e), col(gqkv[:, :d].astype(F32)), col(gqkv[:, 2 * d :].astype(F32))]
    base = half - VEC_ROWS
    gw_ref[base:half] = jnp.zeros((VEC_ROWS, LANES), F32)
    gw_ref[half + base :] = jnp.zeros((VEC_ROWS, LANES), F32)
    for r, row in enumerate(rows):
        for g in range(d // LANES):
            at = base + r * (d // LANES) + g
            gw_ref[at : at + 1] = row[:, g * LANES : (g + 1) * LANES]
    split_halves(core_ref, gw_ref, keep_ref, send_ref)


def last_call(core, blk, grads, n1, x, gmid, gain, w_qkv, vec_mid):
    t, d = x.shape
    half = 3 * d * d // LANES // 2 + VEC_ROWS
    return pl.pallas_call(
        last_kernel,
        grid=(1,),
        in_specs=[SMEM_SPEC, SMEM_SPEC]
        + [whole(a.shape) for a in grads]
        + [by_row(d, t), by_row(d, t), by_row(d, t), whole((1, d)), whole(w_qkv.shape), whole((8, d))],
        out_specs=[whole((t // 4, d)), whole((t // 4, d)), whole((t // 2, d)), whole((half, LANES)), whole((half, LANES))],
        out_shape=[
            pltpu.HBM((t // 4, d), BF16),
            pltpu.HBM((t // 4, d), BF16),
            pltpu.HBM((t // 2, d), BF16),
            jax.ShapeDtypeStruct((half, LANES), BF16),
            jax.ShapeDtypeStruct((half, LANES), BF16),
        ],
        scratch_shapes=[pltpu.VMEM((2 * half, LANES), F32), pltpu.VMEM((t, d), BF16)],
        compiler_params=params(28),
        cost_estimate=cost(L_FLOPS, 1e5),
        name="last",
    )(core, blk, *grads, n1, x, gmid, gain[None], w_qkv, vec_mid)


def ordered_halves(core_ref, own_ref, got_ref, write):
    pl.when(core_ref[0] == 0)(functools.partial(write, own_ref, got_ref))
    pl.when(core_ref[0] == 1)(functools.partial(write, got_ref, own_ref))


def finish_mid_kernel(core_ref, own_ref, got_ref, down_ref, up_ref, wo_ref):
    ff, d = down_ref.shape
    half = own_ref.shape[0]

    def write(low_ref, high_ref):
        def take(first, last):
            if last <= half:
                return low_ref[first:last].astype(F32)
            if first >= half:
                return high_ref[first - half : last - half].astype(F32)
            return jnp.concatenate([take(first, half), take(half, last)], axis=0)

        down_ref[...] = take(0, ff)
        up_ref[:, :d] = take(ff, ff + d)
        up_ref[:, d:] = take(ff + d, ff + 2 * d)
        wo_ref[...] = take(ff + 2 * d, ff + 3 * d)

    ordered_halves(core_ref, own_ref, got_ref, write)


def finish_last_kernel(core_ref, own_ref, got_ref, qkv_ref, *vec_refs):
    d = qkv_ref.shape[0]
    half = own_ref.shape[0]
    blocks = qkv_ref.shape[1] // LANES

    def write(low_ref, high_ref):
        for p in range(blocks):
            ref = (low_ref, high_ref)[p // (blocks // 2)]
            at = (p % (blocks // 2)) * d
            qkv_ref[:, p * LANES : (p + 1) * LANES] = ref[at : at + d].astype(F32)
        at = half - VEC_ROWS
        for ref in vec_refs:
            for g in range(ref.shape[1] // LANES):
                ref[:, g * LANES : (g + 1) * LANES] = low_ref[at : at + 1].astype(F32)
                at += 1

    ordered_halves(core_ref, own_ref, got_ref, write)


def finish_call(kernel, core, own, got, shapes, name):
    return pl.pallas_call(
        kernel,
        grid=(1,),
        in_specs=[SMEM_SPEC, whole(own.shape), whole(got.shape)],
        out_specs=[whole(shape) for shape in shapes],
        out_shape=[jax.ShapeDtypeStruct(shape, F32) for shape in shapes],
        compiler_params=params(28),
        cost_estimate=cost(1e8, 8e6),
        name=name,
    )(core, own, got)


def send_xor(values, flip):
    count = lax.axis_size(BOTH)
    return lax.ppermute(values, BOTH, [(i, i ^ flip) for i in range(count)])


def add_kernel(place_ref, *refs):
    outs = place_ref.shape[0]
    terms, results = refs[:-outs], refs[-outs:]
    size = results[0].shape[0]
    for flip, result in enumerate(results):
        rows = pl.ds(pl.multiple_of(jnp.bitwise_xor(place_ref[0], flip) * size, size), size)
        total = terms[0][rows, :].astype(F32)
        for term in terms[1:]:
            total = total + term[rows, :].astype(F32)
        result[...] = total.astype(result.dtype)


def add_call(place, parts, terms, own_dtype):
    rows, lanes = terms[0].shape
    shape = (rows // parts, lanes)
    places = jnp.broadcast_to(place, (parts,)).astype(jnp.int32)
    return pl.pallas_call(
        add_kernel,
        grid=(1,),
        in_specs=[SMEM_SPEC] + [whole(a.shape) for a in terms],
        out_specs=[whole(shape)] * parts,
        out_shape=[jax.ShapeDtypeStruct(shape, own_dtype if p == 0 else BF16) for p in range(parts)],
        compiler_params=params(28),
        cost_estimate=cost(1e8, 4e6),
        name="add",
    )(places, *terms)


def join_kernel(place_ref, *refs):
    out_ref = refs[-1]
    for flip, ref in enumerate(refs[:-1]):
        size = ref.shape[0]
        rows = pl.ds(pl.multiple_of(jnp.bitwise_xor(place_ref[0], flip) * size, size), size)
        out_ref[rows, :] = ref[...]


def join_call(place, pieces):
    rows, lanes = pieces[0].shape
    shape = (rows * len(pieces), lanes)
    return pl.pallas_call(
        join_kernel,
        grid=(1,),
        in_specs=[SMEM_SPEC] + [whole(p.shape) for p in pieces],
        out_specs=whole(shape),
        out_shape=jax.ShapeDtypeStruct(shape, pieces[0].dtype),
        compiler_params=params(28),
        cost_estimate=cost(1e8, 2e6),
        name="join",
    )(place[None].astype(jnp.int32), *pieces)


def swap_parts(parts, shift):
    return [send_xor(part, (flip + 1) << shift) for flip, part in enumerate(parts)]


def spread(part, shift, parts):
    return [send_xor(part, flip << shift) for flip in range(1, parts)]


def after(values, *others):
    return lax.optimization_barrier((values,) + others)[0]


def row_device(
    tokens, seg_lengths, ln1_gain, ln1_bias, w_qkv, b_qv, w_o, b_o, ln2_gain, ln2_bias,
    w_up, b_up, w_down, b_down, cotangent,
):
    row_count, slice_len, d = tokens.shape
    row = lax.axis_index("blk")
    me = lax.axis_index("rows") * lax.axis_size("blk") + row
    place_core = me & 1
    place_plane = (me >> 1) & 3
    place_deep = me >> 3
    core = place_core[None].astype(jnp.int32)
    blk = row[None].astype(jnp.int32)
    ends = jnp.cumsum(seg_lengths, axis=1)
    ends = lax.dynamic_index_in_dim(ends, row, 0, keepdims=False).astype(jnp.int32)

    def cut(values):
        return [lax.dynamic_index_in_dim(values, row ^ flip, 0, keepdims=False) for flip in range(row_count)]

    def swap(pieces):
        return [pieces[0]] + swap_parts(pieces[1:], 0)

    x = swap(cut(tokens))
    cot = cut(cotangent)
    cot = lax.optimization_barrier(tuple(cot) + tuple(x))[:row_count]
    cot = swap(list(cot))
    x, q, k, v, n1, att, lse = forward_call(ends, blk, x, ln1_gain, ln1_bias, w_qkv, b_qv)
    out, out_near, out_far, gmid, gatt, delta, keep, send, vec_mid = middle_call(
        core, blk, att, x, cot, w_o, b_o, ln2_gain, ln2_bias, w_up, b_up, w_down, b_down
    )
    own, *parts = add_call(place_plane, 4, [keep, send_xor(send, 1)], F32)
    grads = backward_call(after(ends, own), q, k, v, gatt, lse, delta, 0, d // LANES)
    own, *parts = add_call(after(place_deep, grads[0]), 4, [own] + swap_parts(parts, 1), F32)
    out_far = send_xor(after(out_far, own), 2)
    first = [own] + swap_parts(parts, 3)
    gin, gin_near, gin_far, keep, send = last_call(
        after(core, own), blk, grads, n1, x, gmid, ln1_gain, w_qkv, vec_mid
    )
    (first,) = add_call(0, 1, first, BF16)
    send, first, out_far = lax.optimization_barrier((send, first, out_far))
    first_z = spread(first, 3, 2)
    own, *parts = add_call(place_plane, 4, [keep, send_xor(send, 1)], F32)
    first = join_call(after(place_deep & 1, own), [first] + first_z)
    first_z = spread(first, 4, 2)
    second = swap_parts(parts, 1)
    own, *parts = add_call(place_deep, 4, [own] + second, F32)
    out_near = send_xor(relay_call(after(out_near, own), out_far), 1)
    first = join_call(place_deep >> 1, [first] + first_z)
    first, gin_far = lax.optimization_barrier((first, gin_far, own))[:2]
    gin_far = send_xor(gin_far, 2)
    (second,) = add_call(0, 1, [own] + swap_parts(parts, 3), BF16)
    first = join_call(after(place_plane & 1, second), [first] + spread(first, 1, 2))
    second = join_call(place_deep, [second] + spread(second, 3, 4))
    first = join_call(after(place_plane >> 1, second), [first] + spread(first, 2, 2))
    gin_near = send_xor(relay_call(after(gin_near, second), gin_far), 1)
    output = arrive_call(after(blk, second), out, out_near, out_far, BF16)
    input_grad = arrive_call(blk, gin, gin_near, gin_far, F32)
    second = join_call(after(place_plane, output, input_grad), [second] + spread(second, 1, 4))
    gw_down, gw_up, gw_o = finish_call(
        finish_mid_kernel, core, first, send_xor(first, 1), [w_down.shape, w_up.shape, w_o.shape], "finish_mid"
    )
    gw_qkv, *vecs = finish_call(
        finish_last_kernel, after(core, gw_down), second, send_xor(second, 1),
        [w_qkv.shape] + [(1, size) for size in (d, 2 * d, d, d, d, d, d, 2 * d)], "finish_last",
    )
    vecs = [vec.reshape(-1) for vec in vecs]
    g_down_b, g_up_b, g_ln2_gain, g_ln2_bias, g_o_b, g_ln1_gain, g_ln1_bias, g_qv_b = vecs
    return (
        output, input_grad, g_ln1_gain, g_ln1_bias, gw_qkv, g_qv_b, gw_o, g_o_b, g_ln2_gain, g_ln2_bias,
        gw_up, g_up_b, gw_down, g_down_b,
    )


def layer_norm(values, gain_vec, bias_vec):
    average = jnp.mean(values, axis=-1, keepdims=True)
    centered = values - average
    variance = jnp.mean(centered * centered, axis=-1, keepdims=True)
    return centered * lax.rsqrt(variance + norm_eps) * gain_vec + bias_vec


def segment_of(cell_ends, positions):
    return jnp.sum((cell_ends[:, None, :] <= positions[None, :, None]).astype(jnp.int32), axis=-1)


def block_scores(query_heads, key_heads, query_pos, key_pos, query_seg, key_seg, scale_qk):
    raw_scores = (
        jnp.einsum("rqhd,rkhd->rqhk", query_heads, key_heads, preferred_element_type=jnp.float32)
        * scale_qk
    )
    causal = key_pos[None, :] <= query_pos[:, None]
    same_cell = query_seg[:, :, None] == key_seg[:, None, :]
    allowed = (causal[None] & same_cell)[:, :, None, :]
    return (jnp.where(allowed, raw_scores, neg_big), allowed)


def block_active(query_pos, key_pos, query_seg, key_seg):
    return (key_pos[0] <= query_pos[-1]) & jnp.any(key_seg[:, -1] >= query_seg[:, 0])


def backward_block(
    query_heads,
    grad_heads,
    log_total,
    delta_sum,
    key_heads,
    value_heads,
    query_pos,
    key_pos,
    query_seg,
    key_seg,
    scale_qk,
):
    scores, allowed = block_scores(
        query_heads, key_heads, query_pos, key_pos, query_seg, key_seg, scale_qk
    )
    softmaxed = jnp.where(allowed, jnp.exp(scores - log_total[..., None]), 0.0)
    grad_probs = jnp.einsum(
        "rqhd,rkhd->rqhk", grad_heads, value_heads, preferred_element_type=jnp.float32
    )
    grad_scores = (softmaxed * (grad_probs - delta_sum[..., None])).astype(jnp.bfloat16)
    grad_query = (
        jnp.einsum("rqhk,rkhd->rqhd", grad_scores, key_heads, preferred_element_type=jnp.float32)
        * scale_qk
    )
    grad_key = (
        jnp.einsum("rqhk,rqhd->rkhd", grad_scores, query_heads, preferred_element_type=jnp.float32)
        * scale_qk
    )
    grad_value = jnp.einsum(
        "rqhk,rqhd->rkhd",
        softmaxed.astype(jnp.bfloat16),
        grad_heads,
        preferred_element_type=jnp.float32,
    )
    return (grad_query, grad_key, grad_value)


def unchanged(old_state):
    return old_state


def general_device(
    tokens,
    seg_lengths,
    ln1_gain,
    ln1_bias,
    w_qkv,
    b_qv,
    w_o,
    b_o,
    ln2_gain,
    ln2_bias,
    w_up,
    b_up,
    w_down,
    b_down,
    cotangent,
):
    row_count, slice_len, width_all = tokens.shape
    head_size = width_all // HEADS
    scale_qk = head_size ** (-0.5)
    head_shape = (row_count, slice_len, HEADS, head_size)
    stat_shape = (row_count, slice_len, HEADS)
    full_length = lax.axis_size("blk") * slice_len
    offsets = jnp.arange(slice_len, dtype=jnp.int32)
    query_pos = lax.axis_index("blk") * slice_len + offsets
    cell_ends = jnp.cumsum(seg_lengths, axis=1)
    query_seg = segment_of(cell_ends, query_pos)

    def take_block(piece, block_index):
        return lax.dynamic_slice_in_dim(piece, block_index * slice_len, slice_len, 1).reshape(
            head_shape
        )

    inputs = tokens.astype(jnp.float32)
    normed_val, first_pull = jax.vjp(layer_norm, inputs, ln1_gain, ln1_bias)
    normed_one = normed_val.astype(jnp.bfloat16)
    projected = jnp.dot(normed_one, w_qkv, preferred_element_type=jnp.float32)
    query_b = (projected[..., :width_all] + b_qv[:width_all]).astype(jnp.bfloat16)
    key_b = projected[..., width_all : 2 * width_all].astype(jnp.bfloat16)
    value_b = (projected[..., 2 * width_all :] + b_qv[width_all:]).astype(jnp.bfloat16)
    query_heads = query_b.reshape(head_shape)
    start_state = (
        jnp.full(stat_shape, neg_big, jnp.float32),
        jnp.zeros(stat_shape, jnp.float32),
        jnp.zeros(head_shape, jnp.float32),
    )
    key_piece = lax.all_gather(key_b, "blk", axis=1, tiled=True)
    value_piece = lax.all_gather(value_b, "blk", axis=1, tiled=True)

    def forward_block_step(block_index, inner_state):
        key_pos = block_index * slice_len + offsets
        key_seg = segment_of(cell_ends, key_pos)
        key_heads = take_block(key_piece, block_index)
        value_heads = take_block(value_piece, block_index)

        def forward_update(old_state):
            running_top, running_total, running_sum = old_state
            scores, allowed = block_scores(
                query_heads, key_heads, query_pos, key_pos, query_seg, key_seg, scale_qk
            )
            new_top = jnp.maximum(running_top, jnp.max(scores, axis=-1))
            factor = jnp.exp(running_top - new_top)
            weights_now = jnp.where(allowed, jnp.exp(scores - new_top[..., None]), 0.0)
            new_total = running_total * factor + jnp.sum(weights_now, axis=-1)
            new_sum = running_sum * factor[..., None] + jnp.einsum(
                "rqhk,rkhd->rqhd",
                weights_now.astype(jnp.bfloat16),
                value_heads,
                preferred_element_type=jnp.float32,
            )
            return (new_top, new_total, new_sum)

        return lax.cond(
            block_active(query_pos, key_pos, query_seg, key_seg),
            forward_update,
            unchanged,
            inner_state,
        )

    running_top, running_total, running_sum = lax.fori_loop(
        0, key_piece.shape[1] // slice_len, forward_block_step, start_state
    )
    attn_f32 = (running_sum / running_total[..., None]).reshape(row_count, slice_len, width_all)
    log_total = running_top + jnp.log(running_total)
    attn_b = attn_f32.astype(jnp.bfloat16)
    middle = inputs + jnp.dot(attn_b, w_o, preferred_element_type=jnp.float32) + b_o
    normed_two_val, second_pull = jax.vjp(layer_norm, middle, ln2_gain, ln2_bias)
    normed_two = normed_two_val.astype(jnp.bfloat16)
    hidden_pre = jnp.dot(normed_two, w_up, preferred_element_type=jnp.float32) + b_up
    hidden_val, gelu_pull = jax.vjp(jax.nn.gelu, hidden_pre)
    hidden_b = hidden_val.astype(jnp.bfloat16)
    output = (
        middle + jnp.dot(hidden_b, w_down, preferred_element_type=jnp.float32) + b_down
    ).astype(jnp.bfloat16)
    grad_out = cotangent.astype(jnp.float32)
    grad_w_down = jnp.einsum("rcf,rcd->fd", hidden_b, cotangent, preferred_element_type=jnp.float32)
    grad_b_down = jnp.sum(grad_out, axis=(0, 1))
    grad_hidden = jnp.einsum("rcd,fd->rcf", cotangent, w_down, preferred_element_type=jnp.float32)
    (grad_pre,) = gelu_pull(grad_hidden)
    grad_pre_b = grad_pre.astype(jnp.bfloat16)
    grad_w_up = jnp.einsum(
        "rcd,rcf->df", normed_two, grad_pre_b, preferred_element_type=jnp.float32
    )
    grad_b_up = jnp.sum(grad_pre_b.astype(jnp.float32), axis=(0, 1))
    grad_normed_two = jnp.einsum(
        "rcf,df->rcd", grad_pre_b, w_up, preferred_element_type=jnp.float32
    )
    grad_mid_norm, grad_ln2_gain, grad_ln2_bias = second_pull(grad_normed_two)
    grad_middle = grad_out + grad_mid_norm
    grad_branch_b = grad_middle.astype(jnp.bfloat16)
    grad_w_o = jnp.einsum("rce,rcd->ed", attn_b, grad_branch_b, preferred_element_type=jnp.float32)
    grad_b_o = jnp.sum(grad_branch_b.astype(jnp.float32), axis=(0, 1))
    grad_attn_b = jnp.einsum(
        "rcd,ed->rce", grad_branch_b, w_o, preferred_element_type=jnp.float32
    ).astype(jnp.bfloat16)
    delta_sum = jnp.sum((grad_attn_b.astype(jnp.float32) * attn_f32).reshape(head_shape), axis=-1)
    grad_heads = grad_attn_b.reshape(head_shape)
    whole_shape = (row_count, full_length, HEADS, head_size)
    back_state = (
        jnp.zeros(head_shape, jnp.float32),
        jnp.zeros(whole_shape, jnp.float32),
        jnp.zeros(whole_shape, jnp.float32),
    )
    backward_key_piece = lax.all_gather(key_b, "blk", axis=1, tiled=True)
    backward_value_piece = lax.all_gather(value_b, "blk", axis=1, tiled=True)

    def backward_block_step(block_index, inner_state):
        key_pos = block_index * slice_len + offsets
        key_seg = segment_of(cell_ends, key_pos)
        key_heads = take_block(backward_key_piece, block_index)
        value_heads = take_block(backward_value_piece, block_index)

        def backward_update(old_state):
            grad_query, grad_key, grad_value = backward_block(
                query_heads,
                grad_heads,
                log_total,
                delta_sum,
                key_heads,
                value_heads,
                query_pos,
                key_pos,
                query_seg,
                key_seg,
                scale_qk,
            )
            at_row = block_index * slice_len
            return (
                old_state[0] + grad_query,
                lax.dynamic_update_slice_in_dim(old_state[1], grad_key, at_row, 1),
                lax.dynamic_update_slice_in_dim(old_state[2], grad_value, at_row, 1),
            )

        return lax.cond(
            block_active(query_pos, key_pos, query_seg, key_seg),
            backward_update,
            unchanged,
            inner_state,
        )

    back_result = lax.fori_loop(
        0, backward_key_piece.shape[1] // slice_len, backward_block_step, back_state
    )
    grad_query_sum = back_result[0]
    grad_key_sum, grad_value_sum = (
        lax.psum_scatter(
            back_result[1].astype(jnp.bfloat16), "blk", scatter_dimension=1, tiled=True
        ).astype(jnp.float32),
        lax.psum_scatter(
            back_result[2].astype(jnp.bfloat16), "blk", scatter_dimension=1, tiled=True
        ).astype(jnp.float32),
    )
    flat_shape = (row_count, slice_len, width_all)
    grad_qkv_b = jnp.concatenate(
        [
            grad_query_sum.reshape(flat_shape),
            grad_key_sum.reshape(flat_shape),
            grad_value_sum.reshape(flat_shape),
        ],
        axis=-1,
    ).astype(jnp.bfloat16)
    grad_w_qkv = jnp.einsum(
        "rcd,rce->de", normed_one, grad_qkv_b, preferred_element_type=jnp.float32
    )
    column_sums = jnp.sum(grad_qkv_b.astype(jnp.float32), axis=(0, 1))
    grad_b_qv = jnp.concatenate([column_sums[:width_all], column_sums[2 * width_all :]])
    grad_normed_one = jnp.einsum(
        "rce,de->rcd", grad_qkv_b, w_qkv, preferred_element_type=jnp.float32
    )
    grad_in_norm, grad_ln1_gain, grad_ln1_bias = first_pull(grad_normed_one)
    input_grad = grad_middle + grad_in_norm
    grads = (
        grad_ln1_gain,
        grad_ln1_bias,
        grad_w_qkv,
        grad_b_qv,
        grad_w_o,
        grad_b_o,
        grad_ln2_gain,
        grad_ln2_bias,
        grad_w_up,
        grad_b_up,
        grad_w_down,
        grad_b_down,
    )
    summed = lax.psum(
        (
            grads[0],
            grads[1],
            grads[2],
            grads[3],
            grads[4],
            grads[5],
            grads[6],
            grads[7],
            grads[8],
            grads[9],
            grads[10],
            grads[11],
        ),
        ("rows", "blk"),
    )
    return (
        output,
        input_grad,
        summed[0],
        summed[1],
        summed[2],
        summed[3],
        summed[4],
        summed[5],
        summed[6],
        summed[7],
        summed[8],
        summed[9],
        summed[10],
        summed[11],
    )


def device_function(tokens, *rest):
    d = tokens.shape[2]
    whole_rows = (
        lax.axis_size("blk") == tokens.shape[0] == 4
        and lax.axis_size("rows") == 8
        and tokens.shape[1] == TILE
        and d == 512
    )
    return (row_device if whole_rows else general_device)(tokens, *rest)


def solution(mesh):
    in_specs = (
        P("rows", "blk", None),
        P("rows", None),
        P(),
        P(),
        P(),
        P(),
        P(),
        P(),
        P(),
        P(),
        P(),
        P(),
        P(),
        P(),
        P("rows", "blk", None),
    )
    out_specs = (
        P("rows", "blk", None),
        P("rows", "blk", None),
        P(),
        P(),
        P(),
        P(),
        P(),
        P(),
        P(),
        P(),
        P(),
        P(),
        P(),
        P(),
    )
    return jax.shard_map(
        device_function, mesh=mesh, in_specs=in_specs, out_specs=out_specs, check_vma=False
    )
```
